32 devices in a mesh: tok: 16 (over z, x, core), blk: 2 (over y).
Axes of the slice: x: 2, y: 2, z: 4, core: 2. Of those that a mesh axis runs over, the one named last changes fastest.
Arguments:
- tokens: bfloat16 [83968, 512], P(('tok', 'blk')), may hold values from -6 to 6
- cotangent: float32 [83968, 512], P(('tok', 'blk')), may hold values from -6 to 6
- grid_class: int32 [1024], P('tok'), may hold values from 0 to 2, as said below
- qkv_weight: float32 [2, 512, 1536], P(None, 'tok', 'blk'), may hold values from -0.25 to 0.25
- proj_weight: float32 [2, 512, 512], P(None, 'blk', 'tok'), may hold values from -0.25 to 0.25
- up_weight: float32 [2, 512, 2048], P(None, 'tok', 'blk'), may hold values from -0.25 to 0.25
- down_weight: float32 [2, 2048, 512], P(None, 'blk', 'tok'), may hold values from -0.125 to 0.125
- norm_params: float32 [2, 4, 512], replicated, may hold values from -1 to 1.6, as said below
- cpe_weight: float32 [2, 9, 512], replicated, may hold values from -2 to 2
- crpe_weight: float32 [2, 49, 512], replicated, may hold values from -0.9 to 0.9
- qkv_moment: float32 [2, 512, 1536], P(None, 'tok', 'blk'), may hold values from -695.45355 to 695.45355
- proj_moment: float32 [2, 512, 512], P(None, 'blk', 'tok'), may hold values from -695.45355 to 695.45355
- up_moment: float32 [2, 512, 2048], P(None, 'tok', 'blk'), may hold values from -695.45355 to 695.45355
- down_moment: float32 [2, 2048, 512], P(None, 'blk', 'tok'), may hold values from -695.45355 to 695.45355
- norm_moment: float32 [2, 4, 512], replicated, may hold values from -1043.1804 to 1043.1804
- cpe_moment: float32 [2, 9, 512], replicated, may hold values from -1043.1804 to 1043.1804
- crpe_moment: float32 [2, 49, 512], replicated, may hold values from -521.5902 to 521.5902
Outputs:
- block_out: bfloat16 [83968, 512], P(('tok', 'blk'))
- tokens_grad: float32 [83968, 512], P(('tok', 'blk'))
- qkv_moment_new: float32 [2, 512, 1536], P(None, 'tok', 'blk')
- qkv_new: float32 [2, 512, 1536], P(None, 'tok', 'blk')
- qkv_copy: bfloat16 [2, 512, 1536], P(None, 'tok', 'blk')
- proj_moment_new: float32 [2, 512, 512], P(None, 'blk', 'tok')
- proj_new: float32 [2, 512, 512], P(None, 'blk', 'tok')
- proj_copy: bfloat16 [2, 512, 512], P(None, 'blk', 'tok')
- up_moment_new: float32 [2, 512, 2048], P(None, 'tok', 'blk')
- up_new: float32 [2, 512, 2048], P(None, 'tok', 'blk')
- up_copy: bfloat16 [2, 512, 2048], P(None, 'tok', 'blk')
- down_moment_new: float32 [2, 2048, 512], P(None, 'blk', 'tok')
- down_new: float32 [2, 2048, 512], P(None, 'blk', 'tok')
- down_copy: bfloat16 [2, 2048, 512], P(None, 'blk', 'tok')
- norm_moment_new: float32 [2, 4, 512], replicated
- norm_new: float32 [2, 4, 512], replicated
- cpe_moment_new: float32 [2, 9, 512], replicated
- cpe_new: float32 [2, 9, 512], replicated
- crpe_moment_new: float32 [2, 49, 512], replicated
- crpe_new: float32 [2, 49, 512], replicated
The draws below stay inside these ranges and needn't reach their ends.
Inputs may be any that keep to these rules, and one draw needn't show every extreme that they name: `grid_class`: grid class c is an image of (5 + 2c) x (5 + 2c) patches; images lie 64 to an index of tok in order, and larger classes grow more common with that index. `norm_params`: rows 0 and 2 of each layer are gains of the two norms, rows 1 and 3 their shifts.
All inputs are finite; a program needn't handle non-finite values.
Results may differ from the reference program's by a relative error of at most 0.023.
Values may be sent and summed in bfloat16 or wider, within the bound.
A program may use at most 960 MiB of HBM per device.

```python
import math
from functools import partial
import jax
import jax.numpy as jnp
from jax import lax

D = 512
FF = 2048
HEADS = 8
HD = 64
GROUPS = 8
GROUP_W = 256
SLOT = 82
LAYERS = 2
IMG_DEV = 64
IMAGES = 1024
TOKENS = 83968


def draw_grid_class(key, part):
    key = jax.random.fold_in(key, 11)
    first_key, second_key = jax.random.split(key)
    device_at = jnp.arange(IMAGES, dtype=jnp.int32) // IMG_DEV
    devices = IMAGES // IMG_DEV
    first_draw = jax.random.randint(first_key, (IMAGES,), 0, devices + 1)
    second_draw = jax.random.randint(second_key, (IMAGES,), 0, devices + 1)
    return (first_draw <= device_at).astype(jnp.int32) + (second_draw <= device_at).astype(jnp.int32)


def draw_norm_params(key, part):
    key = jax.random.fold_in(key, 5)
    gain_key, shift_key = jax.random.split(key)
    shape_all = (LAYERS, 4, D)
    gain_vals = jnp.clip(1.0 + 0.15 * jax.random.normal(gain_key, shape_all, jnp.float32), 0.4, 1.6)
    shift_vals = jnp.clip(0.3 * jax.random.normal(shift_key, shape_all, jnp.float32), -1.0, 1.0)
    even_rows = (jnp.arange(4) % 2 == 0)[None, :, None]
    return jnp.where(even_rows, gain_vals, shift_vals)


def level_of(key, dims, cuts, least, largest):
    def one(dim, blocks):
        steps = jax.random.uniform(jax.random.fold_in(jax.random.fold_in(key, 6), dim), (blocks,), jnp.float32, least / len(cuts), largest / len(cuts))
        return jnp.repeat(jnp.exp(steps), dims[dim] // blocks).reshape((-1,) + (1,) * (len(dims) - dim - 1))

    factor_of = one(*cuts[0])
    for cut in cuts[1:]:
        factor_of = factor_of * one(*cut)
    return factor_of


def noise(key, dims, deviation, most, cuts=(), kind=jnp.bfloat16):
    values = deviation * jax.random.normal(key, dims, jnp.float32)
    if cuts:
        values = values * level_of(key, dims, cuts, -0.22, 0.18)
    return jnp.clip(values, -most, most).astype(kind)


def setup_inputs(seed: int = 0) -> dict:
    arg_keys = jax.random.split(jax.random.key(seed), 18)
    tokens = noise(arg_keys[0], (TOKENS, D), 1.0, 6.0, ((0, 32),))
    cotangent = noise(arg_keys[1], (TOKENS, D), 1.0, 6.0, ((0, 32),), jnp.float32)
    grid_class = draw_grid_class(jax.random.fold_in(arg_keys[17], 71), 0)
    qkv_weight = noise(arg_keys[3], (LAYERS, D, 3 * D), D ** -0.5, 0.25, ((1, 16), (2, 2)), jnp.float32)
    proj_weight = noise(arg_keys[4], (LAYERS, D, D), D ** -0.5, 0.25, ((1, 2), (2, 16)), jnp.float32)
    up_weight = noise(arg_keys[5], (LAYERS, D, FF), D ** -0.5, 0.25, ((1, 16), (2, 2)), jnp.float32)
    down_weight = noise(arg_keys[6], (LAYERS, FF, D), FF ** -0.5, 0.125, ((1, 2), (2, 16)), jnp.float32)
    norm_params = draw_norm_params(jax.random.fold_in(arg_keys[17], 71), 0)
    cpe_weight = noise(arg_keys[8], (LAYERS, 9, D), 0.33, 2.0, (), jnp.float32)
    crpe_weight = noise(arg_keys[9], (LAYERS, 49, D), 0.15, 0.9, (), jnp.float32)
    qkv_moment = noise(arg_keys[10], (LAYERS, D, 3 * D), (0.4 * TOKENS ** 0.5), 695.45355, ((1, 16), (2, 2)), jnp.float32)
    proj_moment = noise(arg_keys[11], (LAYERS, D, D), (0.4 * TOKENS ** 0.5), 695.45355, ((1, 2), (2, 16)), jnp.float32)
    up_moment = noise(arg_keys[12], (LAYERS, D, FF), (0.4 * TOKENS ** 0.5), 695.45355, ((1, 16), (2, 2)), jnp.float32)
    down_moment = noise(arg_keys[13], (LAYERS, FF, D), (0.4 * TOKENS ** 0.5), 695.45355, ((1, 2), (2, 16)), jnp.float32)
    norm_moment = noise(arg_keys[14], (LAYERS, 4, D), (0.6 * TOKENS ** 0.5), 1043.1804, (), jnp.float32)
    cpe_moment = noise(arg_keys[15], (LAYERS, 9, D), (0.6 * TOKENS ** 0.5), 1043.1804, (), jnp.float32)
    crpe_moment = noise(arg_keys[16], (LAYERS, 49, D), (0.3 * TOKENS ** 0.5), 521.5902, (), jnp.float32)
    return {"tokens": tokens, "cotangent": cotangent, "grid_class": grid_class, "qkv_weight": qkv_weight, "proj_weight": proj_weight, "up_weight": up_weight, "down_weight": down_weight, "norm_params": norm_params, "cpe_weight": cpe_weight, "crpe_weight": crpe_weight, "qkv_moment": qkv_moment, "proj_moment": proj_moment, "up_moment": up_moment, "down_moment": down_moment, "norm_moment": norm_moment, "cpe_moment": cpe_moment, "crpe_moment": crpe_moment}


FULL_PRECISION = lax.Precision.HIGHEST
SCHULZ_COEFFS = (3.4445, -4.775, 2.0315)
MUON_RATES = (0.8, 0.8, 0.8, 0.4)
SMALL_RATES = (0.3, 0.3, 0.15)

@jax.custom_vjp
def low(v):
    return lax.optimization_barrier(v.astype(jnp.bfloat16)).astype(jnp.float32)

@jax.custom_vjp
def low_back(v):
    return v

def low_keep(v):
    return (low(v), None)

def low_pass(kept, grad):
    return (grad,)

def back_keep(v):
    return (v, None)

def back_low(kept, grad):
    return (low(grad),)
low.defvjp(low_keep, low_pass)
low_back.defvjp(back_keep, back_low)

def spatial_masks(grid_class):
    extent = 5 + 2 * grid_class
    across = (jnp.arange(9, dtype=jnp.int32)[None, :] < extent[:, None]).astype(jnp.float32)
    cell_mask = across[:, :, None] * across[:, None, :]
    images = grid_class.shape[0]
    key_mask = jnp.concatenate([jnp.ones((images, 1), jnp.float32), cell_mask.reshape(images, 81)], axis=1)
    return (cell_mask, key_mask)

def tap_mask(head_ids):
    radius = jnp.where(head_ids < 2, 1, jnp.where(head_ids < 5, 2, 3))
    offsets = jnp.abs(jnp.arange(7, dtype=jnp.int32) - 3)
    within = (offsets[:, None] <= radius[None, :]).astype(jnp.float32)
    return (within[:, None, :] * within[None, :, :]).reshape(49, head_ids.shape[0])

def depthwise(grid_cells, kernel, extent):
    margin = extent // 2
    padded = jnp.pad(grid_cells, ((0, 0), (margin, margin), (margin, margin), (0, 0)))
    summed = jnp.zeros_like(grid_cells)
    for row_at in range(extent):
        for col_at in range(extent):
            summed = summed + padded[:, row_at:row_at + 9, col_at:col_at + 9, :] * kernel[row_at * extent + col_at]
    return summed

def position_conv(stream, kernel, cell_mask):
    images, slot_len, channels = stream.shape
    grid_cells = stream[:, 1:, :].reshape(images, 9, 9, channels) * cell_mask[..., None]
    conv_out = depthwise(grid_cells, kernel, 3) * cell_mask[..., None]
    return stream + jnp.concatenate([jnp.zeros((images, 1, channels), jnp.float32), conv_out.reshape(images, 81, channels)], axis=1)

def layer_norm(values, norm_gain, norm_shift):
    center = values - lax.optimization_barrier(jnp.mean(values, axis=-1, keepdims=True))
    spread = lax.optimization_barrier(jnp.mean(center * center, axis=-1, keepdims=True))
    return center * lax.rsqrt(spread + 1e-06) * norm_gain + norm_shift

def factor_attention(packed, kernel, cell_mask, key_mask):
    images, slot_len, head_count, triple, head_dim = packed.shape
    query_rows = packed[:, :, :, 0]
    key_rows = packed[:, :, :, 1]
    value_rows = packed[:, :, :, 2]
    key_live = key_mask[:, :, None, None]
    top_key = lax.optimization_barrier(jnp.max(jnp.where(key_live > 0, key_rows, -1e+30), axis=1, keepdims=True))
    shifted = jnp.where(key_live > 0, key_rows - top_key, -60.0)
    weights_raw = jnp.exp(shifted) * key_live
    key_weights = weights_raw / lax.optimization_barrier(jnp.sum(weights_raw, axis=1, keepdims=True))
    context = jnp.einsum('nthc,nthd->nhcd', key_weights, value_rows, precision=FULL_PRECISION)
    factor = jnp.einsum('nthc,nhcd->nthd', query_rows, context, precision=FULL_PRECISION) * head_dim ** (-0.5)
    grid_cells = value_rows[:, 1:].reshape(images, 9, 9, head_count * head_dim) * cell_mask[..., None]
    conv_out = depthwise(grid_cells, kernel.reshape(49, head_count * head_dim), 7) * cell_mask[..., None]
    relative = query_rows[:, 1:] * conv_out.reshape(images, 81, head_count, head_dim)
    relative = jnp.concatenate([jnp.zeros_like(query_rows[:, :1]), relative], axis=1)
    return (factor + relative).reshape(images, slot_len, head_count * head_dim)

def attend(packed_rows, kernel_raw, tap_weights, cell_mask, key_mask):
    images = cell_mask.shape[0]
    head_count = tap_weights.shape[1]
    head_dim = kernel_raw.shape[1] // head_count
    total_rows = packed_rows.shape[0]
    kernel = kernel_raw.reshape(49, head_count, head_dim) * tap_weights[:, :, None]
    mixed_heads = factor_attention(packed_rows.reshape(images, total_rows // images, head_count, 3, head_dim), kernel, cell_mask, key_mask)
    return mixed_heads.reshape(total_rows, head_count * head_dim)

def front_part(stream, norm_gain, norm_shift, kernel, cell_mask):
    images = cell_mask.shape[0]
    after_conv = position_conv(stream.reshape(images, stream.shape[0] // images, stream.shape[1]), kernel, cell_mask).reshape(stream.shape)
    return (layer_norm(after_conv, norm_gain, norm_shift), after_conv)

def gelu_exact(values):
    return jax.nn.gelu(values, approximate=False)

def orthogonalize(matrix):
    is_tall = matrix.shape[0] > matrix.shape[1]
    current = matrix.T if is_tall else matrix
    current = current / (jnp.sqrt(jnp.sum(current * current)) + 1e-07)
    first_coef, second_coef, third_coef = SCHULZ_COEFFS
    for sweep_at in range(5):
        gram_matrix = jnp.dot(current, current.T, precision=FULL_PRECISION)
        polynomial = second_coef * gram_matrix + third_coef * jnp.dot(gram_matrix, gram_matrix, precision=FULL_PRECISION)
        current = first_coef * current + jnp.dot(polynomial, current, precision=FULL_PRECISION)
    return current.T if is_tall else current

def column_blocks(matrix, pieces):
    layers, height, breadth = matrix.shape
    return matrix.reshape(layers, height, pieces, breadth // pieces).transpose(0, 2, 1, 3).reshape(layers * pieces, height, breadth // pieces)

def from_column_blocks(blocks, layers, pieces):
    block_count, height, narrow = blocks.shape
    return blocks.reshape(layers, pieces, height, narrow).transpose(0, 2, 1, 3).reshape(layers, height, pieces * narrow)

def row_blocks(matrix, pieces):
    return matrix.reshape(matrix.shape[0] * pieces, matrix.shape[1] // pieces, matrix.shape[2])

def from_row_blocks(blocks, layers, pieces):
    return blocks.reshape(layers, pieces * blocks.shape[1], blocks.shape[2])

def block_scale(height, breadth):
    return math.sqrt(max(1.0, height / breadth))

def normalized_step(param_vals, moment, grads_in, rate, axes):
    fresh = 0.5 * moment + grads_in
    level = jnp.sqrt(lax.optimization_barrier(jnp.mean(fresh * fresh, axis=axes, keepdims=True)))
    return (fresh, param_vals - rate * fresh / (level + 1e-06))

def muon_update(weight, moment, grads_in, blocked, unblocked, rate):
    fresh = 0.5 * moment + grads_in
    ortho = unblocked(jax.vmap(orthogonalize)(blocked(fresh)))
    return (fresh, weight - rate * ortho)

def forward(params, values, cell_mask, key_mask, tap_weights):
    qkv_weight, proj_weight, up_weight, down_weight, norm_params, cpe_weight, crpe_weight = params
    stream = values
    for layer_at in range(LAYERS):
        normed, after_conv = front_part(stream, norm_params[layer_at, 0], norm_params[layer_at, 1], cpe_weight[layer_at], cell_mask)
        normed = low(normed)
        packed = low_back(low(jnp.dot(normed, low(qkv_weight[layer_at]), precision=FULL_PRECISION)))
        mixed_heads = low(attend(packed, crpe_weight[layer_at], tap_weights, cell_mask, key_mask))
        after_att = after_conv + low_back(jnp.dot(mixed_heads, low(proj_weight[layer_at]), precision=FULL_PRECISION))
        normed_mid = low(layer_norm(after_att, norm_params[layer_at, 2], norm_params[layer_at, 3]))
        hidden = low_back(jnp.dot(normed_mid, low(up_weight[layer_at]), precision=FULL_PRECISION))
        active = low(gelu_exact(hidden))
        stream = after_att + low_back(jnp.dot(active, low(down_weight[layer_at]), precision=FULL_PRECISION))
    return stream

def reference(tokens, cotangent, grid_class, qkv_weight, proj_weight, up_weight, down_weight, norm_params, cpe_weight, crpe_weight, qkv_moment, proj_moment, up_moment, down_moment, norm_moment, cpe_moment, crpe_moment):
    params = (qkv_weight, proj_weight, up_weight, down_weight, norm_params, cpe_weight, crpe_weight)
    tap_weights = tap_mask(jnp.arange(HEADS, dtype=jnp.int32))
    steps_count = IMAGES // 8
    stream_blocks = tokens.astype(jnp.float32).reshape(steps_count, 8 * SLOT, D)
    cot_blocks = cotangent.reshape(steps_count, 8 * SLOT, D)
    class_blocks = grid_class.reshape(steps_count, 8)

    def one_block(totals, item_set):
        stream, cot_rows, classes = item_set
        cell_mask, key_mask = spatial_masks(classes)
        result, pullback = jax.vjp(lambda weights, values: forward(weights, values, cell_mask, key_mask, tap_weights), params, stream)
        weight_grads, input_grad = pullback(cot_rows * key_mask.reshape(8 * SLOT)[:, None])
        totals = jax.tree.map(lambda former, latter: former + latter, totals, weight_grads)
        return (totals, (result, input_grad))
    zero_grads = jax.tree.map(jnp.zeros_like, params)
    weight_sums, (results, input_grads) = lax.scan(one_block, zero_grads, (stream_blocks, cot_blocks, class_blocks))
    block_out = results.reshape(TOKENS, D).astype(jnp.bfloat16)
    tokens_grad = input_grads.reshape(TOKENS, D)
    qkv_fresh, qkv_new = muon_update(qkv_weight, qkv_moment, weight_sums[0], partial(column_blocks, pieces=HEADS), partial(from_column_blocks, layers=LAYERS, pieces=HEADS), MUON_RATES[0] * block_scale(D, 3 * HD))
    proj_fresh, proj_new = muon_update(proj_weight, proj_moment, weight_sums[1], partial(row_blocks, pieces=HEADS), partial(from_row_blocks, layers=LAYERS, pieces=HEADS), MUON_RATES[1] * block_scale(HD, D))
    up_fresh, up_new = muon_update(up_weight, up_moment, weight_sums[2], partial(column_blocks, pieces=GROUPS), partial(from_column_blocks, layers=LAYERS, pieces=GROUPS), MUON_RATES[2] * block_scale(D, GROUP_W))
    down_fresh, down_new = muon_update(down_weight, down_moment, weight_sums[3], partial(row_blocks, pieces=GROUPS), partial(from_row_blocks, layers=LAYERS, pieces=GROUPS), MUON_RATES[3] * block_scale(GROUP_W, D))
    norm_fresh, norm_new = normalized_step(norm_params, norm_moment, weight_sums[4], SMALL_RATES[0], (2,))
    conv_fresh, conv_new = normalized_step(cpe_weight, cpe_moment, weight_sums[5], SMALL_RATES[1], (1, 2))
    head_shape = (LAYERS, 49, HEADS, HD)
    kernel_fresh, kernel_new = normalized_step(crpe_weight.reshape(head_shape), crpe_moment.reshape(head_shape), weight_sums[6].reshape(head_shape), SMALL_RATES[2], (1, 3))
    return (block_out, tokens_grad, qkv_fresh, qkv_new, qkv_new.astype(jnp.bfloat16), proj_fresh, proj_new, proj_new.astype(jnp.bfloat16), up_fresh, up_new, up_new.astype(jnp.bfloat16), down_fresh, down_new, down_new.astype(jnp.bfloat16), norm_fresh, norm_new, conv_fresh, conv_new, kernel_fresh.reshape(LAYERS, 49, D), kernel_new.reshape(LAYERS, 49, D))
```

```python
import math

import jax
import jax.numpy as jnp
from jax import lax
from jax.experimental import pallas as pl
from jax.experimental.pallas import tpu as pltpu
from jax.sharding import PartitionSpec as P

HEADS = 8
GROUPS = 8
SLOT = 82
SIDE = 9
LANES = 128
IMGS = 8
ROWS = SLOT * IMGS
SCHULZ_COEFFS = (3.4445, -4.775, 2.0315)
MUON_RATES = (0.8, 0.8, 0.8, 0.4)
SMALL_RATES = (0.3, 0.3, 0.15)
VMEM_BYTES = 60 * 1024 * 1024
F32 = jnp.float32
BF16 = jnp.bfloat16


def mm(a, b):
    return jnp.dot(a, b, preferred_element_type=F32)


def mm_nt(a, b):
    return lax.dot_general(a, b, (((1,), (1,)), ((), ())), preferred_element_type=F32)


def mm_tn(a, b):
    return lax.dot_general(a, b, (((0,), (0,)), ((), ())), preferred_element_type=F32)


def tap_mask(head_ids):
    radius = jnp.where(head_ids < 2, 1, jnp.where(head_ids < 5, 2, 3))
    offsets = jnp.abs(jnp.arange(7, dtype=jnp.int32) - 3)
    within = (offsets[:, None] <= radius[None, :]).astype(F32)
    return (within[:, None, :] * within[None, :, :]).reshape(49, head_ids.shape[0])


def tile_radius(lane_at, head_dim):
    last = ((lane_at + 1) * LANES - 1) // head_dim
    return 1 if last < 2 else (2 if last < 5 else 3)


def normalize(values):
    center = values - jnp.mean(values, axis=-1, keepdims=True)
    spread = jnp.mean(center * center, axis=-1, keepdims=True)
    inv = lax.rsqrt(spread + 1e-06)
    return center * inv, inv


def norm_back(grad, unit, inv, gain):
    scaled = grad * gain
    first = jnp.mean(scaled, axis=-1, keepdims=True)
    second = jnp.mean(scaled * unit, axis=-1, keepdims=True)
    return inv * (scaled - first - unit * second)


def lane(at):
    return slice(at * LANES, (at + 1) * LANES)


def grid_rows(row_at):
    return pl.ds(pl.multiple_of((1 + SIDE * row_at) * IMGS, IMGS), SIDE * IMGS)


def conv_row(padded_ref, kernel_ref, cols, row_at, pad, reach, width, flip):
    mid = width // 2
    acc = [None] * SIDE
    for down in range(-reach, reach + 1):
        line = padded_ref[row_at + pad + down]
        for along in range(-reach, reach + 1):
            tap = (mid - down, mid - along) if flip else (mid + down, mid + along)
            weight = kernel_ref[pl.ds(tap[0] * width + tap[1], 1), cols]
            weight = jnp.broadcast_to(weight, (IMGS, LANES))
            for col in range(SIDE):
                if 0 <= col + along < SIDE:
                    term = line[col + along] * weight
                    acc[col] = term if acc[col] is None else acc[col] + term
    return jnp.concatenate(acc, axis=0)


def conv_kernel_grad(grad_ref, padded_ref, total_ref, cols, pad, reach, width, grad_pad):
    mid = width // 2

    def one(step, carry):
        down = step - reach
        acc = [None] * (2 * reach + 1)
        for row_at in range(SIDE):
            grad_line = grad_ref[row_at + grad_pad]
            line = padded_ref[row_at + pad + down]
            for along in range(-reach, reach + 1):
                for col in range(SIDE):
                    if 0 <= col + along < SIDE:
                        term = grad_line[col] * line[col + along]
                        at = along + reach
                        acc[at] = term if acc[at] is None else acc[at] + term
        for along in range(-reach, reach + 1):
            total_ref[(mid + down) * width + mid + along, :, cols] += acc[along + reach]
        return carry

    lax.fori_loop(0, 2 * reach + 1, one, 0)


def key_softmax(key_tile, mask_tile):
    keys = key_tile.reshape(SLOT, IMGS, LANES)
    live = mask_tile.reshape(SLOT, IMGS, LANES)
    top = jnp.max(jnp.where(live > 0, keys, -1e30), axis=0, keepdims=True)
    raw = jnp.exp(jnp.where(live > 0, keys - top, -60.0)) * live
    return (raw / jnp.sum(raw, axis=0, keepdims=True)).reshape(ROWS, LANES)


def head_mask(size, head_dim):
    down = lax.broadcasted_iota(jnp.int32, (size, size), 0) // head_dim
    along = lax.broadcasted_iota(jnp.int32, (size, size), 1) // head_dim
    return jnp.where(down == along, F32(head_dim ** -0.5), F32(0.0))


def image_rows(ref, quad, image):
    rows = pl.ds(image, SLOT, stride=IMGS)
    return jnp.concatenate([ref[2 * quad, rows, :], ref[2 * quad + 1, rows, :]], axis=1)


def put_image_rows(ref, quad, image, values):
    rows = pl.ds(image, SLOT, stride=IMGS)
    ref[2 * quad, rows, :] = values[:, :LANES]
    ref[2 * quad + 1, rows, :] = values[:, LANES:]


def attend_forward(
    x_ref, mask_ref, qkv_ref, proj_ref, norm_ref, cpe_ref, crpe_ref,
    conv_ref, packed_ref, rel_ref, mixed_ref, att_ref,
    x_pad, v_pad, q_s, k_s, v_s, f_s, c_s,
):
    channels = x_ref.shape[1]
    tiles = channels // LANES
    head_dim = channels // HEADS

    @pl.when(pl.program_id(0) == 0)
    def _():
        x_pad[...] = jnp.zeros_like(x_pad)
        v_pad[...] = jnp.zeros_like(v_pad)

    mask = mask_ref[...]
    for at in range(tiles):
        cols = lane(at)
        masked = x_ref[:, cols] * mask
        x_pad[1 : 1 + SIDE] = masked[IMGS:].reshape(SIDE, SIDE, IMGS, LANES)
        conv_ref[:IMGS, cols] = x_ref[:IMGS, cols]

        def conv_step(row_at, carry):
            rows = grid_rows(row_at)
            out = conv_row(x_pad, cpe_ref, cols, row_at, 1, 1, 3, False)
            conv_ref[rows, cols] = x_ref[rows, cols] + out * mask_ref[rows, :]
            return carry

        lax.fori_loop(0, SIDE, conv_step, 0)
    unit, _ = normalize(conv_ref[...])
    normed = (unit * norm_ref[0:1, :] + norm_ref[1:2, :]).astype(BF16)
    for third, keep in enumerate((q_s, k_s, v_s)):
        part = mm(normed, qkv_ref[:, third * channels : (third + 1) * channels]).astype(BF16)
        packed_ref[:, third * channels : (third + 1) * channels] = part
        part = part.astype(F32)
        for at in range(tiles):
            keep[at] = part[:, lane(at)]
    for at in range(tiles):
        k_s[at] = key_softmax(k_s[at], mask_ref[...])
    block = head_mask(2 * LANES, head_dim)

    def one_image(image, carry):
        for quad in range(tiles // 2):
            keys = image_rows(k_s, quad, image).astype(BF16)
            values = image_rows(v_s, quad, image).astype(BF16)
            query = image_rows(q_s, quad, image).astype(BF16)
            context = (mm_tn(keys, values) * block).astype(BF16)
            put_image_rows(f_s, quad, image, mm(query, context))
        return carry

    lax.fori_loop(0, IMGS, one_image, 0)
    for at in range(tiles):
        cols = lane(at)
        masked = v_s[at] * mask_ref[...]
        v_pad[3 : 3 + SIDE] = masked[IMGS:].reshape(SIDE, SIDE, IMGS, LANES)
        c_s[:IMGS, :] = jnp.zeros((IMGS, LANES), F32)
        reach = tile_radius(at, head_dim)

        def rel_step(row_at, carry):
            rows = grid_rows(row_at)
            out = conv_row(v_pad, crpe_ref, cols, row_at, 3, reach, 7, False)
            c_s[rows, :] = out * mask_ref[rows, :]
            return carry

        lax.fori_loop(0, SIDE, rel_step, 0)
        rel = c_s[...]
        rel_ref[:, cols] = rel.astype(BF16)
        mixed_ref[:, cols] = (f_s[at] + q_s[at] * rel).astype(BF16)
    att_ref[...] = conv_ref[...] + mm_nt(mixed_ref[...], proj_ref[...])


def gelu_parts(values):
    size = jnp.abs(values)
    t = 1.0 / (1.0 + (0.3275911 * 0.7071067811865476) * size)
    bell = jnp.exp(-0.5 * values * values)
    poly = 0.5 * 1.061405429
    for coef in (-1.453152027, 1.421413741, -0.284496736, 0.254829592):
        poly = poly * t + 0.5 * coef
    tail = poly * t * bell
    phi = jnp.where(values >= 0, 1.0 - tail, tail)
    return values * phi, phi + (values * 0.3989422804014327) * bell


def feed_forward(att_ref, up_down_ref, norm_ref, out_ref, act_ref, slope_ref, chunk):
    blks, _, both = up_down_ref.shape
    width = both // 2
    att = att_ref[...]
    unit, _ = normalize(att)
    normed = (unit * norm_ref[2:3, :] + norm_ref[3:4, :]).astype(BF16)
    total = att
    for blk in range(blks):
        for at in range(0, width, chunk):
            hidden = mm(normed, up_down_ref[blk, :, at : at + chunk])
            active, slope = gelu_parts(hidden)
            active = active.astype(BF16)
            cols = slice(blk * width + at, blk * width + at + chunk)
            act_ref[:, cols] = active
            slope_ref[:, cols] = slope.astype(BF16)
            total = total + mm_nt(active, up_down_ref[blk, :, width + at : width + at + chunk])
    out_ref[...] = total.astype(out_ref.dtype)


def feed_back(
    up_ref, att_ref, act_ref, slope_ref, up_down_ref, norm_ref,
    gatt_ref, gweight_ref, gnorm_ref, total_s, chunk,
):
    step, steps = pl.program_id(0), pl.num_programs(0)
    blks, _, both = up_down_ref.shape
    width = both // 2

    @pl.when(step == 0)
    def _():
        total_s[...] = jnp.zeros_like(total_s)
        gnorm_ref[...] = jnp.zeros_like(gnorm_ref)

    upstream = up_ref[...]
    unit, inv = normalize(att_ref[...])
    gain = norm_ref[2:3, :]
    normed_t = (unit * gain + norm_ref[3:4, :]).astype(BF16).T
    down_in = upstream.astype(BF16)
    down_t = down_in.T
    grad_mid = None
    for blk in range(blks):
        for at in range(0, width, chunk):
            cols = slice(blk * width + at, blk * width + at + chunk)
            ups = slice(at, at + chunk)
            downs = slice(width + at, width + at + chunk)
            grad_active = mm(down_in, up_down_ref[blk, :, downs])
            grad_hidden = (grad_active * slope_ref[:, cols].astype(F32)).astype(BF16)
            total_s[blk, :, ups] += mm(normed_t, grad_hidden)
            total_s[blk, :, downs] += mm(down_t, act_ref[:, cols])
            part = mm_nt(grad_hidden, up_down_ref[blk, :, ups])
            grad_mid = part if grad_mid is None else grad_mid + part
    gatt_ref[...] = upstream + norm_back(grad_mid, unit, inv, gain)
    gnorm_ref[0:1, :] += jnp.sum(grad_mid * unit, axis=0, keepdims=True)
    gnorm_ref[1:2, :] += jnp.sum(grad_mid, axis=0, keepdims=True)

    @pl.when(step == steps - 1)
    def _():
        gweight_ref[...] = total_s[...].astype(BF16)


def attend_back(
    gatt_ref, x_ref, conv_ref, packed_ref, rel_ref, mixed_ref, mask_ref,
    qkv_ref, proj_ref, norm_ref, cpe_ref, crpe_ref,
    up_ref, gqkv_ref, gproj_ref, gnorm_ref, gcpe_ref, gcrpe_ref,
    qkv_s, proj_s, x_pad, g_pad, v_pad, c_pad, q_s, k_s, v_s, f_s, dq_s, dk_s, dv_s, c_s, gp_s,
):
    channels = x_ref.shape[1]
    tiles = channels // LANES
    head_dim = channels // HEADS
    step, steps = pl.program_id(0), pl.num_programs(0)

    @pl.when(step == 0)
    def _():
        for ref in (x_pad, g_pad, v_pad, c_pad, qkv_s, proj_s, gnorm_ref, gcpe_ref, gcrpe_ref):
            ref[...] = jnp.zeros_like(ref)

    att_in = gatt_ref[...].astype(BF16)
    proj_s[...] += mm(att_in.T, mixed_ref[...])
    grad_mixed = mm(att_in, proj_ref[...])
    for at in range(tiles):
        f_s[at] = grad_mixed[:, lane(at)]
    for third, keep in enumerate((q_s, k_s, v_s)):
        for at in range(tiles):
            cols = slice(third * channels + at * LANES, third * channels + (at + 1) * LANES)
            keep[at] = packed_ref[:, cols].astype(F32)
    for at in range(tiles):
        k_s[at] = key_softmax(k_s[at], mask_ref[...])
    block = head_mask(2 * LANES, head_dim)

    def one_image(image, carry):
        for quad in range(tiles // 2):
            keys = image_rows(k_s, quad, image).astype(BF16)
            values = image_rows(v_s, quad, image).astype(BF16)
            query = image_rows(q_s, quad, image).astype(BF16)
            grads = image_rows(f_s, quad, image).astype(BF16)
            context = (mm_tn(keys, values) * block).astype(BF16)
            grad_context = (mm_tn(query, grads) * block).astype(BF16)
            put_image_rows(dq_s, quad, image, mm_nt(grads, context))
            put_image_rows(dk_s, quad, image, mm_nt(values, grad_context))
            put_image_rows(dv_s, quad, image, mm(keys, grad_context))
        return carry

    lax.fori_loop(0, IMGS, one_image, 0)
    for at in range(tiles):
        cols = lane(at)
        mask = mask_ref[...]
        weights = k_s[at]
        share = weights * dk_s[at]
        total = jnp.sum(share.reshape(SLOT, IMGS, LANES), axis=0, keepdims=True)
        back = share.reshape(SLOT, IMGS, LANES) - weights.reshape(SLOT, IMGS, LANES) * total
        gp_s[:, channels + at * LANES : channels + (at + 1) * LANES] = back.reshape(
            ROWS, LANES
        ).astype(BF16)
        grads = f_s[at]
        gp_s[:, cols] = (dq_s[at] + grads * rel_ref[:, cols].astype(F32)).astype(BF16)
        reach = tile_radius(at, head_dim)
        masked = v_s[at] * mask
        v_pad[3 : 3 + SIDE] = masked[IMGS:].reshape(SIDE, SIDE, IMGS, LANES)
        cgrad = grads * q_s[at] * mask
        c_pad[3 : 3 + SIDE] = cgrad[IMGS:].reshape(SIDE, SIDE, IMGS, LANES)
        c_s[:IMGS, :] = dv_s[at, :IMGS, :]

        def rel_step(row_at, carry):
            rows = grid_rows(row_at)
            out = conv_row(c_pad, crpe_ref, cols, row_at, 3, reach, 7, True)
            c_s[rows, :] = dv_s[at, rows, :] + out * mask_ref[rows, :]
            return carry

        lax.fori_loop(0, SIDE, rel_step, 0)
        conv_kernel_grad(c_pad, v_pad, gcrpe_ref, cols, 3, reach, 7, 3)
        gp_s[:, 2 * channels + at * LANES : 2 * channels + (at + 1) * LANES] = c_s[...].astype(BF16)
    unit, inv = normalize(conv_ref[...])
    gain = norm_ref[0:1, :]
    normed_t = (unit * gain + norm_ref[1:2, :]).astype(BF16).T
    grad_rows = None
    for third in range(3):
        cols = slice(third * channels, (third + 1) * channels)
        part_in = gp_s[:, cols]
        qkv_s[:, cols] += mm(normed_t, part_in)
        part = mm_nt(part_in, qkv_ref[:, cols])
        grad_rows = part if grad_rows is None else grad_rows + part
    gnorm_ref[0:1, :] += jnp.sum(grad_rows * unit, axis=0, keepdims=True)
    gnorm_ref[1:2, :] += jnp.sum(grad_rows, axis=0, keepdims=True)
    up_ref[...] = gatt_ref[...] + norm_back(grad_rows, unit, inv, gain)
    for at in range(tiles):
        cols = lane(at)
        mask = mask_ref[...]
        masked = x_ref[:, cols] * mask
        x_pad[1 : 1 + SIDE] = masked[IMGS:].reshape(SIDE, SIDE, IMGS, LANES)
        gmasked = up_ref[:, cols] * mask
        g_pad[1 : 1 + SIDE] = gmasked[IMGS:].reshape(SIDE, SIDE, IMGS, LANES)

        def conv_step(row_at, carry):
            rows = grid_rows(row_at)
            out = conv_row(g_pad, cpe_ref, cols, row_at, 1, 1, 3, True)
            up_ref[rows, cols] += out * mask_ref[rows, :]
            return carry

        lax.fori_loop(0, SIDE, conv_step, 0)
        conv_kernel_grad(g_pad, x_pad, gcpe_ref, cols, 1, 1, 3, 1)

    @pl.when(step == steps - 1)
    def _():
        gqkv_ref[...] = qkv_s[...].astype(BF16)
        gproj_ref[...] = proj_s[...].astype(BF16)


def schulz(fresh_ref, out_ref, width):
    def dot3(a, b, dims):
        a_hi = a.astype(BF16)
        b_hi = b.astype(BF16)
        a_lo = (a - a_hi.astype(F32)).astype(BF16)
        b_lo = (b - b_hi.astype(F32)).astype(BF16)
        one = lambda u, v: lax.dot_general(u, v, (dims, ((), ())), preferred_element_type=F32)
        return one(a_hi, b_hi) + (one(a_hi, b_lo) + one(a_lo, b_hi))

    first, second, third = SCHULZ_COEFFS
    parts = range(0, fresh_ref.shape[2], width)
    current = []
    for at in parts:
        value = fresh_ref[0, :, at : at + width].astype(F32)
        level = jnp.sum(jnp.sum(value * value, axis=0, keepdims=True), axis=1, keepdims=True)
        current.append(value / (jnp.sqrt(level) + 1e-07))
    for _ in range(5):
        for at, value in enumerate(current):
            gram = dot3(value, value, ((0,), (0,)))
            poly = second * gram + third * dot3(gram, gram, ((1,), (0,)))
            current[at] = first * value + dot3(value, poly, ((1,), (0,)))
    for at, value in zip(parts, current):
        out_ref[0, :, at : at + width] = value.astype(BF16)


def params_for(**more):
    return pltpu.CompilerParams(vmem_limit_bytes=VMEM_BYTES, **more)


def block_of(cols):
    return pl.BlockSpec((ROWS, cols), lambda g: (g, 0))


def whole(array):
    shape = array.shape
    return pl.BlockSpec(shape, lambda g: (0,) * len(shape), pipeline_mode=pl.Buffered(1))


def whole_out(shape):
    return pl.BlockSpec(shape, lambda g: (0,) * len(shape))


def run_attend_forward(x, mask, qkv, proj, norm, cpe, crpe):
    count, channels = x.shape
    tiles = channels // LANES
    flat = pltpu.VMEM((tiles, ROWS, LANES), F32)
    return pl.pallas_call(
        attend_forward,
        grid=(count // ROWS,),
        in_specs=[block_of(channels), block_of(LANES)]
        + [whole(a) for a in (qkv, proj, norm, cpe, crpe)],
        out_specs=[block_of(channels), block_of(3 * channels)] + [block_of(channels)] * 3,
        out_shape=[
            jax.ShapeDtypeStruct((count, channels), F32),
            jax.ShapeDtypeStruct((count, 3 * channels), BF16),
            jax.ShapeDtypeStruct((count, channels), BF16),
            jax.ShapeDtypeStruct((count, channels), BF16),
            jax.ShapeDtypeStruct((count, channels), F32),
        ],
        scratch_shapes=[
            pltpu.VMEM((SIDE + 2, SIDE, IMGS, LANES), F32),
            pltpu.VMEM((SIDE + 6, SIDE, IMGS, LANES), F32),
            flat, flat, flat, flat,
            pltpu.VMEM((ROWS, LANES), F32),
        ],
        compiler_params=params_for(),
        name="attend_forward",
    )(x, mask, qkv, proj, norm, cpe, crpe)


def run_feed_forward(att, up_down, norm, out_type, chunk=256):
    count, channels = att.shape
    hidden = up_down.shape[0] * up_down.shape[2] // 2
    return pl.pallas_call(
        lambda *refs: feed_forward(*refs, chunk=chunk),
        grid=(count // ROWS,),
        in_specs=[block_of(channels), whole(up_down), whole(norm)],
        out_specs=[block_of(channels), block_of(hidden), block_of(hidden)],
        out_shape=[
            jax.ShapeDtypeStruct((count, channels), out_type),
            jax.ShapeDtypeStruct((count, hidden), BF16),
            jax.ShapeDtypeStruct((count, hidden), BF16),
        ],
        compiler_params=params_for(),
        name="feed_forward",
    )(att, up_down, norm)


def run_feed_back(upstream, att, active, slope, up_down, norm, chunk=256):
    count, channels = att.shape
    hidden = active.shape[1]
    return pl.pallas_call(
        lambda *refs: feed_back(*refs, chunk=chunk),
        grid=(count // ROWS,),
        in_specs=[block_of(channels), block_of(channels), block_of(hidden), block_of(hidden)]
        + [whole(up_down), whole(norm)],
        out_specs=[block_of(channels), whole_out(up_down.shape), whole_out((2, channels))],
        out_shape=[
            jax.ShapeDtypeStruct((count, channels), F32),
            jax.ShapeDtypeStruct(up_down.shape, BF16),
            jax.ShapeDtypeStruct((2, channels), F32),
        ],
        scratch_shapes=[pltpu.VMEM(up_down.shape, F32)],
        compiler_params=params_for(),
        name="feed_back",
    )(upstream, att, active, slope, up_down, norm)


def run_attend_back(gatt, x, conv, packed, rel, mixed, mask, qkv, proj, norm, cpe, crpe):
    count, channels = x.shape
    tiles = channels // LANES
    flat = pltpu.VMEM((tiles, ROWS, LANES), F32)
    three = pltpu.VMEM((SIDE + 2, SIDE, IMGS, LANES), F32)
    seven = pltpu.VMEM((SIDE + 6, SIDE, IMGS, LANES), F32)
    small = [(2, channels), (9, IMGS, channels), (49, IMGS, channels)]
    return pl.pallas_call(
        attend_back,
        grid=(count // ROWS,),
        in_specs=[block_of(channels)] * 3
        + [block_of(3 * channels), block_of(channels), block_of(channels), block_of(LANES)]
        + [whole(a) for a in (qkv, proj, norm, cpe, crpe)],
        out_specs=[block_of(channels), whole_out(qkv.shape), whole_out(proj.shape)]
        + [whole_out(shape) for shape in small],
        out_shape=[
            jax.ShapeDtypeStruct((count, channels), F32),
            jax.ShapeDtypeStruct(qkv.shape, BF16),
            jax.ShapeDtypeStruct(proj.shape, BF16),
        ]
        + [jax.ShapeDtypeStruct(shape, F32) for shape in small],
        scratch_shapes=[
            pltpu.VMEM(qkv.shape, F32),
            pltpu.VMEM(proj.shape, F32),
            three, three, seven, seven,
            flat, flat, flat, flat, flat, flat, flat,
            pltpu.VMEM((ROWS, LANES), F32),
            pltpu.VMEM((ROWS, 3 * channels), BF16),
        ],
        compiler_params=params_for(),
        name="attend_back",
    )(gatt, x, conv, packed, rel, mixed, mask, qkv, proj, norm, cpe, crpe)


def run_schulz(fresh, width):
    units, height, both = fresh.shape
    spec = pl.BlockSpec((1, height, both), lambda g: (g, 0, 0))
    return pl.pallas_call(
        lambda *refs: schulz(*refs, width=width),
        grid=(units,),
        in_specs=[spec],
        out_specs=spec,
        out_shape=jax.ShapeDtypeStruct(fresh.shape, BF16),
        compiler_params=params_for(),
        name="schulz",
    )(fresh)


def token_major(rows):
    count, channels = rows.shape
    split = rows.reshape(count // ROWS, IMGS, SLOT, channels)
    return split.transpose(0, 2, 1, 3).reshape(count, channels)


def image_major(rows):
    count, channels = rows.shape
    split = rows.reshape(count // ROWS, SLOT, IMGS, channels)
    return split.transpose(0, 2, 1, 3).reshape(count, channels)


def key_masks(grid_class):
    extent = 5 + 2 * grid_class
    across = (jnp.arange(SIDE, dtype=jnp.int32)[None, :] < extent[:, None]).astype(F32)
    cells = (across[:, :, None] * across[:, None, :]).reshape(-1, SIDE * SIDE)
    return jnp.concatenate([jnp.ones((cells.shape[0], 1), F32), cells], axis=1)


def split_heads(shard, heads_own, head_dim):
    lead = shard.shape[:-1]
    parts = shard.reshape(lead + (heads_own, 3, head_dim))
    return jnp.swapaxes(parts, -3, -2).reshape(lead + (3 * heads_own * head_dim,))


def join_heads(shard, heads_own, head_dim):
    lead = shard.shape[:-1]
    parts = shard.reshape(lead + (3, heads_own, head_dim))
    return jnp.swapaxes(parts, -3, -2).reshape(lead + (3 * heads_own * head_dim,))


def block_scale(height, breadth):
    return math.sqrt(max(1.0, height / breadth))


def normalized_step(param_vals, moment, grads_in, rate, axes):
    fresh = 0.5 * moment + grads_in
    level = jnp.sqrt(jnp.mean(fresh * fresh, axis=axes, keepdims=True))
    return (fresh, param_vals - rate * fresh / (level + 1e-06))


def on_device(
    tokens, cotangent, grid_class,
    qkv_weight, proj_weight, up_weight, down_weight, norm_params, cpe_weight, crpe_weight,
    qkv_moment, proj_moment, up_moment, down_moment, norm_moment, cpe_moment, crpe_moment,
):
    own_count, channels = tokens.shape
    blk_count = lax.axis_size("blk")
    tok_count = lax.axis_size("tok")
    blk_at = lax.axis_index("blk")
    layers = qkv_weight.shape[0]
    images_own = grid_class.shape[0] // blk_count
    head_dim = channels // HEADS
    heads_own = HEADS // blk_count
    groups_own = GROUPS // blk_count
    group_width = up_weight.shape[2] // groups_own
    own_rows = qkv_weight.shape[1]
    both = ("blk", "tok")

    attn_shard = jnp.concatenate(
        [split_heads(qkv_weight, heads_own, head_dim), jnp.swapaxes(proj_weight, 1, 2)], axis=2
    )
    feed_shard = jnp.concatenate([up_weight, jnp.swapaxes(down_weight, 1, 2)], axis=2)
    qkv_all, proj_all, feed_all = [], [], []
    for layer in range(layers):
        attn = lax.all_gather(attn_shard[layer].astype(BF16), both, axis=0, tiled=True)
        attn = attn.reshape(blk_count, channels, 4, heads_own * head_dim)
        attn = attn.transpose(1, 2, 0, 3).reshape(channels, 4 * channels)
        qkv_all.append(attn[:, : 3 * channels])
        proj_all.append(attn[:, 3 * channels :])
        feed = lax.all_gather(feed_shard[layer].astype(BF16), both, axis=0, tiled=True)
        feed_all.append(feed.reshape(blk_count, channels, feed.shape[1]))

    own_class = lax.dynamic_slice_in_dim(grid_class, blk_at * images_own, images_own)
    keys = key_masks(own_class)
    mask = jnp.broadcast_to(
        token_major(keys.reshape(own_count, 1)), (own_count, LANES)
    )
    taps = jnp.repeat(tap_mask(jnp.arange(HEADS, dtype=jnp.int32)), head_dim, axis=1)

    stream = token_major(tokens).astype(F32)
    saved = []
    for layer in range(layers):
        crpe = crpe_weight[layer] * taps
        conv, packed, rel, mixed, att = run_attend_forward(
            stream, mask, qkv_all[layer], proj_all[layer], norm_params[layer],
            cpe_weight[layer], crpe,
        )
        last = layer == layers - 1
        out, active, slope = run_feed_forward(
            att, feed_all[layer], norm_params[layer], BF16 if last else F32
        )
        saved.append((stream, conv, packed, rel, mixed, att, active, slope, crpe))
        stream = out
    block_out = image_major(stream)

    upstream = token_major(cotangent * keys.reshape(own_count, 1))
    attn_sums, feed_sums = [None] * layers, [None] * layers
    small_rows = 4 + 9 + 49
    for layer in reversed(range(layers)):
        x, conv, packed, rel, mixed, att, active, slope, crpe = saved[layer]
        gatt, gfeed, gmid = run_feed_back(
            upstream, att, active, slope, feed_all[layer], norm_params[layer]
        )
        feed_sums[layer] = lax.psum_scatter(
            gfeed.reshape(blk_count * channels, gfeed.shape[2]), both,
            scatter_dimension=0, tiled=True,
        ).astype(F32)
        upstream, gqkv, gproj, gfront, gcpe, gcrpe = run_attend_back(
            gatt, x, conv, packed, rel, mixed, mask, qkv_all[layer], proj_all[layer],
            norm_params[layer], cpe_weight[layer], crpe,
        )
        small = jnp.concatenate([gfront, gmid, gcpe.sum(1), gcrpe.sum(1) * taps], axis=0)
        small = jnp.pad(small, ((0, LANES - small_rows), (0, 0))).T.astype(BF16)
        grads = jnp.concatenate([gqkv, gproj], axis=1)
        grads = grads.reshape(channels, 4, blk_count, heads_own * head_dim)
        grads = grads.transpose(2, 0, 1, 3).reshape(blk_count, channels, 4 * heads_own * head_dim)
        grads = jnp.concatenate(
            [grads, jnp.broadcast_to(small, (blk_count, channels, LANES))], axis=2
        )
        attn_sums[layer] = lax.psum_scatter(
            grads.reshape(blk_count * channels, grads.shape[2]), both,
            scatter_dimension=0, tiled=True,
        ).astype(F32)
    tokens_grad = image_major(upstream)

    attn_sum = jnp.stack(attn_sums)
    feed_sum = jnp.stack(feed_sums)
    small_sum = attn_sum[:, :, -LANES:][:, :, :small_rows]
    attn_sum = attn_sum[:, :, :-LANES]
    attn_moment = jnp.concatenate(
        [split_heads(qkv_moment, heads_own, head_dim), jnp.swapaxes(proj_moment, 1, 2)], axis=2
    )
    feed_moment = jnp.concatenate([up_moment, jnp.swapaxes(down_moment, 1, 2)], axis=2)
    attn_fresh = 0.5 * attn_moment + attn_sum
    feed_fresh = 0.5 * feed_moment + feed_sum

    units = layers * 2 * groups_own
    per_dev = -(-units // tok_count)
    big = feed_fresh.reshape(layers, own_rows, 2 * groups_own, group_width)
    big = big.transpose(0, 2, 1, 3).reshape(units, own_rows, group_width)
    heads = attn_fresh.reshape(layers, own_rows, 4, heads_own, head_dim).transpose(0, 3, 1, 2, 4)
    heads_qkv = heads[:, :, :, :3].reshape(layers, heads_own, own_rows, 3 * head_dim)
    heads_proj = heads[:, :, :, 3]
    widen = lambda v: jnp.pad(v, ((0, 0), (0, 0), (0, 0), (0, group_width - v.shape[3])))
    little = jnp.concatenate([widen(heads_qkv), widen(heads_proj)], axis=1)
    little = little.reshape(units, own_rows, group_width)
    send = jnp.concatenate([big, little], axis=2).astype(BF16)
    send = jnp.pad(send, ((0, per_dev * tok_count - units), (0, 0), (0, 0)))
    send = send.reshape(tok_count, per_dev, own_rows, 2 * group_width)
    got = lax.all_to_all(send, "tok", 0, 0, tiled=True)
    got = got.transpose(1, 0, 2, 3).reshape(per_dev, channels, 2 * group_width)
    ortho = run_schulz(got, group_width)
    ortho = ortho.reshape(per_dev, tok_count, own_rows, 2 * group_width).transpose(1, 0, 2, 3)
    ortho = lax.all_to_all(ortho, "tok", 0, 0, tiled=True)
    ortho = ortho.reshape(per_dev * tok_count, own_rows, 2 * group_width)[:units].astype(F32)
    big = ortho[:, :, :group_width].reshape(layers, 2, groups_own, own_rows, group_width)
    big = big.transpose(1, 0, 3, 2, 4).reshape(2, layers, own_rows, groups_own * group_width)
    little = ortho[:, :, group_width:].reshape(layers, 2, heads_own, own_rows, group_width)
    little_qkv = little[:, 0, :, :, : 3 * head_dim].transpose(0, 2, 1, 3)
    little_qkv = little_qkv.reshape(layers, own_rows, heads_own * 3 * head_dim)
    little_proj = little[:, 1, :, :, :head_dim].transpose(0, 1, 3, 2)
    little_proj = little_proj.reshape(layers, heads_own * head_dim, own_rows)

    qkv_fresh = join_heads(attn_fresh[:, :, : qkv_weight.shape[2]], heads_own, head_dim)
    proj_fresh = jnp.swapaxes(attn_fresh[:, :, qkv_weight.shape[2] :], 1, 2)
    up_fresh = feed_fresh[:, :, : up_weight.shape[2]]
    down_fresh = jnp.swapaxes(feed_fresh[:, :, up_weight.shape[2] :], 1, 2)
    scales = (
        block_scale(channels, 3 * head_dim),
        block_scale(head_dim, channels),
        block_scale(channels, group_width),
        block_scale(group_width, channels),
    )
    results = []
    for kind, (weight, fresh, turned) in enumerate(
        (
            (qkv_weight, qkv_fresh, little_qkv),
            (proj_weight, proj_fresh, little_proj),
            (up_weight, up_fresh, big[0]),
            (down_weight, down_fresh, jnp.swapaxes(big[1], 1, 2)),
        )
    ):
        new = weight - MUON_RATES[kind] * scales[kind] * turned
        results.extend([fresh, new, new.astype(BF16)])

    small_all = lax.all_gather(small_sum.astype(BF16), "tok", axis=1, tiled=True)
    small_all = jnp.swapaxes(small_all, 1, 2).astype(F32)
    norm_fresh, norm_new = normalized_step(
        norm_params, norm_moment, small_all[:, :4], SMALL_RATES[0], (2,)
    )
    cpe_fresh, cpe_new = normalized_step(
        cpe_weight, cpe_moment, small_all[:, 4:13], SMALL_RATES[1], (1, 2)
    )
    head_shape = (layers, 49, HEADS, head_dim)
    crpe_fresh, crpe_new = normalized_step(
        crpe_weight.reshape(head_shape),
        crpe_moment.reshape(head_shape),
        small_all[:, 13:].reshape(head_shape),
        SMALL_RATES[2],
        (1, 3),
    )
    return (
        (block_out, tokens_grad)
        + tuple(results)
        + (norm_fresh, norm_new, cpe_fresh, cpe_new)
        + (crpe_fresh.reshape(crpe_weight.shape), crpe_new.reshape(crpe_weight.shape))
    )


def solution(mesh):
    rows = P(("tok", "blk"), None)
    down_cols = P(None, "tok", "blk")
    cross = P(None, "blk", "tok")
    mats = (down_cols, cross, down_cols, cross)
    in_specs = (rows, rows, P("tok")) + mats + (P(),) * 3 + mats + (P(),) * 3
    out_specs = (rows, rows) + tuple(spec for spec in mats for _ in range(3)) + (P(),) * 6
    return jax.shard_map(
        on_device, mesh=mesh, in_specs=in_specs, out_specs=out_specs, check_vma=False
    )
```

```python
import functools
import math

import jax
import jax.numpy as jnp
from jax import lax
from jax.experimental import pallas as pl
from jax.experimental.pallas import tpu as pltpu
from jax.sharding import PartitionSpec as P

HEADS = 8
GROUPS = 8
SLOT = 82
SIDE = 9
LANES = 128
IMGS = 8
ROWS = SLOT * IMGS
SCHULZ_COEFFS = (3.4445, -4.775, 2.0315)
MUON_RATES = (0.8, 0.8, 0.8, 0.4)
SMALL_RATES = (0.3, 0.3, 0.15)
VMEM_BYTES = 60 * 1024 * 1024
F32 = jnp.float32
BF16 = jnp.bfloat16


def mm(a, b):
    return jnp.dot(a, b, preferred_element_type=F32)


def mm_nt(a, b):
    return lax.dot_general(a, b, (((1,), (1,)), ((), ())), preferred_element_type=F32)


def mm_tn(a, b):
    return lax.dot_general(a, b, (((0,), (0,)), ((), ())), preferred_element_type=F32)


def tap_mask(head_ids):
    radius = jnp.where(head_ids < 2, 1, jnp.where(head_ids < 5, 2, 3))
    offsets = jnp.abs(jnp.arange(7, dtype=jnp.int32) - 3)
    within = (offsets[:, None] <= radius[None, :]).astype(F32)
    return (within[:, None, :] * within[None, :, :]).reshape(49, head_ids.shape[0])


def tile_radius(lane_at, head_dim):
    last = ((lane_at + 1) * LANES - 1) // head_dim
    return 1 if last < 2 else (2 if last < 5 else 3)


def normalize(values):
    center = values - jnp.mean(values, axis=-1, keepdims=True)
    spread = jnp.mean(center * center, axis=-1, keepdims=True)
    inv = lax.rsqrt(spread + 1e-06)
    return center * inv, inv


def norm_back(grad, unit, inv, gain):
    scaled = grad * gain
    first = jnp.mean(scaled, axis=-1, keepdims=True)
    second = jnp.mean(scaled * unit, axis=-1, keepdims=True)
    return inv * (scaled - first - unit * second)


def lane(at):
    return slice(at * LANES, (at + 1) * LANES)


def grid_rows(row_at):
    return pl.ds(pl.multiple_of((1 + SIDE * row_at) * IMGS, IMGS), SIDE * IMGS)


def conv_row(padded_ref, kernel_ref, cols, row_at, pad, reach, width, flip):
    mid = width // 2
    acc = [None] * SIDE
    for down in range(-reach, reach + 1):
        line = padded_ref[row_at + pad + down]
        for along in range(-reach, reach + 1):
            tap = (mid - down, mid - along) if flip else (mid + down, mid + along)
            weight = kernel_ref[pl.ds(tap[0] * width + tap[1], 1), cols]
            weight = jnp.broadcast_to(weight, (IMGS, LANES))
            for col in range(SIDE):
                if 0 <= col + along < SIDE:
                    term = line[col + along] * weight
                    acc[col] = term if acc[col] is None else acc[col] + term
    return jnp.concatenate(acc, axis=0)


def conv_kernel_grad(grad_ref, padded_ref, total_ref, cols, pad, reach, width, grad_pad):
    mid = width // 2

    def one(step, carry):
        down = step - reach
        acc = [None] * (2 * reach + 1)
        for row_at in range(SIDE):
            grad_line = grad_ref[row_at + grad_pad]
            line = padded_ref[row_at + pad + down]
            for along in range(-reach, reach + 1):
                for col in range(SIDE):
                    if 0 <= col + along < SIDE:
                        term = grad_line[col] * line[col + along]
                        at = along + reach
                        acc[at] = term if acc[at] is None else acc[at] + term
        for along in range(-reach, reach + 1):
            total_ref[(mid + down) * width + mid + along, :, cols] += acc[along + reach]
        return carry

    lax.fori_loop(0, 2 * reach + 1, one, 0)


def key_softmax(key_tile, mask_tile):
    keys = key_tile.reshape(SLOT, IMGS, LANES)
    live = mask_tile.reshape(SLOT, IMGS, LANES)
    top = jnp.max(jnp.where(live > 0, keys, -1e30), axis=0, keepdims=True)
    raw = jnp.exp(jnp.where(live > 0, keys - top, -60.0)) * live
    return (raw / jnp.sum(raw, axis=0, keepdims=True)).reshape(ROWS, LANES)


def head_mask(size, head_dim):
    down = lax.broadcasted_iota(jnp.int32, (size, size), 0) // head_dim
    along = lax.broadcasted_iota(jnp.int32, (size, size), 1) // head_dim
    return jnp.where(down == along, F32(head_dim ** -0.5), F32(0.0))


def image_rows(ref, quad, image):
    rows = pl.ds(image, SLOT, stride=IMGS)
    return jnp.concatenate([ref[2 * quad, rows, :], ref[2 * quad + 1, rows, :]], axis=1)


def put_image_rows(ref, quad, image, values):
    rows = pl.ds(image, SLOT, stride=IMGS)
    ref[2 * quad, rows, :] = values[:, :LANES]
    ref[2 * quad + 1, rows, :] = values[:, LANES:]


def to_token_major(src_ref, put):
    for token in range(SLOT):
        put(slice(token * IMGS, (token + 1) * IMGS), src_ref[pl.ds(token, IMGS, stride=SLOT), :])


def to_image_major(src_ref, put):
    for image in range(IMGS):
        put(slice(image * SLOT, (image + 1) * SLOT), src_ref[pl.ds(image, SLOT, stride=IMGS), :])


def attend_forward(*refs, first):
    if first:
        tokens_ref, refs = refs[0], refs[1:]
        (mask_ref, w_ref, norm_ref, cpe_ref, crpe_ref, x_ref, conv_ref, packed_ref, rel_ref,
         mixed_ref, att_ref, x_pad, v_pad, q_s, k_s, v_s, f_s, c_s) = refs
    else:
        (x_ref, mask_ref, w_ref, norm_ref, cpe_ref, crpe_ref, conv_ref, packed_ref, rel_ref,
         mixed_ref, att_ref, x_pad, v_pad, q_s, k_s, v_s, f_s, c_s) = refs
    channels = x_ref.shape[1]
    tiles = channels // LANES
    head_dim = channels // HEADS
    half = channels // 2

    @pl.when(pl.program_id(0) == 0)
    def _():
        x_pad[...] = jnp.zeros_like(x_pad)
        v_pad[...] = jnp.zeros_like(v_pad)

    if first:
        for at in range(tiles):
            cols = lane(at)
            f_s[at] = tokens_ref[:, cols].astype(F32)

            def put(rows, values, cols=cols):
                x_ref[rows, cols] = values

            to_token_major(f_s.at[at], put)
    mask = mask_ref[...]
    for at in range(tiles):
        cols = lane(at)
        masked = x_ref[:, cols] * mask
        x_pad[1 : 1 + SIDE] = masked[IMGS:].reshape(SIDE, SIDE, IMGS, LANES)
        conv_ref[:IMGS, cols] = x_ref[:IMGS, cols]

        def conv_step(row_at, carry):
            rows = grid_rows(row_at)
            out = conv_row(x_pad, cpe_ref, cols, row_at, 1, 1, 3, False)
            conv_ref[rows, cols] = x_ref[rows, cols] + out * mask_ref[rows, :]
            return carry

        lax.fori_loop(0, SIDE, conv_step, 0)
    unit, _ = normalize(conv_ref[...])
    normed = (unit * norm_ref[0:1, :] + norm_ref[1:2, :]).astype(BF16)
    for side in range(2):
        for third, keep in enumerate((q_s, k_s, v_s)):
            cols = slice(third * half, (third + 1) * half)
            part = mm(normed, w_ref[side, :, cols]).astype(BF16)
            packed_ref[:, side * 3 * half + third * half : side * 3 * half + (third + 1) * half] = part
            part = part.astype(F32)
            for at in range(tiles // 2):
                keep[side * (tiles // 2) + at] = part[:, lane(at)]
    for at in range(tiles):
        k_s[at] = key_softmax(k_s[at], mask_ref[...])
    block = head_mask(2 * LANES, head_dim)

    def one_image(image, carry):
        for quad in range(tiles // 2):
            keys = image_rows(k_s, quad, image).astype(BF16)
            values = image_rows(v_s, quad, image).astype(BF16)
            query = image_rows(q_s, quad, image).astype(BF16)
            context = (mm_tn(keys, values) * block).astype(BF16)
            put_image_rows(f_s, quad, image, mm(query, context))
        return carry

    lax.fori_loop(0, IMGS, one_image, 0)
    for at in range(tiles):
        cols = lane(at)
        masked = v_s[at] * mask_ref[...]
        v_pad[3 : 3 + SIDE] = masked[IMGS:].reshape(SIDE, SIDE, IMGS, LANES)
        c_s[:IMGS, :] = jnp.zeros((IMGS, LANES), F32)
        reach = tile_radius(at, head_dim)

        def rel_step(row_at, carry):
            rows = grid_rows(row_at)
            out = conv_row(v_pad, crpe_ref, cols, row_at, 3, reach, 7, False)
            c_s[rows, :] = out * mask_ref[rows, :]
            return carry

        lax.fori_loop(0, SIDE, rel_step, 0)
        rel = c_s[...]
        rel_ref[:, cols] = rel.astype(BF16)
        mixed_ref[:, cols] = (f_s[at] + q_s[at] * rel).astype(BF16)
    out = conv_ref[...]
    for side in range(2):
        cols = slice(side * half, (side + 1) * half)
        out = out + mm_nt(mixed_ref[:, cols], w_ref[side, :, 3 * half :])
    att_ref[...] = out


def gelu_parts(values):
    size = jnp.abs(values)
    t = 1.0 / (1.0 + (0.3275911 * 0.7071067811865476) * size)
    bell = jnp.exp(-0.5 * values * values)
    poly = 0.5 * 1.061405429
    for coef in (-1.453152027, 1.421413741, -0.284496736, 0.254829592):
        poly = poly * t + 0.5 * coef
    tail = poly * t * bell
    phi = jnp.where(values >= 0, 1.0 - tail, tail)
    return values * phi, phi + (values * 0.3989422804014327) * bell


def feed_forward(att_ref, up_down_ref, norm_ref, out_ref, act_ref, slope_ref, *scratch, chunk):
    blks, _, both = up_down_ref.shape
    width = both // 2
    att = att_ref[...]
    unit, _ = normalize(att)
    normed = (unit * norm_ref[2:3, :] + norm_ref[3:4, :]).astype(BF16)
    total = att
    for blk in range(blks):
        for at in range(0, width, chunk):
            hidden = mm(normed, up_down_ref[blk, :, at : at + chunk])
            active, slope = gelu_parts(hidden)
            active = active.astype(BF16)
            cols = slice(blk * width + at, blk * width + at + chunk)
            act_ref[:, cols] = active
            slope_ref[:, cols] = slope.astype(BF16)
            total = total + mm_nt(active, up_down_ref[blk, :, width + at : width + at + chunk])
    if not scratch:
        out_ref[...] = total
        return
    turn_s, whole_s = scratch
    for at in range(att.shape[1] // LANES):
        cols = lane(at)
        turn_s[...] = total[:, cols]

        def put(rows, values, cols=cols):
            whole_s[rows, cols] = values

        to_image_major(turn_s, put)
    out_ref[...] = whole_s[...].astype(BF16)


def feed_back(*refs, first, chunk):
    if first:
        mask_ref, refs = refs[0], refs[1:]
    (up_ref, att_ref, act_ref, slope_ref, up_down_ref, norm_ref,
     gatt_ref, gweight_ref, gnorm_ref, total_s) = refs[:10]
    step, steps = pl.program_id(0), pl.num_programs(0)
    blks, _, both = up_down_ref.shape
    width = both // 2

    @pl.when(step == 0)
    def _():
        total_s[...] = jnp.zeros_like(total_s)
        gnorm_ref[...] = jnp.zeros_like(gnorm_ref)

    if first:
        turn_s, whole_s = refs[10:]
        for at in range(up_ref.shape[1] // LANES):
            cols = lane(at)
            turn_s[...] = up_ref[:, cols]

            def put(rows, values, cols=cols):
                whole_s[rows, cols] = values * mask_ref[rows, :]

            to_token_major(turn_s, put)
        upstream = whole_s[...]
    else:
        upstream = up_ref[...]
    unit, inv = normalize(att_ref[...])
    gain = norm_ref[2:3, :]
    normed_t = (unit * gain + norm_ref[3:4, :]).astype(BF16).T
    down_in = upstream.astype(BF16)
    down_t = down_in.T
    grad_mid = None
    for blk in range(blks):
        for at in range(0, width, chunk):
            cols = slice(blk * width + at, blk * width + at + chunk)
            ups = slice(at, at + chunk)
            downs = slice(width + at, width + at + chunk)
            grad_active = mm(down_in, up_down_ref[blk, :, downs])
            grad_hidden = (grad_active * slope_ref[:, cols].astype(F32)).astype(BF16)
            total_s[blk, :, ups] += mm(normed_t, grad_hidden)
            total_s[blk, :, downs] += mm(down_t, act_ref[:, cols])
            part = mm_nt(grad_hidden, up_down_ref[blk, :, ups])
            grad_mid = part if grad_mid is None else grad_mid + part
    gatt_ref[...] = upstream + norm_back(grad_mid, unit, inv, gain)
    gnorm_ref[0:1, :] += jnp.sum(grad_mid * unit, axis=0, keepdims=True)
    gnorm_ref[1:2, :] += jnp.sum(grad_mid, axis=0, keepdims=True)

    @pl.when(step == steps - 1)
    def _():
        gweight_ref[...] = total_s[...].astype(BF16)


def attend_back(
    gatt_ref, x_ref, conv_ref, packed_ref, rel_ref, mixed_ref, mask_ref,
    w_ref, norm_ref, cpe_ref, crpe_ref,
    out_ref, gw_ref, gnorm_ref, gcpe_ref, gcrpe_ref,
    w_s, x_pad, g_pad, v_pad, c_pad, q_s, k_s, v_s, f_s, dq_s, dk_s, dv_s, c_s, gp_s,
    *scratch,
):
    channels = x_ref.shape[1]
    tiles = channels // LANES
    head_dim = channels // HEADS
    half = channels // 2
    step, steps = pl.program_id(0), pl.num_programs(0)
    up_ref = scratch[0] if scratch else out_ref

    @pl.when(step == 0)
    def _():
        for ref in (x_pad, g_pad, v_pad, c_pad, w_s, gnorm_ref, gcpe_ref, gcrpe_ref):
            ref[...] = jnp.zeros_like(ref)

    att_in = gatt_ref[...].astype(BF16)
    att_t = att_in.T
    for side in range(2):
        cols = slice(side * half, (side + 1) * half)
        w_s[side, :, 3 * half :] += mm(att_t, mixed_ref[:, cols])
        grad_mixed = mm(att_in, w_ref[side, :, 3 * half :])
        for at in range(tiles // 2):
            f_s[side * (tiles // 2) + at] = grad_mixed[:, lane(at)]
        for third, keep in enumerate((q_s, k_s, v_s)):
            for at in range(tiles // 2):
                start = (3 * side + third) * half + at * LANES
                keep[side * (tiles // 2) + at] = packed_ref[:, start : start + LANES].astype(F32)
    for at in range(tiles):
        k_s[at] = key_softmax(k_s[at], mask_ref[...])
    block = head_mask(2 * LANES, head_dim)

    def one_image(image, carry):
        for quad in range(tiles // 2):
            keys = image_rows(k_s, quad, image).astype(BF16)
            values = image_rows(v_s, quad, image).astype(BF16)
            query = image_rows(q_s, quad, image).astype(BF16)
            grads = image_rows(f_s, quad, image).astype(BF16)
            context = (mm_tn(keys, values) * block).astype(BF16)
            grad_context = (mm_tn(query, grads) * block).astype(BF16)
            put_image_rows(dq_s, quad, image, mm_nt(grads, context))
            put_image_rows(dk_s, quad, image, mm_nt(values, grad_context))
            put_image_rows(dv_s, quad, image, mm(keys, grad_context))
        return carry

    lax.fori_loop(0, IMGS, one_image, 0)
    for at in range(tiles):
        cols = lane(at)
        start = (3 * (at // (tiles // 2))) * half + (at % (tiles // 2)) * LANES
        place = lambda third: slice(start + third * half, start + third * half + LANES)
        mask = mask_ref[...]
        weights = k_s[at]
        share = weights * dk_s[at]
        total = jnp.sum(share.reshape(SLOT, IMGS, LANES), axis=0, keepdims=True)
        back = share.reshape(SLOT, IMGS, LANES) - weights.reshape(SLOT, IMGS, LANES) * total
        gp_s[:, place(1)] = back.reshape(ROWS, LANES).astype(BF16)
        grads = f_s[at]
        gp_s[:, place(0)] = (dq_s[at] + grads * rel_ref[:, cols].astype(F32)).astype(BF16)
        reach = tile_radius(at, head_dim)
        masked = v_s[at] * mask
        v_pad[3 : 3 + SIDE] = masked[IMGS:].reshape(SIDE, SIDE, IMGS, LANES)
        cgrad = grads * q_s[at] * mask
        c_pad[3 : 3 + SIDE] = cgrad[IMGS:].reshape(SIDE, SIDE, IMGS, LANES)
        c_s[:IMGS, :] = dv_s[at, :IMGS, :]

        def rel_step(row_at, carry):
            rows = grid_rows(row_at)
            out = conv_row(c_pad, crpe_ref, cols, row_at, 3, reach, 7, True)
            c_s[rows, :] = dv_s[at, rows, :] + out * mask_ref[rows, :]
            return carry

        lax.fori_loop(0, SIDE, rel_step, 0)
        conv_kernel_grad(c_pad, v_pad, gcrpe_ref, cols, 3, reach, 7, 3)
        gp_s[:, place(2)] = c_s[...].astype(BF16)
    unit, inv = normalize(conv_ref[...])
    gain = norm_ref[0:1, :]
    normed_t = (unit * gain + norm_ref[1:2, :]).astype(BF16).T
    grad_rows = None
    for side in range(2):
        part_in = gp_s[:, side * 3 * half : (side + 1) * 3 * half]
        w_s[side, :, : 3 * half] += mm(normed_t, part_in)
        part = mm_nt(part_in, w_ref[side, :, : 3 * half])
        grad_rows = part if grad_rows is None else grad_rows + part
    gnorm_ref[0:1, :] += jnp.sum(grad_rows * unit, axis=0, keepdims=True)
    gnorm_ref[1:2, :] += jnp.sum(grad_rows, axis=0, keepdims=True)
    up_ref[...] = gatt_ref[...] + norm_back(grad_rows, unit, inv, gain)
    for at in range(tiles):
        cols = lane(at)
        mask = mask_ref[...]
        masked = x_ref[:, cols] * mask
        x_pad[1 : 1 + SIDE] = masked[IMGS:].reshape(SIDE, SIDE, IMGS, LANES)
        gmasked = up_ref[:, cols] * mask
        g_pad[1 : 1 + SIDE] = gmasked[IMGS:].reshape(SIDE, SIDE, IMGS, LANES)

        def conv_step(row_at, carry):
            rows = grid_rows(row_at)
            out = conv_row(g_pad, cpe_ref, cols, row_at, 1, 1, 3, True)
            up_ref[rows, cols] += out * mask_ref[rows, :]
            return carry

        lax.fori_loop(0, SIDE, conv_step, 0)
        conv_kernel_grad(g_pad, x_pad, gcpe_ref, cols, 1, 1, 3, 1)
        if scratch:
            c_s[...] = up_ref[:, cols]

            def put(rows, values, cols=cols):
                out_ref[rows, cols] = values

            to_image_major(c_s, put)

    @pl.when(step == steps - 1)
    def _():
        gw_ref[...] = w_s[...].astype(BF16)


def schulz(fresh_ref, out_ref, width):
    def dot3(a, b, dims):
        a_hi = a.astype(BF16)
        b_hi = b.astype(BF16)
        a_lo = (a - a_hi.astype(F32)).astype(BF16)
        b_lo = (b - b_hi.astype(F32)).astype(BF16)
        one = lambda u, v: lax.dot_general(u, v, (dims, ((), ())), preferred_element_type=F32)
        return one(a_hi, b_hi) + (one(a_hi, b_lo) + one(a_lo, b_hi))

    first, second, third = SCHULZ_COEFFS
    parts = range(0, fresh_ref.shape[2], width)
    current = []
    for at in parts:
        value = fresh_ref[0, :, at : at + width].astype(F32)
        level = jnp.sum(jnp.sum(value * value, axis=0, keepdims=True), axis=1, keepdims=True)
        current.append(value / (jnp.sqrt(level) + 1e-07))
    for _ in range(5):
        for at, value in enumerate(current):
            gram = dot3(value, value, ((0,), (0,)))
            poly = second * gram + third * dot3(gram, gram, ((1,), (0,)))
            current[at] = first * value + dot3(value, poly, ((1,), (0,)))
    for at, value in zip(parts, current):
        out_ref[0, :, at : at + width] = value.astype(BF16)


def params_for(**more):
    return pltpu.CompilerParams(vmem_limit_bytes=VMEM_BYTES, **more)


def block_of(cols):
    return pl.BlockSpec((ROWS, cols), lambda g: (g, 0))


def whole(array):
    shape = array.shape
    return pl.BlockSpec(shape, lambda g: (0,) * len(shape), pipeline_mode=pl.Buffered(1))


def some_columns(weights):
    array, width, at = weights
    shape = array.shape[:2] + (width,)
    return pl.BlockSpec(shape, lambda g: (0, 0, at), pipeline_mode=pl.Buffered(1))


def whole_out(shape):
    return pl.BlockSpec(shape, lambda g: (0,) * len(shape))


def cost(us):
    return pl.CostEstimate(flops=int(us * 1e9), bytes_accessed=int(us * 1e5), transcendentals=0)


def run_attend_forward(x, mask, weights, norm, cpe, crpe, first):
    count, channels = x.shape
    tiles = channels // LANES
    flat = pltpu.VMEM((tiles, ROWS, LANES), F32)
    out = lambda cols, kind: jax.ShapeDtypeStruct((count, cols), kind)
    outs = [out(channels, F32), out(3 * channels, BF16)] + [out(channels, BF16)] * 2
    outs = [out(channels, F32)] * first + outs + [out(channels, F32)]
    return pl.pallas_call(
        functools.partial(attend_forward, first=first),
        grid=(count // ROWS,),
        in_specs=[block_of(channels), block_of(LANES)]
        + [some_columns(weights)]
        + [whole(a) for a in (norm, cpe, crpe)],
        out_specs=[block_of(array.shape[1]) for array in outs],
        out_shape=outs,
        scratch_shapes=[
            pltpu.VMEM((SIDE + 2, SIDE, IMGS, LANES), F32),
            pltpu.VMEM((SIDE + 6, SIDE, IMGS, LANES), F32),
            flat, flat, flat, flat,
            pltpu.VMEM((ROWS, LANES), F32),
        ],
        compiler_params=params_for(),
        cost_estimate=cost(50),
        name="attend_forward",
    )(x, mask, weights[0], norm, cpe, crpe)


def run_feed_forward(att, up_down, norm, last, chunk=256):
    count, channels = att.shape
    hidden = up_down[0].shape[0] * up_down[1] // 2
    turn = [pltpu.VMEM((ROWS, LANES), F32), pltpu.VMEM((ROWS, channels), F32)]
    return pl.pallas_call(
        functools.partial(feed_forward, chunk=chunk),
        grid=(count // ROWS,),
        in_specs=[block_of(channels), some_columns(up_down), whole(norm)],
        out_specs=[block_of(channels), block_of(hidden), block_of(hidden)],
        out_shape=[
            jax.ShapeDtypeStruct((count, channels), BF16 if last else F32),
            jax.ShapeDtypeStruct((count, hidden), BF16),
            jax.ShapeDtypeStruct((count, hidden), BF16),
        ],
        scratch_shapes=turn if last else [],
        compiler_params=params_for(),
        cost_estimate=cost(32),
        name="feed_forward",
    )(att, up_down[0], norm)


def run_feed_back(mask, upstream, att, active, slope, up_down, norm, first, chunk=256):
    count, channels = att.shape
    hidden = active.shape[1]
    turn = [pltpu.VMEM((ROWS, LANES), F32), pltpu.VMEM((ROWS, channels), F32)]
    shape = up_down[0].shape[:2] + (up_down[1],)
    return pl.pallas_call(
        functools.partial(feed_back, first=first, chunk=chunk),
        grid=(count // ROWS,),
        in_specs=[block_of(LANES)] * first
        + [block_of(channels), block_of(channels), block_of(hidden), block_of(hidden)]
        + [some_columns(up_down), whole(norm)],
        out_specs=[block_of(channels), whole_out(shape), whole_out((2, channels))],
        out_shape=[
            jax.ShapeDtypeStruct((count, channels), F32),
            jax.ShapeDtypeStruct(shape, BF16),
            jax.ShapeDtypeStruct((2, channels), F32),
        ],
        scratch_shapes=[pltpu.VMEM(shape, F32)] + turn * first,
        compiler_params=params_for(),
        cost_estimate=cost(41),
        name="feed_back",
    )(*(([mask] if first else []) + [upstream, att, active, slope, up_down[0], norm]))


def run_attend_back(gatt, x, conv, packed, rel, mixed, mask, weights, norm, cpe, crpe, last):
    count, channels = x.shape
    tiles = channels // LANES
    flat = pltpu.VMEM((tiles, ROWS, LANES), F32)
    three = pltpu.VMEM((SIDE + 2, SIDE, IMGS, LANES), F32)
    seven = pltpu.VMEM((SIDE + 6, SIDE, IMGS, LANES), F32)
    small = [(2, channels), (9, IMGS, channels), (49, IMGS, channels)]
    shape = weights[0].shape[:2] + (weights[1],)
    return pl.pallas_call(
        attend_back,
        grid=(count // ROWS,),
        in_specs=[block_of(channels)] * 3
        + [block_of(3 * channels), block_of(channels), block_of(channels), block_of(LANES)]
        + [some_columns(weights)]
        + [whole(a) for a in (norm, cpe, crpe)],
        out_specs=[block_of(channels), whole_out(shape)]
        + [whole_out(each) for each in small],
        out_shape=[
            jax.ShapeDtypeStruct((count, channels), F32),
            jax.ShapeDtypeStruct(shape, BF16),
        ]
        + [jax.ShapeDtypeStruct(each, F32) for each in small],
        scratch_shapes=[
            pltpu.VMEM(shape, F32),
            three, three, seven, seven,
            flat, flat, flat, flat, flat, flat, flat,
            pltpu.VMEM((ROWS, LANES), F32),
            pltpu.VMEM((ROWS, 3 * channels), BF16),
        ]
        + [pltpu.VMEM((ROWS, channels), F32)] * last,
        compiler_params=params_for(),
        cost_estimate=cost(92),
        name="attend_back",
    )(gatt, x, conv, packed, rel, mixed, mask, weights[0], norm, cpe, crpe)


def where_am_i():
    tok, blk = lax.axis_index("tok"), lax.axis_index("blk")
    core, x, z = lax.rem(tok, 2), lax.rem(tok // 2, 2), tok // 4
    return blk, z, x, core


def device_at(y, z, x, core):
    return (z * 4 + x * 2 + core, y)


def neighbours(y, z, x, core):
    fx, fy = 1 - core, core
    flip = lambda value, by: value + by - 2 * value * by
    first = (flip(y, fy), flip(x, fx))
    second = (flip(y, fx), flip(x, fy))
    cross = (1 - y, 1 - x)
    return first, second, cross


def greet(targets):
    barrier = pltpu.get_barrier_semaphore()
    for target in targets:
        pl.semaphore_signal(barrier, inc=1, device_id=target, device_id_type=pl.DeviceIdType.MESH)
    pl.semaphore_wait(barrier, len(targets))


def spread_kernel(shard_ref, out_ref, send_sem, recv_sem, own_sem):
    y, z, x, core = where_am_i()
    first, second, cross = neighbours(y, z, x, core)
    line = [lax.rem(z + d, 4) for d in range(4)]
    back = [lax.rem(z + 4 - d, 4) for d in range(4)]
    to_first = device_at(first[0], z, first[1], core)
    to_second = device_at(second[0], z, second[1], core)
    to_core = device_at(y, z, x, 1 - core)
    greet([to_first, to_second, to_core] + [device_at(y, line[d], x, core) for d in (1, 2, 3)])
    slot = lambda at, layer, side: at[0] * 16 + layer * 4 + at[1] * 2 + side
    own = pltpu.make_async_copy(shard_ref, out_ref.at[slot((y, x), z, core)], own_sem)
    own.start()
    copies = []

    def send(src, at, layer, side, target, number):
        copy = pltpu.make_async_remote_copy(
            src_ref=src, dst_ref=out_ref.at[slot(at, layer, side)],
            send_sem=send_sem.at[number], recv_sem=recv_sem.at[number],
            device_id=target, device_id_type=pl.DeviceIdType.MESH,
        )
        copy.start()
        copies.append(copy)

    def arrive(at, layer, side, number):
        here = out_ref.at[slot(at, layer, side)]
        pltpu.make_async_remote_copy(
            src_ref=here, dst_ref=here, send_sem=send_sem.at[number], recv_sem=recv_sem.at[number],
            device_id=to_core, device_id_type=pl.DeviceIdType.MESH,
        ).wait_recv()

    me = (y, x)
    for d in (1, 2, 3):
        send(shard_ref, me, z, core, device_at(y, line[d], x, core), d - 1)
    for d in range(4):
        layer = back[d]
        if d:
            arrive(me, layer, core, d - 1)
        src = out_ref.at[slot(me, layer, core)] if d else shard_ref
        send(src, me, layer, core, to_first, 3 + d)
        send(src, me, layer, core, to_second, 7 + d)
        send(src, me, layer, core, to_core, 15 + d)
    for d in range(4):
        arrive(first, back[d], core, 3 + d)
        src = out_ref.at[slot(first, back[d], core)]
        send(src, first, back[d], core, to_second, 11 + d)
        send(src, first, back[d], core, to_core, 19 + d)
    for d in range(4):
        arrive(second, back[d], core, 7 + d)
        send(out_ref.at[slot(second, back[d], core)], second, back[d], core, to_core, 23 + d)
    for d in range(4):
        arrive(cross, back[d], core, 11 + d)
        send(out_ref.at[slot(cross, back[d], core)], cross, back[d], core, to_core, 27 + d)
    for d in range(4):
        arrive(me, back[d], 1 - core, 15 + d)
        arrive(second, back[d], 1 - core, 19 + d)
        arrive(first, back[d], 1 - core, 23 + d)
        arrive(cross, back[d], 1 - core, 27 + d)
    own.wait()
    for copy in copies:
        copy.wait_send()


def spread(shard, collective_id):
    return pl.pallas_call(
        spread_kernel,
        in_specs=[pl.BlockSpec(memory_space=pl.ANY)],
        out_specs=pl.BlockSpec(memory_space=pl.ANY),
        out_shape=jax.ShapeDtypeStruct((32,) + shard.shape, shard.dtype),
        scratch_shapes=[
            pltpu.SemaphoreType.DMA((31,)), pltpu.SemaphoreType.DMA((31,)), pltpu.SemaphoreType.DMA,
        ],
        compiler_params=pltpu.CompilerParams(
            collective_id=collective_id, has_side_effects=True, vmem_limit_bytes=VMEM_BYTES
        ),
        name="spread",
    )(shard)


def collect_kernel(*refs, widths):
    parts = len(widths)
    grads, out_ref = refs[:parts], refs[parts]
    own_s, chip_s, second_s, first_s, line_s, send_sem, recv_sem, load_sem = refs[parts + 1 :]
    y, z, x, core = where_am_i()
    first, second, cross = neighbours(y, z, x, core)
    line = [lax.rem(z + d, 4) for d in range(4)]
    back = [lax.rem(z + 4 - d, 4) for d in range(4)]
    to_first = device_at(first[0], z, first[1], core)
    to_second = device_at(second[0], z, second[1], core)
    to_core = device_at(y, z, x, 1 - core)
    greet([to_first, to_second, to_core] + [device_at(y, line[d], x, core) for d in (1, 2, 3)])
    slot = lambda at, layer, side: at[0] * 16 + layer * 4 + at[1] * 2 + side
    loads = []
    start = 0
    for number, (grad, width) in enumerate(zip(grads, widths)):
        copy = pltpu.make_async_copy(
            grad, own_s.at[:, :, start : start + width], load_sem.at[number]
        )
        copy.start()
        loads.append(copy)
        start += width
    for copy in loads:
        copy.wait()
    copies = []

    def send(src, dst, target, number):
        copy = pltpu.make_async_remote_copy(
            src_ref=src, dst_ref=dst, send_sem=send_sem.at[number], recv_sem=recv_sem.at[number],
            device_id=target, device_id_type=pl.DeviceIdType.MESH,
        )
        copy.start()
        copies.append(copy)

    def arrive(ref, number):
        pltpu.make_async_remote_copy(
            src_ref=ref, dst_ref=ref, send_sem=send_sem.at[number], recv_sem=recv_sem.at[number],
            device_id=to_core, device_id_type=pl.DeviceIdType.MESH,
        ).wait_recv()

    def add(ref, *others):
        total = ref[...].astype(F32)
        for other in others:
            total = total + other[...].astype(F32)
        ref[...] = total.astype(BF16)

    me = (y, x)
    order = [(cross, 0), (second, 1), (first, 2), (me, 3)]
    theirs = {0: 0, 1: 2, 2: 1, 3: 3}
    for place, kind in order:
        for d in range(4):
            number = theirs[kind] * 4 + d
            send(own_s.at[slot(place, line[d], 1 - core)], chip_s.at[number], to_core, number)
    for place, kind, there in ((cross, 0, 0), (second, 1, 4)):
        for d in range(4):
            here = chip_s.at[kind * 4 + d]
            arrive(here, kind * 4 + d)
            add(here, own_s.at[slot(place, line[d], core)])
            send(here, second_s.at[there + d], to_second, 16 + there + d)
    for d in range(4):
        here = chip_s.at[8 + d]
        arrive(here, 8 + d)
        arrive(second_s.at[d], 16 + d)
        add(here, own_s.at[slot(first, line[d], core)], second_s.at[d])
        send(here, first_s.at[d], to_first, 24 + d)
    for d in (1, 2, 3, 0):
        here = chip_s.at[12 + d]
        arrive(here, 12 + d)
        arrive(second_s.at[4 + d], 20 + d)
        arrive(first_s.at[d], 24 + d)
        if d:
            add(here, own_s.at[slot(me, line[d], core)], second_s.at[4 + d], first_s.at[d])
            send(here, line_s.at[d - 1], device_at(y, line[d], x, core), 27 + d)
    for d in (1, 2, 3):
        arrive(line_s.at[d - 1], 27 + d)
    total = chip_s[12].astype(F32) + own_s[slot(me, z, core)].astype(F32)
    for ref in (second_s.at[4], first_s.at[0], line_s.at[0], line_s.at[1], line_s.at[2]):
        total = total + ref[...].astype(F32)
    out_ref[...] = total
    for copy in copies:
        copy.wait_send()


def collect(grads, collective_id):
    rows = grads[0].shape[1]
    widths = tuple(grad.shape[2] for grad in grads)
    block = lambda count: pltpu.VMEM((count, rows, sum(widths)), BF16)
    return pl.pallas_call(
        functools.partial(collect_kernel, widths=widths),
        in_specs=[pl.BlockSpec(memory_space=pl.ANY)] * len(grads),
        out_specs=pl.BlockSpec(memory_space=pltpu.VMEM),
        out_shape=jax.ShapeDtypeStruct((rows, sum(widths)), F32),
        scratch_shapes=[
            block(32), block(16), block(8), block(4), block(3),
            pltpu.SemaphoreType.DMA((31,)), pltpu.SemaphoreType.DMA((31,)),
            pltpu.SemaphoreType.DMA((len(widths),)),
        ],
        compiler_params=pltpu.CompilerParams(
            collective_id=collective_id, has_side_effects=True, vmem_limit_bytes=VMEM_BYTES
        ),
        name="collect",
    )(*grads)


def run_schulz(fresh, width):
    units, height, _ = fresh.shape
    spec = pl.BlockSpec((1, height, 2 * width), lambda g: (g, 0, 0))
    return pl.pallas_call(
        lambda *refs: schulz(*refs, width=width),
        grid=(units,),
        in_specs=[spec],
        out_specs=spec,
        out_shape=jax.ShapeDtypeStruct((units, height, 2 * width), BF16),
        compiler_params=params_for(),
        name="schulz",
    )(fresh)


def token_major(rows):
    count, channels = rows.shape
    split = rows.reshape(count // ROWS, IMGS, SLOT, channels)
    return split.transpose(0, 2, 1, 3).reshape(count, channels)


def image_major(rows):
    count, channels = rows.shape
    split = rows.reshape(count // ROWS, SLOT, IMGS, channels)
    return split.transpose(0, 2, 1, 3).reshape(count, channels)


def key_masks(grid_class):
    extent = 5 + 2 * grid_class
    across = (jnp.arange(SIDE, dtype=jnp.int32)[None, :] < extent[:, None]).astype(F32)
    cells = (across[:, :, None] * across[:, None, :]).reshape(-1, SIDE * SIDE)
    return jnp.concatenate([jnp.ones((cells.shape[0], 1), F32), cells], axis=1)


def split_heads(shard, heads_own, head_dim):
    lead = shard.shape[:-1]
    parts = shard.reshape(lead + (heads_own, 3, head_dim))
    return jnp.swapaxes(parts, -3, -2).reshape(lead + (3 * heads_own * head_dim,))


def join_heads(shard, heads_own, head_dim):
    lead = shard.shape[:-1]
    parts = shard.reshape(lead + (3, heads_own, head_dim))
    return jnp.swapaxes(parts, -3, -2).reshape(lead + (3 * heads_own * head_dim,))


def block_scale(height, breadth):
    return math.sqrt(max(1.0, height / breadth))


def normalized_step(param_vals, moment, grads_in, rate, axes):
    fresh = 0.5 * moment + grads_in
    level = jnp.sqrt(jnp.mean(fresh * fresh, axis=axes, keepdims=True))
    return (fresh, param_vals - rate * fresh / (level + 1e-06))


def on_device(
    tokens, cotangent, grid_class,
    qkv_weight, proj_weight, up_weight, down_weight, norm_params, cpe_weight, crpe_weight,
    qkv_moment, proj_moment, up_moment, down_moment, norm_moment, cpe_moment, crpe_moment,
):
    own_count, channels = tokens.shape
    blk_count = lax.axis_size("blk")
    tok_count = lax.axis_size("tok")
    blk_at = lax.axis_index("blk")
    layers = qkv_weight.shape[0]
    images_own = grid_class.shape[0] // blk_count
    head_dim = channels // HEADS
    heads_own = HEADS // blk_count
    groups_own = GROUPS // blk_count
    group_width = up_weight.shape[2] // groups_own
    own_rows = qkv_weight.shape[1]
    both = ("blk", "tok")

    attn_cols, feed_cols = 4 * heads_own * head_dim, 2 * up_weight.shape[2]
    shard = jnp.concatenate(
        [
            up_weight,
            jnp.swapaxes(down_weight, 1, 2),
            split_heads(qkv_weight, heads_own, head_dim),
            jnp.swapaxes(proj_weight, 1, 2),
        ],
        axis=2,
    ).astype(BF16)
    near = (tok_count, blk_count) == (16, 2)

    def gather(piece, kernel):
        if kernel:
            return spread(piece, 1).reshape(blk_count, channels, piece.shape[1])
        full = lax.all_gather(piece, both, axis=0, tiled=True)
        return full.reshape(blk_count, channels, piece.shape[1])

    def halves(full):
        full = full.reshape(blk_count, channels, 4, heads_own * head_dim).transpose(1, 2, 0, 3)
        full = full.reshape(channels, 4, 2, channels // 2).transpose(2, 0, 1, 3)
        return full.reshape(2, channels, 2 * channels)

    def shares(grads):
        if blk_count == 2:
            return grads
        full = grads.reshape(2, channels, 4, channels // 2).transpose(1, 2, 0, 3)
        full = full.reshape(channels, 4, blk_count, heads_own * head_dim).transpose(2, 0, 1, 3)
        return full.reshape(blk_count, channels, attn_cols)

    attn_all, feed_all = [], []
    for layer in range(layers):
        piece = shard[layer]
        if layer and near:
            piece, full = lax.optimization_barrier((piece, full))
            attn_all[0], feed_all[0] = (full, attn_cols, 2), (full, feed_cols, 0)
        full = gather(piece, near and layer == 0)
        if blk_count == 2:
            attn_all.append((full, attn_cols, 2))
            feed_all.append((full, feed_cols, 0))
        else:
            attn_all.append((halves(full[:, :, feed_cols:]), 2 * channels, 0))
            feed_all.append((full[:, :, :feed_cols], feed_cols, 0))

    own_class = lax.dynamic_slice_in_dim(grid_class, blk_at * images_own, images_own)
    keys = key_masks(own_class)
    mask = jnp.broadcast_to(token_major(keys.reshape(own_count, 1)), (own_count, LANES))
    taps = jnp.repeat(tap_mask(jnp.arange(HEADS, dtype=jnp.int32)), head_dim, axis=1)

    stream = tokens
    saved = []
    for layer in range(layers):
        crpe = crpe_weight[layer] * taps
        outs = run_attend_forward(
            stream, mask, attn_all[layer], norm_params[layer], cpe_weight[layer], crpe, layer == 0
        )
        if layer:
            outs = [stream] + list(outs)
        stream, active, slope = run_feed_forward(
            outs[-1], feed_all[layer], norm_params[layer], layer == layers - 1
        )
        saved.append(tuple(outs) + (active, slope, crpe))
    block_out = stream

    upstream = cotangent
    attn_sums, feed_sums = [None] * layers, [None] * layers
    small_rows = 4 + 9 + 49
    for layer in reversed(range(layers)):
        x, conv, packed, rel, mixed, att, active, slope, crpe = saved[layer]
        gatt, gfeed, gmid = run_feed_back(
            mask, upstream, att, active, slope, feed_all[layer], norm_params[layer],
            layer == layers - 1,
        )
        if near and layer == 0:
            early, gatt = lax.optimization_barrier((early, gatt))
        upstream, gattn, gfront, gcpe, gcrpe = run_attend_back(
            gatt, x, conv, packed, rel, mixed, mask, attn_all[layer],
            norm_params[layer], cpe_weight[layer], crpe, layer == 0,
        )
        if near and layer == layers - 1:
            early = lax.psum_scatter(
                gfeed.reshape(blk_count * channels, gfeed.shape[2]), both,
                scatter_dimension=0, tiled=True,
            )
        small = jnp.concatenate([gfront, gmid, gcpe.sum(1), gcrpe.sum(1) * taps], axis=0)
        small = jnp.pad(small, ((0, LANES - small_rows), (0, 0))).T.astype(BF16)
        small = jnp.broadcast_to(small, (blk_count, channels, LANES))
        gattn = shares(gattn)
        pieces = [g.reshape(blk_count * tok_count, own_rows, -1) for g in (gattn, small, gfeed)]
        if near:
            waiting = pieces[:2] if layer else waiting + pieces
        else:
            scatter = lambda g: lax.psum_scatter(
                g.reshape(blk_count * channels, g.shape[2]), both, scatter_dimension=0, tiled=True
            ).astype(F32)
            feed_sums[layer] = scatter(pieces[2])
            attn_sums[layer] = scatter(jnp.concatenate(pieces[:2], axis=2))
    if near:
        total = collect(waiting, 2)
        cut = attn_cols + LANES
        attn_sums = [total[:, cut : 2 * cut], total[:, :cut]]
        feed_sums = [total[:, 2 * cut :], early.astype(F32)]
    tokens_grad = upstream

    attn_sum = jnp.stack(attn_sums)
    feed_sum = jnp.stack(feed_sums)
    small_sum = attn_sum[:, :, -LANES:][:, :, :small_rows]
    attn_sum = attn_sum[:, :, :-LANES]
    attn_moment = jnp.concatenate(
        [split_heads(qkv_moment, heads_own, head_dim), jnp.swapaxes(proj_moment, 1, 2)], axis=2
    )
    feed_moment = jnp.concatenate([up_moment, jnp.swapaxes(down_moment, 1, 2)], axis=2)
    attn_fresh = 0.5 * attn_moment + attn_sum
    feed_fresh = 0.5 * feed_moment + feed_sum

    units = layers * 2 * groups_own
    per_dev = -(-units // tok_count)
    big = feed_fresh.reshape(layers, own_rows, 2 * groups_own, group_width)
    big = big.transpose(0, 2, 1, 3).reshape(units, own_rows, group_width)
    heads = attn_fresh.reshape(layers, own_rows, 4, heads_own, head_dim).transpose(0, 3, 1, 2, 4)
    heads_qkv = heads[:, :, :, :3].reshape(layers, heads_own, own_rows, 3 * head_dim)
    heads_proj = heads[:, :, :, 3]
    widen = lambda v: jnp.pad(v, ((0, 0), (0, 0), (0, 0), (0, group_width - v.shape[3])))
    little = jnp.concatenate([widen(heads_qkv), widen(heads_proj)], axis=1)
    little = little.reshape(units, own_rows, group_width)
    send = jnp.concatenate([big, little], axis=2).astype(BF16)
    send = jnp.pad(send, ((0, per_dev * tok_count - units), (0, 0), (0, 0)))
    send = send.reshape(tok_count, per_dev, own_rows, 2 * group_width)
    small_own = jnp.swapaxes(small_sum, 0, 1).reshape(own_rows, layers * small_rows)
    small_own = jnp.pad(small_own, ((0, 0), (0, LANES - layers * small_rows))).astype(BF16)
    small_own = jnp.broadcast_to(small_own, (tok_count, per_dev, own_rows, LANES))
    got = lax.all_to_all(jnp.concatenate([send, small_own], axis=3), "tok", 0, 0, tiled=True)
    got = got.transpose(1, 0, 2, 3).reshape(per_dev, channels, 2 * group_width + LANES)
    small_all = got[0, :, 2 * group_width :].astype(F32).T[: layers * small_rows]
    small_all = small_all.reshape(layers, small_rows, channels)
    ortho = run_schulz(got, group_width)
    ortho = ortho.reshape(per_dev, tok_count, own_rows, 2 * group_width).transpose(1, 0, 2, 3)
    ortho = lax.all_to_all(ortho, "tok", 0, 0, tiled=True)
    ortho = ortho.reshape(per_dev * tok_count, own_rows, 2 * group_width)[:units].astype(F32)
    big = ortho[:, :, :group_width].reshape(layers, 2, groups_own, own_rows, group_width)
    big = big.transpose(1, 0, 3, 2, 4).reshape(2, layers, own_rows, groups_own * group_width)
    little = ortho[:, :, group_width:].reshape(layers, 2, heads_own, own_rows, group_width)
    little_qkv = little[:, 0, :, :, : 3 * head_dim].transpose(0, 2, 1, 3)
    little_qkv = little_qkv.reshape(layers, own_rows, heads_own * 3 * head_dim)
    little_proj = little[:, 1, :, :, :head_dim].transpose(0, 1, 3, 2)
    little_proj = little_proj.reshape(layers, heads_own * head_dim, own_rows)

    qkv_fresh = join_heads(attn_fresh[:, :, : qkv_weight.shape[2]], heads_own, head_dim)
    proj_fresh = jnp.swapaxes(attn_fresh[:, :, qkv_weight.shape[2] :], 1, 2)
    up_fresh = feed_fresh[:, :, : up_weight.shape[2]]
    down_fresh = jnp.swapaxes(feed_fresh[:, :, up_weight.shape[2] :], 1, 2)
    scales = (
        block_scale(channels, 3 * head_dim),
        block_scale(head_dim, channels),
        block_scale(channels, group_width),
        block_scale(group_width, channels),
    )
    results = []
    for kind, (weight, fresh, turned) in enumerate(
        (
            (qkv_weight, qkv_fresh, little_qkv),
            (proj_weight, proj_fresh, little_proj),
            (up_weight, up_fresh, big[0]),
            (down_weight, down_fresh, jnp.swapaxes(big[1], 1, 2)),
        )
    ):
        new = weight - MUON_RATES[kind] * scales[kind] * turned
        results.extend([fresh, new, new.astype(BF16)])

    norm_fresh, norm_new = normalized_step(
        norm_params, norm_moment, small_all[:, :4], SMALL_RATES[0], (2,)
    )
    cpe_fresh, cpe_new = normalized_step(
        cpe_weight, cpe_moment, small_all[:, 4:13], SMALL_RATES[1], (1, 2)
    )
    head_shape = (layers, 49, HEADS, head_dim)
    crpe_fresh, crpe_new = normalized_step(
        crpe_weight.reshape(head_shape),
        crpe_moment.reshape(head_shape),
        small_all[:, 13:].reshape(head_shape),
        SMALL_RATES[2],
        (1, 3),
    )
    return (
        (block_out, tokens_grad)
        + tuple(results)
        + (norm_fresh, norm_new, cpe_fresh, cpe_new)
        + (crpe_fresh.reshape(crpe_weight.shape), crpe_new.reshape(crpe_weight.shape))
    )


def solution(mesh):
    rows = P(("tok", "blk"), None)
    down_cols = P(None, "tok", "blk")
    cross = P(None, "blk", "tok")
    mats = (down_cols, cross, down_cols, cross)
    in_specs = (rows, rows, P("tok")) + mats + (P(),) * 3 + mats + (P(),) * 3
    out_specs = (rows, rows) + tuple(spec for spec in mats for _ in range(3)) + (P(),) * 6
    return jax.shard_map(
        on_device, mesh=mesh, in_specs=in_specs, out_specs=out_specs, check_vma=False
    )
```

```python
import functools
import math

import jax
import jax.numpy as jnp
from jax import lax
from jax.experimental import pallas as pl
from jax.experimental.pallas import tpu as pltpu
from jax.sharding import PartitionSpec as P

HEADS = 8
GROUPS = 8
SLOT = 82
SIDE = 9
LANES = 128
IMGS = 8
ROWS = SLOT * IMGS
SCHULZ_COEFFS = (3.4445, -4.775, 2.0315)
MUON_RATES = (0.8, 0.8, 0.8, 0.4)
SMALL_RATES = (0.3, 0.3, 0.15)
VMEM_BYTES = 60 * 1024 * 1024
F32 = jnp.float32
BF16 = jnp.bfloat16


def mm(a, b):
    return jnp.dot(a, b, preferred_element_type=F32)


def mm_nt(a, b):
    return lax.dot_general(a, b, (((1,), (1,)), ((), ())), preferred_element_type=F32)


def mm_tn(a, b):
    return lax.dot_general(a, b, (((0,), (0,)), ((), ())), preferred_element_type=F32)


def tap_mask(head_ids):
    radius = jnp.where(head_ids < 2, 1, jnp.where(head_ids < 5, 2, 3))
    offsets = jnp.abs(jnp.arange(7, dtype=jnp.int32) - 3)
    within = (offsets[:, None] <= radius[None, :]).astype(F32)
    return (within[:, None, :] * within[None, :, :]).reshape(49, head_ids.shape[0])


def tile_radius(lane_at, head_dim):
    last = ((lane_at + 1) * LANES - 1) // head_dim
    return 1 if last < 2 else (2 if last < 5 else 3)


def normalize(values):
    center = values - jnp.mean(values, axis=-1, keepdims=True)
    spread = jnp.mean(center * center, axis=-1, keepdims=True)
    inv = lax.rsqrt(spread + 1e-06)
    return center * inv, inv


def norm_back(grad, unit, inv, gain):
    scaled = grad * gain
    first = jnp.mean(scaled, axis=-1, keepdims=True)
    second = jnp.mean(scaled * unit, axis=-1, keepdims=True)
    return inv * (scaled - first - unit * second)


def lane(at):
    return slice(at * LANES, (at + 1) * LANES)


def grid_rows(row_at):
    return slice((1 + SIDE * row_at) * IMGS, (1 + SIDE * (row_at + 1)) * IMGS)


def lane_pair(low, high):
    cells = lambda tile: tile[IMGS:].reshape(SIDE, SIDE, IMGS, LANES)
    return jnp.concatenate([cells(low), cells(high)], axis=2).astype(BF16)


def split_pair(line):
    line = line.astype(F32)
    turn = lambda part: part.reshape(SIDE * IMGS, LANES)
    return turn(line[:, :IMGS]), turn(line[:, IMGS:])


def conv_row(cells_ref, kernel_ref, pair, row_at, reach, width, flip):
    mid = width // 2
    total = [None] * SIDE
    for down in range(-reach, reach + 1):
        if not 0 <= row_at + down < SIDE:
            continue
        line = cells_ref[row_at + down]
        acc = [None] * SIDE
        for along in range(-reach, reach + 1):
            tap = (mid - down, mid - along) if flip else (mid + down, mid + along)
            weight = kernel_ref[pair, tap[0] * width + tap[1]]
            for col in range(SIDE):
                if 0 <= col + along < SIDE:
                    term = line[col + along] * weight
                    acc[col] = term if acc[col] is None else acc[col] + term
        total = [new if old is None else old + new for old, new in zip(total, acc)]
    return jnp.stack(total, axis=0)


def conv_kernel_grad(grad_ref, cells_ref, total_ref, pair, reach, width):
    mid = width // 2
    for down in range(-reach, reach + 1):
        rows = [at for at in range(SIDE) if 0 <= at + down < SIDE]
        whole_sum = [None] * (2 * reach + 1)
        for start in range(0, len(rows), 3):
            acc = [None] * (2 * reach + 1)
            for row_at in rows[start : start + 3]:
                grad_line = grad_ref[row_at]
                line = cells_ref[row_at + down]
                for along in range(-reach, reach + 1):
                    for col in range(SIDE):
                        if 0 <= col + along < SIDE:
                            term = grad_line[col] * line[col + along]
                            at = along + reach
                            acc[at] = term if acc[at] is None else acc[at] + term
            acc = [value.astype(F32) for value in acc]
            whole_sum = [new if old is None else old + new for old, new in zip(whole_sum, acc)]
        for along in range(-reach, reach + 1):
            tap = (mid + down) * width + mid + along
            value = whole_sum[along + reach]
            total_ref[tap, :, lane(2 * pair)] += value[:IMGS]
            total_ref[tap, :, lane(2 * pair + 1)] += value[IMGS:]


def pair_kernel(kernel):
    taps, channels = kernel.shape
    kernel = kernel.reshape(taps, channels // (2 * LANES), 2, 1, LANES)
    kernel = jnp.broadcast_to(kernel, (taps, channels // (2 * LANES), 2, IMGS, LANES))
    kernel = kernel.transpose(1, 0, 2, 3, 4).astype(BF16)
    return kernel.reshape(channels // (2 * LANES), taps, 2 * IMGS, LANES)


def key_softmax(key_tile, mask_tile):
    keys = key_tile.reshape(SLOT, IMGS, LANES)
    live = mask_tile.reshape(SLOT, IMGS, LANES)
    top = jnp.max(jnp.where(live > 0, keys, -1e30), axis=0, keepdims=True)
    raw = jnp.exp(jnp.where(live > 0, keys - top, -60.0)) * live
    return (raw / jnp.sum(raw, axis=0, keepdims=True)).reshape(ROWS, LANES)


def head_mask(size, head_dim):
    down = lax.broadcasted_iota(jnp.int32, (size, size), 0) // head_dim
    along = lax.broadcasted_iota(jnp.int32, (size, size), 1) // head_dim
    return jnp.where(down == along, F32(head_dim ** -0.5), F32(0.0))


def image_rows(ref, quad, image):
    rows = pl.ds(image, SLOT, stride=IMGS)
    return jnp.concatenate([ref[2 * quad, rows, :], ref[2 * quad + 1, rows, :]], axis=1)


def put_image_rows(ref, quad, image, values):
    rows = pl.ds(image, SLOT, stride=IMGS)
    ref[2 * quad, rows, :] = values[:, :LANES]
    ref[2 * quad + 1, rows, :] = values[:, LANES:]


def to_token_major(src_ref, put):
    for token in range(SLOT):
        put(slice(token * IMGS, (token + 1) * IMGS), src_ref[pl.ds(token, IMGS, stride=SLOT), :])


def to_image_major(src_ref, put):
    for image in range(IMGS):
        put(slice(image * SLOT, (image + 1) * SLOT), src_ref[pl.ds(image, SLOT, stride=IMGS), :])


def attend_forward(*refs, first):
    if first:
        tokens_ref, refs = refs[0], refs[1:]
        (mask_ref, w_ref, norm_ref, cpe_ref, crpe_ref, x_ref, conv_ref, packed_ref, rel_ref,
         mixed_ref, att_ref, x_cells, v_cells, q_s, k_s, v_s, f_s, c_s) = refs
    else:
        (x_ref, mask_ref, w_ref, norm_ref, cpe_ref, crpe_ref, conv_ref, packed_ref, rel_ref,
         mixed_ref, att_ref, x_cells, v_cells, q_s, k_s, v_s, f_s, c_s) = refs
    channels = x_ref.shape[1]
    tiles = channels // LANES
    head_dim = channels // HEADS
    half = channels // 2

    if first:
        for at in range(tiles):
            cols = lane(at)
            f_s[at] = tokens_ref[:, cols].astype(F32)

            def put(rows, values, cols=cols):
                x_ref[rows, cols] = values

            to_token_major(f_s.at[at], put)
    for pair in range(tiles // 2):
        both = (lane(2 * pair), lane(2 * pair + 1))
        mask = mask_ref[...]
        x_cells[...] = lane_pair(*[x_ref[:, cols] * mask for cols in both])
        for cols in both:
            conv_ref[:IMGS, cols] = x_ref[:IMGS, cols]
        for row_at in range(SIDE):
            rows = grid_rows(row_at)
            out = split_pair(conv_row(x_cells, cpe_ref, pair, row_at, 1, 3, False))
            for cols, value in zip(both, out):
                conv_ref[rows, cols] = x_ref[rows, cols] + value * mask_ref[rows, :]
    unit, _ = normalize(conv_ref[...])
    normed = (unit * norm_ref[0:1, :] + norm_ref[1:2, :]).astype(BF16)
    for side in range(2):
        for third, keep in enumerate((q_s, k_s, v_s)):
            cols = slice(third * half, (third + 1) * half)
            part = mm(normed, w_ref[side, :, cols]).astype(BF16)
            packed_ref[:, side * 3 * half + third * half : side * 3 * half + (third + 1) * half] = part
            part = part.astype(F32)
            for at in range(tiles // 2):
                keep[side * (tiles // 2) + at] = part[:, lane(at)]
    for at in range(tiles):
        k_s[at] = key_softmax(k_s[at], mask_ref[...])
    block = head_mask(2 * LANES, head_dim)

    def one_image(image, carry):
        for quad in range(tiles // 2):
            keys = image_rows(k_s, quad, image).astype(BF16)
            values = image_rows(v_s, quad, image).astype(BF16)
            query = image_rows(q_s, quad, image).astype(BF16)
            context = (mm_tn(keys, values) * block).astype(BF16)
            put_image_rows(f_s, quad, image, mm(query, context))
        return carry

    lax.fori_loop(0, IMGS, one_image, 0, unroll=True)
    c_s[:, :IMGS, :] = jnp.zeros((2, IMGS, LANES), F32)
    for pair in range(tiles // 2):
        mask = mask_ref[...]
        v_cells[...] = lane_pair(v_s[2 * pair] * mask, v_s[2 * pair + 1] * mask)
        reach = tile_radius(2 * pair + 1, head_dim)
        for row_at in range(SIDE):
            rows = grid_rows(row_at)
            out = split_pair(conv_row(v_cells, crpe_ref, pair, row_at, reach, 7, False))
            for half_at, value in enumerate(out):
                c_s[half_at, rows, :] = value * mask_ref[rows, :]
        for half_at in range(2):
            at = 2 * pair + half_at
            rel = c_s[half_at]
            rel_ref[:, lane(at)] = rel.astype(BF16)
            mixed_ref[:, lane(at)] = (f_s[at] + q_s[at] * rel).astype(BF16)
    out = conv_ref[...]
    for side in range(2):
        cols = slice(side * half, (side + 1) * half)
        out = out + mm_nt(mixed_ref[:, cols], w_ref[side, :, 3 * half :])
    att_ref[...] = out


def gelu_parts(hidden):
    number = lambda value: jnp.asarray(value, BF16)
    values = hidden.astype(BF16)
    t = pl.reciprocal(
        number(1.0) + number(0.3275911 * 0.7071067811865476) * jnp.abs(values), approx=True
    )
    bell = jnp.exp2(number(-0.5 * 1.4426950408889634) * (values * values))
    poly = number(0.5 * 1.061405429)
    for coef in (-1.453152027, 1.421413741, -0.284496736, 0.254829592):
        poly = poly * t + number(0.5 * coef)
    tail = poly * t * bell
    phi = jnp.where(values >= 0, number(1.0) - tail, tail)
    return values * phi, phi + (values * number(0.3989422804014327)) * bell


def feed_forward(att_ref, up_down_ref, norm_ref, out_ref, act_ref, slope_ref, *scratch, chunk):
    blks, _, both = up_down_ref.shape
    width = both // 2
    chunk = min(chunk, width)
    att = att_ref[...]
    unit, _ = normalize(att)
    normed = (unit * norm_ref[2:3, :] + norm_ref[3:4, :]).astype(BF16)
    total = att
    for blk in range(blks):
        for at in range(0, width, chunk):
            hidden = mm(normed, up_down_ref[blk, :, at : at + chunk])
            active, slope = gelu_parts(hidden)
            cols = slice(blk * width + at, blk * width + at + chunk)
            act_ref[:, cols] = active
            slope_ref[:, cols] = slope
            total = total + mm_nt(active, up_down_ref[blk, :, width + at : width + at + chunk])
    if not scratch:
        out_ref[...] = total
        return
    turn_s, whole_s = scratch
    for at in range(att.shape[1] // LANES):
        cols = lane(at)
        turn_s[...] = total[:, cols]

        def put(rows, values, cols=cols):
            whole_s[rows, cols] = values

        to_image_major(turn_s, put)
    out_ref[...] = whole_s[...].astype(BF16)


def feed_back(*refs, first, chunk):
    if first:
        mask_ref, refs = refs[0], refs[1:]
    (up_ref, att_ref, act_ref, slope_ref, up_down_ref, norm_ref,
     gatt_ref, gweight_ref, gnorm_ref, total_s) = refs[:10]
    step, steps = pl.program_id(0), pl.num_programs(0)
    blks, _, both = up_down_ref.shape
    width = both // 2
    chunk = min(chunk, width)

    @pl.when(step == 0)
    def _():
        total_s[...] = jnp.zeros_like(total_s)
        gnorm_ref[...] = jnp.zeros_like(gnorm_ref)

    if first:
        turn_s, whole_s = refs[10:]
        for at in range(up_ref.shape[1] // LANES):
            cols = lane(at)
            turn_s[...] = up_ref[:, cols]

            def put(rows, values, cols=cols):
                whole_s[rows, cols] = values * mask_ref[rows, :]

            to_token_major(turn_s, put)
        upstream = whole_s[...]
    else:
        upstream = up_ref[...]
    unit, inv = normalize(att_ref[...])
    gain = norm_ref[2:3, :]
    normed_t = (unit * gain + norm_ref[3:4, :]).astype(BF16).T
    down_in = upstream.astype(BF16)
    down_t = down_in.T
    grad_mid = None
    for blk in range(blks):
        for at in range(0, width, chunk):
            cols = slice(blk * width + at, blk * width + at + chunk)
            ups = slice(at, at + chunk)
            downs = slice(width + at, width + at + chunk)
            grad_active = mm(down_in, up_down_ref[blk, :, downs])
            grad_hidden = (grad_active * slope_ref[:, cols].astype(F32)).astype(BF16)
            total_s[blk, :, ups] += mm(normed_t, grad_hidden)
            total_s[blk, :, downs] += mm(down_t, act_ref[:, cols])
            part = mm_nt(grad_hidden, up_down_ref[blk, :, ups])
            grad_mid = part if grad_mid is None else grad_mid + part
    gatt_ref[...] = upstream + norm_back(grad_mid, unit, inv, gain)
    gnorm_ref[0:1, :] += jnp.sum(grad_mid * unit, axis=0, keepdims=True)
    gnorm_ref[1:2, :] += jnp.sum(grad_mid, axis=0, keepdims=True)

    @pl.when(step == steps - 1)
    def _():
        gweight_ref[...] = total_s[...].astype(BF16)


def attend_back(
    gatt_ref, x_ref, conv_ref, packed_ref, rel_ref, mixed_ref, mask_ref,
    w_ref, norm_ref, cpe_ref, crpe_ref,
    out_ref, gw_ref, gnorm_ref, gcpe_ref, gcrpe_ref,
    w_s, x_cells, g_cells, v_cells, c_cells, q_s, k_s, v_s, f_s, dq_s, dk_s, dv_s, c_s, gp_s,
    *scratch,
):
    channels = x_ref.shape[1]
    tiles = channels // LANES
    head_dim = channels // HEADS
    half = channels // 2
    step, steps = pl.program_id(0), pl.num_programs(0)
    up_ref = scratch[0] if scratch else out_ref

    @pl.when(step == 0)
    def _():
        for ref in (w_s, gnorm_ref, gcpe_ref, gcrpe_ref):
            ref[...] = jnp.zeros_like(ref)

    att_in = gatt_ref[...].astype(BF16)
    att_t = att_in.T
    for side in range(2):
        cols = slice(side * half, (side + 1) * half)
        w_s[side, :, 3 * half :] += mm(att_t, mixed_ref[:, cols])
        grad_mixed = mm(att_in, w_ref[side, :, 3 * half :])
        for at in range(tiles // 2):
            f_s[side * (tiles // 2) + at] = grad_mixed[:, lane(at)]
        for third, keep in enumerate((q_s, k_s, v_s)):
            for at in range(tiles // 2):
                start = (3 * side + third) * half + at * LANES
                keep[side * (tiles // 2) + at] = packed_ref[:, start : start + LANES].astype(F32)
    for at in range(tiles):
        k_s[at] = key_softmax(k_s[at], mask_ref[...])
    block = head_mask(2 * LANES, head_dim)

    def one_image(image, carry):
        for quad in range(tiles // 2):
            keys = image_rows(k_s, quad, image).astype(BF16)
            values = image_rows(v_s, quad, image).astype(BF16)
            query = image_rows(q_s, quad, image).astype(BF16)
            grads = image_rows(f_s, quad, image).astype(BF16)
            context = (mm_tn(keys, values) * block).astype(BF16)
            grad_context = (mm_tn(query, grads) * block).astype(BF16)
            put_image_rows(dq_s, quad, image, mm_nt(grads, context))
            put_image_rows(dk_s, quad, image, mm_nt(values, grad_context))
            put_image_rows(dv_s, quad, image, mm(keys, grad_context))
        return carry

    lax.fori_loop(0, IMGS, one_image, 0, unroll=True)
    for pair in range(tiles // 2):
        mask = mask_ref[...]
        place = lambda at, third: slice(
            (3 * pair + third) * half + at * LANES, (3 * pair + third) * half + (at + 1) * LANES
        )
        for half_at in range(2):
            at = 2 * pair + half_at
            weights = k_s[at]
            share = weights * dk_s[at]
            total = jnp.sum(share.reshape(SLOT, IMGS, LANES), axis=0, keepdims=True)
            back = share.reshape(SLOT, IMGS, LANES) - weights.reshape(SLOT, IMGS, LANES) * total
            gp_s[:, place(half_at, 1)] = back.reshape(ROWS, LANES).astype(BF16)
            rel = rel_ref[:, lane(at)].astype(F32)
            gp_s[:, place(half_at, 0)] = (dq_s[at] + f_s[at] * rel).astype(BF16)
        reach = tile_radius(2 * pair + 1, head_dim)
        v_cells[...] = lane_pair(v_s[2 * pair] * mask, v_s[2 * pair + 1] * mask)
        c_cells[...] = lane_pair(
            *[f_s[at] * q_s[at] * mask for at in (2 * pair, 2 * pair + 1)]
        )
        for row_at in range(SIDE):
            rows = grid_rows(row_at)
            out = split_pair(conv_row(c_cells, crpe_ref, pair, row_at, reach, 7, True))
            for half_at, value in enumerate(out):
                dv_s[2 * pair + half_at, rows, :] += value * mask_ref[rows, :]
        conv_kernel_grad(c_cells, v_cells, gcrpe_ref, pair, reach, 7)
        for half_at in range(2):
            gp_s[:, place(half_at, 2)] = dv_s[2 * pair + half_at].astype(BF16)
    unit, inv = normalize(conv_ref[...])
    gain = norm_ref[0:1, :]
    normed_t = (unit * gain + norm_ref[1:2, :]).astype(BF16).T
    grad_rows = None
    for side in range(2):
        part_in = gp_s[:, side * 3 * half : (side + 1) * 3 * half]
        w_s[side, :, : 3 * half] += mm(normed_t, part_in)
        part = mm_nt(part_in, w_ref[side, :, : 3 * half])
        grad_rows = part if grad_rows is None else grad_rows + part
    gnorm_ref[0:1, :] += jnp.sum(grad_rows * unit, axis=0, keepdims=True)
    gnorm_ref[1:2, :] += jnp.sum(grad_rows, axis=0, keepdims=True)
    up_ref[...] = gatt_ref[...] + norm_back(grad_rows, unit, inv, gain)
    for pair in range(tiles // 2):
        both = (lane(2 * pair), lane(2 * pair + 1))
        mask = mask_ref[...]
        x_cells[...] = lane_pair(*[x_ref[:, cols] * mask for cols in both])
        g_cells[...] = lane_pair(*[up_ref[:, cols] * mask for cols in both])
        for row_at in range(SIDE):
            rows = grid_rows(row_at)
            out = split_pair(conv_row(g_cells, cpe_ref, pair, row_at, 1, 3, True))
            for cols, value in zip(both, out):
                up_ref[rows, cols] += value * mask_ref[rows, :]
        conv_kernel_grad(g_cells, x_cells, gcpe_ref, pair, 1, 3)
    for at in range(tiles if scratch else 0):
        cols = lane(at)
        c_s[...] = up_ref[:, cols]

        def put(rows, values, cols=cols):
            out_ref[rows, cols] = values

        to_image_major(c_s, put)

    @pl.when(step == steps - 1)
    def _():
        gw_ref[...] = w_s[...].astype(BF16)


def schulz(fresh_ref, out_ref, width):
    def dot3(a, b, dims):
        a_hi = a.astype(BF16)
        b_hi = b.astype(BF16)
        a_lo = (a - a_hi.astype(F32)).astype(BF16)
        b_lo = (b - b_hi.astype(F32)).astype(BF16)
        one = lambda u, v: lax.dot_general(u, v, (dims, ((), ())), preferred_element_type=F32)
        return one(a_hi, b_hi) + (one(a_hi, b_lo) + one(a_lo, b_hi))

    first, second, third = SCHULZ_COEFFS
    parts = range(0, fresh_ref.shape[2], width)
    current = []
    for at in parts:
        value = fresh_ref[0, :, at : at + width].astype(F32)
        level = jnp.sum(jnp.sum(value * value, axis=0, keepdims=True), axis=1, keepdims=True)
        current.append(value / (jnp.sqrt(level) + 1e-07))
    for _ in range(5):
        for at, value in enumerate(current):
            gram = dot3(value, value, ((0,), (0,)))
            poly = second * gram + third * dot3(gram, gram, ((1,), (0,)))
            current[at] = first * value + dot3(value, poly, ((1,), (0,)))
    for at, value in zip(parts, current):
        out_ref[0, :, at : at + width] = value.astype(BF16)


def params_for(**more):
    return pltpu.CompilerParams(vmem_limit_bytes=VMEM_BYTES, **more)


def block_of(cols):
    return pl.BlockSpec((ROWS, cols), lambda g: (g, 0))


def whole(array):
    shape = array.shape
    return pl.BlockSpec(shape, lambda g: (0,) * len(shape), pipeline_mode=pl.Buffered(1))


def some_columns(weights):
    array, width, at = weights
    shape = array.shape[:2] + (width,)
    return pl.BlockSpec(shape, lambda g: (0, 0, at), pipeline_mode=pl.Buffered(1))


def whole_out(shape):
    return pl.BlockSpec(shape, lambda g: (0,) * len(shape))


def cost(us):
    return pl.CostEstimate(flops=int(us * 1e9), bytes_accessed=int(us * 1e5), transcendentals=0)


def run_attend_forward(x, mask, weights, norm, cpe, crpe, first):
    count, channels = x.shape
    tiles = channels // LANES
    flat = pltpu.VMEM((tiles, ROWS, LANES), F32)
    cells = pltpu.VMEM((SIDE, SIDE, 2 * IMGS, LANES), BF16)
    out = lambda cols, kind: jax.ShapeDtypeStruct((count, cols), kind)
    outs = [out(channels, F32), out(3 * channels, BF16)] + [out(channels, BF16)] * 2
    outs = [out(channels, F32)] * first + outs + [out(channels, F32)]
    return pl.pallas_call(
        functools.partial(attend_forward, first=first),
        grid=(count // ROWS,),
        in_specs=[block_of(channels), block_of(LANES)]
        + [some_columns(weights)]
        + [whole(a) for a in (norm, cpe, crpe)],
        out_specs=[block_of(array.shape[1]) for array in outs],
        out_shape=outs,
        scratch_shapes=[
            cells, cells, flat, flat, flat, flat,
            pltpu.VMEM((2, ROWS, LANES), F32),
        ],
        compiler_params=params_for(),
        cost_estimate=cost(50),
        name="attend_forward",
    )(x, mask, weights[0], norm, cpe, crpe)


def run_feed_forward(att, up_down, norm, last, chunk=512):
    count, channels = att.shape
    hidden = up_down[0].shape[0] * up_down[1] // 2
    turn = [pltpu.VMEM((ROWS, LANES), F32), pltpu.VMEM((ROWS, channels), F32)]
    return pl.pallas_call(
        functools.partial(feed_forward, chunk=chunk),
        grid=(count // ROWS,),
        in_specs=[block_of(channels), some_columns(up_down), whole(norm)],
        out_specs=[block_of(channels), block_of(hidden), block_of(hidden)],
        out_shape=[
            jax.ShapeDtypeStruct((count, channels), BF16 if last else F32),
            jax.ShapeDtypeStruct((count, hidden), BF16),
            jax.ShapeDtypeStruct((count, hidden), BF16),
        ],
        scratch_shapes=turn if last else [],
        compiler_params=params_for(),
        cost_estimate=cost(32),
        name="feed_forward",
    )(att, up_down[0], norm)


def run_feed_back(mask, upstream, att, active, slope, up_down, norm, first, chunk=512):
    count, channels = att.shape
    hidden = active.shape[1]
    turn = [pltpu.VMEM((ROWS, LANES), F32), pltpu.VMEM((ROWS, channels), F32)]
    shape = up_down[0].shape[:2] + (up_down[1],)
    return pl.pallas_call(
        functools.partial(feed_back, first=first, chunk=chunk),
        grid=(count // ROWS,),
        in_specs=[block_of(LANES)] * first
        + [block_of(channels), block_of(channels), block_of(hidden), block_of(hidden)]
        + [some_columns(up_down), whole(norm)],
        out_specs=[block_of(channels), whole_out(shape), whole_out((2, channels))],
        out_shape=[
            jax.ShapeDtypeStruct((count, channels), F32),
            jax.ShapeDtypeStruct(shape, BF16),
            jax.ShapeDtypeStruct((2, channels), F32),
        ],
        scratch_shapes=[pltpu.VMEM(shape, F32)] + turn * first,
        compiler_params=params_for(),
        cost_estimate=cost(41),
        name="feed_back",
    )(*(([mask] if first else []) + [upstream, att, active, slope, up_down[0], norm]))


def run_attend_back(gatt, x, conv, packed, rel, mixed, mask, weights, norm, cpe, crpe, last):
    count, channels = x.shape
    tiles = channels // LANES
    flat = pltpu.VMEM((tiles, ROWS, LANES), F32)
    cells = pltpu.VMEM((SIDE, SIDE, 2 * IMGS, LANES), BF16)
    small = [(2, channels), (9, IMGS, channels), (49, IMGS, channels)]
    shape = weights[0].shape[:2] + (weights[1],)
    return pl.pallas_call(
        attend_back,
        grid=(count // ROWS,),
        in_specs=[block_of(channels)] * 3
        + [block_of(3 * channels), block_of(channels), block_of(channels), block_of(LANES)]
        + [some_columns(weights)]
        + [whole(a) for a in (norm, cpe, crpe)],
        out_specs=[block_of(channels), whole_out(shape)]
        + [whole_out(each) for each in small],
        out_shape=[
            jax.ShapeDtypeStruct((count, channels), F32),
            jax.ShapeDtypeStruct(shape, BF16),
        ]
        + [jax.ShapeDtypeStruct(each, F32) for each in small],
        scratch_shapes=[
            pltpu.VMEM(shape, F32),
            cells, cells, cells, cells,
            flat, flat, flat, flat, flat, flat, flat,
            pltpu.VMEM((ROWS, LANES), F32),
            pltpu.VMEM((ROWS, 3 * channels), BF16),
        ]
        + [pltpu.VMEM((ROWS, channels), F32)] * last,
        compiler_params=params_for(),
        cost_estimate=cost(92),
        name="attend_back",
    )(gatt, x, conv, packed, rel, mixed, mask, weights[0], norm, cpe, crpe)


def where_am_i():
    tok, blk = lax.axis_index("tok"), lax.axis_index("blk")
    core, x, z = lax.rem(tok, 2), lax.rem(tok // 2, 2), tok // 4
    return blk, z, x, core


def device_at(y, z, x, core):
    return (z * 4 + x * 2 + core, y)


def neighbours(y, z, x, core):
    fx, fy = 1 - core, core
    flip = lambda value, by: value + by - 2 * value * by
    first = (flip(y, fy), flip(x, fx))
    second = (flip(y, fx), flip(x, fy))
    cross = (1 - y, 1 - x)
    return first, second, cross


def greet(targets):
    barrier = pltpu.get_barrier_semaphore()
    for target in targets:
        pl.semaphore_signal(barrier, inc=1, device_id=target, device_id_type=pl.DeviceIdType.MESH)
    pl.semaphore_wait(barrier, len(targets))


def spread_kernel(shard_ref, out_ref, send_sem, recv_sem, own_sem):
    y, z, x, core = where_am_i()
    first, second, cross = neighbours(y, z, x, core)
    line = [lax.rem(z + d, 4) for d in range(4)]
    back = [lax.rem(z + 4 - d, 4) for d in range(4)]
    to_first = device_at(first[0], z, first[1], core)
    to_second = device_at(second[0], z, second[1], core)
    to_core = device_at(y, z, x, 1 - core)
    greet([to_first, to_second, to_core] + [device_at(y, line[d], x, core) for d in (1, 2, 3)])
    slot = lambda at, layer, side: at[0] * 16 + layer * 4 + at[1] * 2 + side
    own = pltpu.make_async_copy(shard_ref, out_ref.at[slot((y, x), z, core)], own_sem)
    own.start()
    copies = []

    def send(src, at, layer, side, target, number):
        copy = pltpu.make_async_remote_copy(
            src_ref=src, dst_ref=out_ref.at[slot(at, layer, side)],
            send_sem=send_sem.at[number], recv_sem=recv_sem.at[number],
            device_id=target, device_id_type=pl.DeviceIdType.MESH,
        )
        copy.start()
        copies.append(copy)

    def arrive(at, layer, side, number):
        here = out_ref.at[slot(at, layer, side)]
        pltpu.make_async_remote_copy(
            src_ref=here, dst_ref=here, send_sem=send_sem.at[number], recv_sem=recv_sem.at[number],
            device_id=to_core, device_id_type=pl.DeviceIdType.MESH,
        ).wait_recv()

    me = (y, x)
    for d in (1, 2, 3):
        send(shard_ref, me, z, core, device_at(y, line[d], x, core), d - 1)
    for d in range(4):
        layer = back[d]
        if d:
            arrive(me, layer, core, d - 1)
        src = out_ref.at[slot(me, layer, core)] if d else shard_ref
        send(src, me, layer, core, to_first, 3 + d)
        send(src, me, layer, core, to_second, 7 + d)
        send(src, me, layer, core, to_core, 15 + d)
    for d in range(4):
        arrive(first, back[d], core, 3 + d)
        src = out_ref.at[slot(first, back[d], core)]
        send(src, first, back[d], core, to_second, 11 + d)
        send(src, first, back[d], core, to_core, 19 + d)
    for d in range(4):
        arrive(second, back[d], core, 7 + d)
        send(out_ref.at[slot(second, back[d], core)], second, back[d], core, to_core, 23 + d)
    for d in range(4):
        arrive(cross, back[d], core, 11 + d)
        send(out_ref.at[slot(cross, back[d], core)], cross, back[d], core, to_core, 27 + d)
    for d in range(4):
        arrive(me, back[d], 1 - core, 15 + d)
        arrive(second, back[d], 1 - core, 19 + d)
        arrive(first, back[d], 1 - core, 23 + d)
        arrive(cross, back[d], 1 - core, 27 + d)
    own.wait()
    for copy in copies:
        copy.wait_send()


def spread(shard, collective_id):
    return pl.pallas_call(
        spread_kernel,
        in_specs=[pl.BlockSpec(memory_space=pl.ANY)],
        out_specs=pl.BlockSpec(memory_space=pl.ANY),
        out_shape=jax.ShapeDtypeStruct((32,) + shard.shape, shard.dtype),
        scratch_shapes=[
            pltpu.SemaphoreType.DMA((31,)), pltpu.SemaphoreType.DMA((31,)), pltpu.SemaphoreType.DMA,
        ],
        compiler_params=pltpu.CompilerParams(
            collective_id=collective_id, has_side_effects=True, vmem_limit_bytes=VMEM_BYTES
        ),
        name="spread",
    )(shard)


def collect_kernel(*refs, widths):
    parts = len(widths)
    grads, out_ref = refs[:parts], refs[parts]
    own_s, chip_s, second_s, first_s, line_s, send_sem, recv_sem, load_sem = refs[parts + 1 :]
    y, z, x, core = where_am_i()
    first, second, cross = neighbours(y, z, x, core)
    line = [lax.rem(z + d, 4) for d in range(4)]
    back = [lax.rem(z + 4 - d, 4) for d in range(4)]
    to_first = device_at(first[0], z, first[1], core)
    to_second = device_at(second[0], z, second[1], core)
    to_core = device_at(y, z, x, 1 - core)
    greet([to_first, to_second, to_core] + [device_at(y, line[d], x, core) for d in (1, 2, 3)])
    slot = lambda at, layer, side: at[0] * 16 + layer * 4 + at[1] * 2 + side
    loads = []
    start = 0
    for number, (grad, width) in enumerate(zip(grads, widths)):
        copy = pltpu.make_async_copy(
            grad, own_s.at[:, :, start : start + width], load_sem.at[number]
        )
        copy.start()
        loads.append(copy)
        start += width
    for copy in loads:
        copy.wait()
    copies = []

    def send(src, dst, target, number):
        copy = pltpu.make_async_remote_copy(
            src_ref=src, dst_ref=dst, send_sem=send_sem.at[number], recv_sem=recv_sem.at[number],
            device_id=target, device_id_type=pl.DeviceIdType.MESH,
        )
        copy.start()
        copies.append(copy)

    def arrive(ref, number):
        pltpu.make_async_remote_copy(
            src_ref=ref, dst_ref=ref, send_sem=send_sem.at[number], recv_sem=recv_sem.at[number],
            device_id=to_core, device_id_type=pl.DeviceIdType.MESH,
        ).wait_recv()

    def add(ref, *others):
        total = ref[...].astype(F32)
        for other in others:
            total = total + other[...].astype(F32)
        ref[...] = total.astype(BF16)

    me = (y, x)
    places = (cross, first, second, me)
    theirs = (0, 2, 1, 3)
    turns = (2, 1, 3, 0)
    for d in turns:
        for kind in (0, 2, 1, 3):
            number = theirs[kind] * 4 + d
            send(own_s.at[slot(places[kind], line[d], 1 - core)], chip_s.at[number], to_core, number)

    def fold(kind, d):
        here = chip_s.at[kind * 4 + d]
        arrive(here, kind * 4 + d)
        own = own_s.at[slot(places[kind], line[d], core)]
        if kind in (0, 2):
            there = 0 if kind == 0 else 4
            add(here, own)
            send(here, second_s.at[there + d], to_second, 16 + there + d)
        elif kind == 1:
            arrive(second_s.at[d], 16 + d)
            add(here, own, second_s.at[d])
            send(here, first_s.at[d], to_first, 24 + d)
        else:
            arrive(second_s.at[4 + d], 20 + d)
            arrive(first_s.at[d], 24 + d)
            if d:
                add(here, own, second_s.at[4 + d], first_s.at[d])
                send(here, line_s.at[d - 1], device_at(y, line[d], x, core), 27 + d)

    stages = [(0, 2), (1,), (3,)]
    for turn in range(len(turns) + 2):
        for stage, kinds in enumerate(stages):
            if 0 <= turn - stage < len(turns):
                for kind in kinds:
                    fold(kind, turns[turn - stage])
    for d in (1, 2, 3):
        arrive(line_s.at[d - 1], 27 + d)
    total = chip_s[12].astype(F32) + own_s[slot(me, z, core)].astype(F32)
    for ref in (second_s.at[4], first_s.at[0], line_s.at[0], line_s.at[1], line_s.at[2]):
        total = total + ref[...].astype(F32)
    out_ref[...] = total
    for copy in copies:
        copy.wait_send()


def collect(grads, collective_id):
    rows = grads[0].shape[1]
    widths = tuple(grad.shape[2] for grad in grads)
    block = lambda count: pltpu.VMEM((count, rows, sum(widths)), BF16)
    return pl.pallas_call(
        functools.partial(collect_kernel, widths=widths),
        in_specs=[pl.BlockSpec(memory_space=pl.ANY)] * len(grads),
        out_specs=pl.BlockSpec(memory_space=pltpu.VMEM),
        out_shape=jax.ShapeDtypeStruct((rows, sum(widths)), F32),
        scratch_shapes=[
            block(32), block(16), block(8), block(4), block(3),
            pltpu.SemaphoreType.DMA((31,)), pltpu.SemaphoreType.DMA((31,)),
            pltpu.SemaphoreType.DMA((len(widths),)),
        ],
        compiler_params=pltpu.CompilerParams(
            collective_id=collective_id, has_side_effects=True, vmem_limit_bytes=VMEM_BYTES
        ),
        name="collect",
    )(*grads)


def run_schulz(fresh, width):
    units, height, _ = fresh.shape
    spec = pl.BlockSpec((1, height, 2 * width), lambda g: (g, 0, 0))
    return pl.pallas_call(
        lambda *refs: schulz(*refs, width=width),
        grid=(units,),
        in_specs=[spec],
        out_specs=spec,
        out_shape=jax.ShapeDtypeStruct((units, height, 2 * width), BF16),
        compiler_params=params_for(),
        name="schulz",
    )(fresh)


def token_major(rows):
    count, channels = rows.shape
    split = rows.reshape(count // ROWS, IMGS, SLOT, channels)
    return split.transpose(0, 2, 1, 3).reshape(count, channels)


def image_major(rows):
    count, channels = rows.shape
    split = rows.reshape(count // ROWS, SLOT, IMGS, channels)
    return split.transpose(0, 2, 1, 3).reshape(count, channels)


def key_masks(grid_class):
    extent = 5 + 2 * grid_class
    across = (jnp.arange(SIDE, dtype=jnp.int32)[None, :] < extent[:, None]).astype(F32)
    cells = (across[:, :, None] * across[:, None, :]).reshape(-1, SIDE * SIDE)
    return jnp.concatenate([jnp.ones((cells.shape[0], 1), F32), cells], axis=1)


def split_heads(shard, heads_own, head_dim):
    lead = shard.shape[:-1]
    parts = shard.reshape(lead + (heads_own, 3, head_dim))
    return jnp.swapaxes(parts, -3, -2).reshape(lead + (3 * heads_own * head_dim,))


def join_heads(shard, heads_own, head_dim):
    lead = shard.shape[:-1]
    parts = shard.reshape(lead + (3, heads_own, head_dim))
    return jnp.swapaxes(parts, -3, -2).reshape(lead + (3 * heads_own * head_dim,))


def block_scale(height, breadth):
    return math.sqrt(max(1.0, height / breadth))


def normalized_step(param_vals, moment, grads_in, rate, axes):
    fresh = 0.5 * moment + grads_in
    level = jnp.sqrt(jnp.mean(fresh * fresh, axis=axes, keepdims=True))
    return (fresh, param_vals - rate * fresh / (level + 1e-06))


def on_device(
    tokens, cotangent, grid_class,
    qkv_weight, proj_weight, up_weight, down_weight, norm_params, cpe_weight, crpe_weight,
    qkv_moment, proj_moment, up_moment, down_moment, norm_moment, cpe_moment, crpe_moment,
):
    own_count, channels = tokens.shape
    blk_count = lax.axis_size("blk")
    tok_count = lax.axis_size("tok")
    blk_at = lax.axis_index("blk")
    layers = qkv_weight.shape[0]
    images_own = grid_class.shape[0] // blk_count
    head_dim = channels // HEADS
    heads_own = HEADS // blk_count
    groups_own = GROUPS // blk_count
    group_width = up_weight.shape[2] // groups_own
    own_rows = qkv_weight.shape[1]
    both = ("blk", "tok")

    attn_cols, feed_cols = 4 * heads_own * head_dim, 2 * up_weight.shape[2]
    shard = jnp.concatenate(
        [
            up_weight,
            jnp.swapaxes(down_weight, 1, 2),
            split_heads(qkv_weight, heads_own, head_dim),
            jnp.swapaxes(proj_weight, 1, 2),
        ],
        axis=2,
    ).astype(BF16)
    near = (tok_count, blk_count) == (16, 2)

    def gather(piece, kernel):
        if kernel:
            return spread(piece, 1).reshape(blk_count, channels, piece.shape[1])
        full = lax.all_gather(piece, both, axis=0, tiled=True)
        return full.reshape(blk_count, channels, piece.shape[1])

    def halves(full):
        full = full.reshape(blk_count, channels, 4, heads_own * head_dim).transpose(1, 2, 0, 3)
        full = full.reshape(channels, 4, 2, channels // 2).transpose(2, 0, 1, 3)
        return full.reshape(2, channels, 2 * channels)

    def shares(grads):
        if blk_count == 2:
            return grads
        full = grads.reshape(2, channels, 4, channels // 2).transpose(1, 2, 0, 3)
        full = full.reshape(channels, 4, blk_count, heads_own * head_dim).transpose(2, 0, 1, 3)
        return full.reshape(blk_count, channels, attn_cols)

    attn_all, feed_all = [], []
    for layer in range(layers):
        piece = shard[layer]
        if layer and near:
            piece, full = lax.optimization_barrier((piece, full))
            attn_all[0], feed_all[0] = (full, attn_cols, 2), (full, feed_cols, 0)
        full = gather(piece, near and layer == 0)
        if blk_count == 2:
            attn_all.append((full, attn_cols, 2))
            feed_all.append((full, feed_cols, 0))
        else:
            attn_all.append((halves(full[:, :, feed_cols:]), 2 * channels, 0))
            feed_all.append((full[:, :, :feed_cols], feed_cols, 0))

    own_class = lax.dynamic_slice_in_dim(grid_class, blk_at * images_own, images_own)
    keys = key_masks(own_class)
    mask = jnp.broadcast_to(token_major(keys.reshape(own_count, 1)), (own_count, LANES))
    taps = jnp.repeat(tap_mask(jnp.arange(HEADS, dtype=jnp.int32)), head_dim, axis=1)

    stream = tokens
    saved = []
    for layer in range(layers):
        cpe, crpe = pair_kernel(cpe_weight[layer]), pair_kernel(crpe_weight[layer] * taps)
        outs = run_attend_forward(
            stream, mask, attn_all[layer], norm_params[layer], cpe, crpe, layer == 0
        )
        if layer:
            outs = [stream] + list(outs)
        stream, active, slope = run_feed_forward(
            outs[-1], feed_all[layer], norm_params[layer], layer == layers - 1
        )
        saved.append(tuple(outs) + (active, slope, cpe, crpe))
    block_out = stream

    upstream = cotangent
    attn_sums, feed_sums = [None] * layers, [None] * layers
    small_rows = 4 + 9 + 49
    for layer in reversed(range(layers)):
        x, conv, packed, rel, mixed, att, active, slope, cpe, crpe = saved[layer]
        gatt, gfeed, gmid = run_feed_back(
            mask, upstream, att, active, slope, feed_all[layer], norm_params[layer],
            layer == layers - 1,
        )
        upstream, gattn, gfront, gcpe, gcrpe = run_attend_back(
            gatt, x, conv, packed, rel, mixed, mask, attn_all[layer],
            norm_params[layer], cpe, crpe, layer == 0,
        )
        if near and layer == layers - 1:
            early = lax.psum_scatter(
                gfeed.reshape(blk_count * channels, gfeed.shape[2]), both,
                scatter_dimension=0, tiled=True,
            )
        small = jnp.concatenate([gfront, gmid, gcpe.sum(1), gcrpe.sum(1) * taps], axis=0)
        small = jnp.pad(small, ((0, LANES - small_rows), (0, 0))).T.astype(BF16)
        small = jnp.broadcast_to(small, (blk_count, channels, LANES))
        gattn = shares(gattn)
        pieces = [g.reshape(blk_count * tok_count, own_rows, -1) for g in (gattn, small, gfeed)]
        if near:
            waiting = pieces[:2] if layer else waiting + pieces
        else:
            scatter = lambda g: lax.psum_scatter(
                g.reshape(blk_count * channels, g.shape[2]), both, scatter_dimension=0, tiled=True
            ).astype(F32)
            feed_sums[layer] = scatter(pieces[2])
            attn_sums[layer] = scatter(jnp.concatenate(pieces[:2], axis=2))
    if near:
        early, waiting = lax.optimization_barrier((early, waiting))
        total = collect(waiting, 2)
        cut = attn_cols + LANES
        attn_sums = [total[:, cut : 2 * cut], total[:, :cut]]
        feed_sums = [total[:, 2 * cut :], early.astype(F32)]
    tokens_grad = upstream

    attn_sum = jnp.stack(attn_sums)
    feed_sum = jnp.stack(feed_sums)
    small_sum = attn_sum[:, :, -LANES:][:, :, :small_rows]
    attn_sum = attn_sum[:, :, :-LANES]
    attn_moment = jnp.concatenate(
        [split_heads(qkv_moment, heads_own, head_dim), jnp.swapaxes(proj_moment, 1, 2)], axis=2
    )
    feed_moment = jnp.concatenate([up_moment, jnp.swapaxes(down_moment, 1, 2)], axis=2)
    attn_fresh = 0.5 * attn_moment + attn_sum
    feed_fresh = 0.5 * feed_moment + feed_sum

    units = layers * 2 * groups_own
    per_dev = -(-units // tok_count)
    big = feed_fresh.reshape(layers, own_rows, 2 * groups_own, group_width)
    big = big.transpose(0, 2, 1, 3).reshape(units, own_rows, group_width)
    heads = attn_fresh.reshape(layers, own_rows, 4, heads_own, head_dim).transpose(0, 3, 1, 2, 4)
    heads_qkv = heads[:, :, :, :3].reshape(layers, heads_own, own_rows, 3 * head_dim)
    heads_proj = heads[:, :, :, 3]
    widen = lambda v: jnp.pad(v, ((0, 0), (0, 0), (0, 0), (0, group_width - v.shape[3])))
    little = jnp.concatenate([widen(heads_qkv), widen(heads_proj)], axis=1)
    little = little.reshape(units, own_rows, group_width)
    send = jnp.concatenate([big, little], axis=2).astype(BF16)
    send = jnp.pad(send, ((0, per_dev * tok_count - units), (0, 0), (0, 0)))
    send = send.reshape(tok_count, per_dev, own_rows, 2 * group_width)
    small_own = jnp.swapaxes(small_sum, 0, 1).reshape(own_rows, layers * small_rows)
    small_own = jnp.pad(small_own, ((0, 0), (0, LANES - layers * small_rows))).astype(BF16)
    small_own = jnp.broadcast_to(small_own, (tok_count, per_dev, own_rows, LANES))
    got = lax.all_to_all(jnp.concatenate([send, small_own], axis=3), "tok", 0, 0, tiled=True)
    got = got.transpose(1, 0, 2, 3).reshape(per_dev, channels, 2 * group_width + LANES)
    small_all = got[0, :, 2 * group_width :].astype(F32).T[: layers * small_rows]
    small_all = small_all.reshape(layers, small_rows, channels)
    ortho = run_schulz(got, group_width)
    ortho = ortho.reshape(per_dev, tok_count, own_rows, 2 * group_width).transpose(1, 0, 2, 3)
    ortho = lax.all_to_all(ortho, "tok", 0, 0, tiled=True)
    ortho = ortho.reshape(per_dev * tok_count, own_rows, 2 * group_width)[:units].astype(F32)
    big = ortho[:, :, :group_width].reshape(layers, 2, groups_own, own_rows, group_width)
    big = big.transpose(1, 0, 3, 2, 4).reshape(2, layers, own_rows, groups_own * group_width)
    little = ortho[:, :, group_width:].reshape(layers, 2, heads_own, own_rows, group_width)
    little_qkv = little[:, 0, :, :, : 3 * head_dim].transpose(0, 2, 1, 3)
    little_qkv = little_qkv.reshape(layers, own_rows, heads_own * 3 * head_dim)
    little_proj = little[:, 1, :, :, :head_dim].transpose(0, 1, 3, 2)
    little_proj = little_proj.reshape(layers, heads_own * head_dim, own_rows)

    qkv_fresh = join_heads(attn_fresh[:, :, : qkv_weight.shape[2]], heads_own, head_dim)
    proj_fresh = jnp.swapaxes(attn_fresh[:, :, qkv_weight.shape[2] :], 1, 2)
    up_fresh = feed_fresh[:, :, : up_weight.shape[2]]
    down_fresh = jnp.swapaxes(feed_fresh[:, :, up_weight.shape[2] :], 1, 2)
    scales = (
        block_scale(channels, 3 * head_dim),
        block_scale(head_dim, channels),
        block_scale(channels, group_width),
        block_scale(group_width, channels),
    )
    results = []
    for kind, (weight, fresh, turned) in enumerate(
        (
            (qkv_weight, qkv_fresh, little_qkv),
            (proj_weight, proj_fresh, little_proj),
            (up_weight, up_fresh, big[0]),
            (down_weight, down_fresh, jnp.swapaxes(big[1], 1, 2)),
        )
    ):
        new = weight - MUON_RATES[kind] * scales[kind] * turned
        results.extend([fresh, new, new.astype(BF16)])

    norm_fresh, norm_new = normalized_step(
        norm_params, norm_moment, small_all[:, :4], SMALL_RATES[0], (2,)
    )
    cpe_fresh, cpe_new = normalized_step(
        cpe_weight, cpe_moment, small_all[:, 4:13], SMALL_RATES[1], (1, 2)
    )
    head_shape = (layers, 49, HEADS, head_dim)
    crpe_fresh, crpe_new = normalized_step(
        crpe_weight.reshape(head_shape),
        crpe_moment.reshape(head_shape),
        small_all[:, 13:].reshape(head_shape),
        SMALL_RATES[2],
        (1, 3),
    )
    return (
        (block_out, tokens_grad)
        + tuple(results)
        + (norm_fresh, norm_new, cpe_fresh, cpe_new)
        + (crpe_fresh.reshape(crpe_weight.shape), crpe_new.reshape(crpe_weight.shape))
    )


def solution(mesh):
    rows = P(("tok", "blk"), None)
    down_cols = P(None, "tok", "blk")
    cross = P(None, "blk", "tok")
    mats = (down_cols, cross, down_cols, cross)
    in_specs = (rows, rows, P("tok")) + mats + (P(),) * 3 + mats + (P(),) * 3
    out_specs = (rows, rows) + tuple(spec for spec in mats for _ in range(3)) + (P(),) * 6
    return jax.shard_map(
        on_device, mesh=mesh, in_specs=in_specs, out_specs=out_specs, check_vma=False
    )
```

```python
import functools
import math

import jax
import jax.numpy as jnp
from jax import lax
from jax.experimental import pallas as pl
from jax.experimental.pallas import tpu as pltpu
from jax.sharding import PartitionSpec as P

HEADS = 8
GROUPS = 8
SLOT = 82
SIDE = 9
LANES = 128
IMGS = 8
ROWS = SLOT * IMGS
SCHULZ_COEFFS = (3.4445, -4.775, 2.0315)
MUON_RATES = (0.8, 0.8, 0.8, 0.4)
SMALL_RATES = (0.3, 0.3, 0.15)
SMALL_ROWS = 4 + 9 + 49
HEAD_DIM = 64
VMEM_BYTES = 60 * 1024 * 1024
F32 = jnp.float32
BF16 = jnp.bfloat16


def mm(a, b):
    return jnp.dot(a, b, preferred_element_type=F32)


def mm_nt(a, b):
    return lax.dot_general(a, b, (((1,), (1,)), ((), ())), preferred_element_type=F32)


def mm_tn(a, b):
    return lax.dot_general(a, b, (((0,), (0,)), ((), ())), preferred_element_type=F32)


def tap_mask(head_ids):
    radius = jnp.where(head_ids < 2, 1, jnp.where(head_ids < 5, 2, 3))
    offsets = jnp.abs(jnp.arange(7, dtype=jnp.int32) - 3)
    within = (offsets[:, None] <= radius[None, :]).astype(F32)
    return (within[:, None, :] * within[None, :, :]).reshape(49, head_ids.shape[0])


def tile_radius(lane_at, head_dim):
    last = ((lane_at + 1) * LANES - 1) // head_dim
    return 1 if last < 2 else (2 if last < 5 else 3)


def normalize(values):
    center = values - jnp.mean(values, axis=-1, keepdims=True)
    spread = jnp.mean(center * center, axis=-1, keepdims=True)
    inv = lax.rsqrt(spread + 1e-06)
    return center * inv, inv


def norm_back(grad, unit, inv, gain):
    scaled = grad * gain
    first = jnp.mean(scaled, axis=-1, keepdims=True)
    second = jnp.mean(scaled * unit, axis=-1, keepdims=True)
    return inv * (scaled - first - unit * second)


def lane(at):
    return slice(at * LANES, (at + 1) * LANES)


def grid_rows(row_at):
    return slice((1 + SIDE * row_at) * IMGS, (1 + SIDE * (row_at + 1)) * IMGS)


def lane_pair(low, high):
    cells = lambda tile: tile[IMGS:].reshape(SIDE, SIDE, IMGS, LANES)
    return jnp.concatenate([cells(low), cells(high)], axis=2).astype(BF16)


def split_pair(line):
    line = line.astype(F32)
    turn = lambda part: part.reshape(SIDE * IMGS, LANES)
    return turn(line[:, :IMGS]), turn(line[:, IMGS:])


def conv_row(cells_ref, kernel_ref, pair, row_at, reach, width, flip):
    mid = width // 2
    total = [None] * SIDE
    for down in range(-reach, reach + 1):
        if not 0 <= row_at + down < SIDE:
            continue
        line = cells_ref[row_at + down]
        acc = [None] * SIDE
        for along in range(-reach, reach + 1):
            tap = (mid - down, mid - along) if flip else (mid + down, mid + along)
            weight = kernel_ref[pair, tap[0] * width + tap[1]]
            for col in range(SIDE):
                if 0 <= col + along < SIDE:
                    term = line[col + along] * weight
                    acc[col] = term if acc[col] is None else acc[col] + term
        total = [new if old is None else old + new for old, new in zip(total, acc)]
    return jnp.stack(total, axis=0)


def conv_kernel_grad(grad_ref, cells_ref, total_ref, pair, reach, width):
    mid = width // 2
    for down in range(-reach, reach + 1):
        rows = [at for at in range(SIDE) if 0 <= at + down < SIDE]
        whole_sum = [None] * (2 * reach + 1)
        for start in range(0, len(rows), 3):
            acc = [None] * (2 * reach + 1)
            for row_at in rows[start : start + 3]:
                grad_line = grad_ref[row_at]
                line = cells_ref[row_at + down]
                for along in range(-reach, reach + 1):
                    for col in range(SIDE):
                        if 0 <= col + along < SIDE:
                            term = grad_line[col] * line[col + along]
                            at = along + reach
                            acc[at] = term if acc[at] is None else acc[at] + term
            acc = [value.astype(F32) for value in acc]
            whole_sum = [new if old is None else old + new for old, new in zip(whole_sum, acc)]
        for along in range(-reach, reach + 1):
            tap = (mid + down) * width + mid + along
            value = whole_sum[along + reach]
            total_ref[tap, :, lane(2 * pair)] += value[:IMGS]
            total_ref[tap, :, lane(2 * pair + 1)] += value[IMGS:]


def fill_taps(kernel_ref, table_ref):
    for pair in range(table_ref.shape[0]):
        for tap in range(table_ref.shape[1]):
            sides = [kernel_ref[tap : tap + 1, lane(2 * pair + side)] for side in range(2)]
            sides = [jnp.broadcast_to(side, (IMGS, LANES)) for side in sides]
            table_ref[pair, tap] = jnp.concatenate(sides, axis=0).astype(BF16)


def key_softmax(key_tile, mask_tile):
    keys = key_tile.reshape(SLOT, IMGS, LANES)
    live = mask_tile.reshape(SLOT, IMGS, LANES)
    top = jnp.max(jnp.where(live > 0, keys, -1e30), axis=0, keepdims=True)
    raw = jnp.exp(jnp.where(live > 0, keys - top, -60.0)) * live
    return (raw / jnp.sum(raw, axis=0, keepdims=True)).reshape(ROWS, LANES)


def head_mask(size, head_dim):
    down = lax.broadcasted_iota(jnp.int32, (size, size), 0) // head_dim
    along = lax.broadcasted_iota(jnp.int32, (size, size), 1) // head_dim
    return jnp.where(down == along, F32(head_dim ** -0.5), F32(0.0))


def image_rows(ref, quad, image):
    rows = pl.ds(image, SLOT, stride=IMGS)
    return jnp.concatenate([ref[2 * quad, rows, :], ref[2 * quad + 1, rows, :]], axis=1)


def put_image_rows(ref, quad, image, values):
    rows = pl.ds(image, SLOT, stride=IMGS)
    ref[2 * quad, rows, :] = values[:, :LANES]
    ref[2 * quad + 1, rows, :] = values[:, LANES:]


def to_token_major(src_ref, put):
    for token in range(SLOT):
        put(slice(token * IMGS, (token + 1) * IMGS), src_ref[pl.ds(token, IMGS, stride=SLOT), :])


def to_image_major(src_ref, put):
    for image in range(IMGS):
        put(slice(image * SLOT, (image + 1) * SLOT), src_ref[pl.ds(image, SLOT, stride=IMGS), :])


def attend_forward(*refs, first):
    if first:
        tokens_ref, refs = refs[0], refs[1:]
        (mask_ref, w_ref, norm_ref, cpe_in, crpe_in, x_ref, conv_ref, packed_ref, rel_ref,
         mixed_ref, att_ref, x_cells, v_cells, cpe_ref, crpe_ref, q_s, k_s, v_s, f_s, c_s) = refs
    else:
        (x_ref, mask_ref, w_ref, norm_ref, cpe_in, crpe_in, conv_ref, packed_ref, rel_ref,
         mixed_ref, att_ref, x_cells, v_cells, cpe_ref, crpe_ref, q_s, k_s, v_s, f_s, c_s) = refs
    channels = x_ref.shape[1]
    tiles = channels // LANES
    head_dim = channels // HEADS
    half = channels // 2

    @pl.when(pl.program_id(0) == 0)
    def _():
        fill_taps(cpe_in, cpe_ref)
        fill_taps(crpe_in, crpe_ref)

    if first:
        for at in range(tiles):
            cols = lane(at)
            f_s[at] = tokens_ref[:, cols].astype(F32)

            def put(rows, values, cols=cols):
                x_ref[rows, cols] = values

            to_token_major(f_s.at[at], put)
    for pair in range(tiles // 2):
        both = (lane(2 * pair), lane(2 * pair + 1))
        mask = mask_ref[...]
        x_cells[...] = lane_pair(*[x_ref[:, cols] * mask for cols in both])
        for cols in both:
            conv_ref[:IMGS, cols] = x_ref[:IMGS, cols]
        for row_at in range(SIDE):
            rows = grid_rows(row_at)
            out = split_pair(conv_row(x_cells, cpe_ref, pair, row_at, 1, 3, False))
            for cols, value in zip(both, out):
                conv_ref[rows, cols] = x_ref[rows, cols] + value * mask_ref[rows, :]
    unit, _ = normalize(conv_ref[...])
    normed = (unit * norm_ref[0:1, :] + norm_ref[1:2, :]).astype(BF16)
    for side in range(2):
        for third, keep in enumerate((q_s, k_s, v_s)):
            cols = slice(third * half, (third + 1) * half)
            part = mm(normed, w_ref[side, :, cols]).astype(BF16)
            if third != 1:
                start = (3 * side + third) * half
                packed_ref[:, start : start + half] = part
            part = part.astype(F32)
            for at in range(tiles // 2):
                keep[side * (tiles // 2) + at] = part[:, lane(at)]
    for at in range(tiles):
        weights = key_softmax(k_s[at], mask_ref[...])
        k_s[at] = weights
        start = (3 * (at // 2) + 1) * half + (at % 2) * LANES
        packed_ref[:, start : start + LANES] = weights.astype(BF16)
    block = head_mask(2 * LANES, head_dim)

    def one_image(image, carry):
        for quad in range(tiles // 2):
            keys = image_rows(k_s, quad, image).astype(BF16)
            values = image_rows(v_s, quad, image).astype(BF16)
            query = image_rows(q_s, quad, image).astype(BF16)
            context = (mm_tn(keys, values) * block).astype(BF16)
            put_image_rows(f_s, quad, image, mm(query, context))
        return carry

    lax.fori_loop(0, IMGS, one_image, 0, unroll=True)
    c_s[:, :IMGS, :] = jnp.zeros((2, IMGS, LANES), F32)
    for pair in range(tiles // 2):
        mask = mask_ref[...]
        v_cells[...] = lane_pair(v_s[2 * pair] * mask, v_s[2 * pair + 1] * mask)
        reach = tile_radius(2 * pair + 1, head_dim)
        for row_at in range(SIDE):
            rows = grid_rows(row_at)
            out = split_pair(conv_row(v_cells, crpe_ref, pair, row_at, reach, 7, False))
            for half_at, value in enumerate(out):
                c_s[half_at, rows, :] = value * mask_ref[rows, :]
        for half_at in range(2):
            at = 2 * pair + half_at
            rel = c_s[half_at]
            rel_ref[:, lane(at)] = rel.astype(BF16)
            mixed_ref[:, lane(at)] = (f_s[at] + q_s[at] * rel).astype(BF16)
    out = conv_ref[...]
    for side in range(2):
        cols = slice(side * half, (side + 1) * half)
        out = out + mm_nt(mixed_ref[:, cols], w_ref[side, :, 3 * half :])
    att_ref[...] = out


def gelu_parts(hidden):
    number = lambda value: jnp.asarray(value, BF16)
    values = hidden.astype(BF16)
    t = pl.reciprocal(
        number(1.0) + number(0.3275911 * 0.7071067811865476) * jnp.abs(values), approx=True
    )
    bell = jnp.exp2(number(-0.5 * 1.4426950408889634) * (values * values))
    poly = number(0.5 * 1.061405429)
    for coef in (-1.453152027, 1.421413741, -0.284496736, 0.254829592):
        poly = poly * t + number(0.5 * coef)
    tail = poly * t * bell
    phi = jnp.where(values >= 0, number(1.0) - tail, tail)
    return values * phi, phi + (values * number(0.3989422804014327)) * bell


def feed_forward(att_ref, up_down_ref, norm_ref, out_ref, act_ref, slope_ref, *scratch, chunk):
    blks, _, both = up_down_ref.shape
    width = both // 2
    chunk = min(chunk, width)
    att = att_ref[...]
    unit, _ = normalize(att)
    normed = (unit * norm_ref[2:3, :] + norm_ref[3:4, :]).astype(BF16)
    total = att
    for blk in range(blks):
        for at in range(0, width, chunk):
            hidden = mm(normed, up_down_ref[blk, :, at : at + chunk])
            active, slope = gelu_parts(hidden)
            cols = slice(blk * width + at, blk * width + at + chunk)
            act_ref[:, cols] = active
            slope_ref[:, cols] = slope
            total = total + mm_nt(active, up_down_ref[blk, :, width + at : width + at + chunk])
    if not scratch:
        out_ref[...] = total
        return
    turn_s, whole_s = scratch
    for at in range(att.shape[1] // LANES):
        cols = lane(at)
        turn_s[...] = total[:, cols]

        def put(rows, values, cols=cols):
            whole_s[rows, cols] = values

        to_image_major(turn_s, put)
    out_ref[...] = whole_s[...].astype(BF16)


def feed_back(*refs, first, chunk):
    if first:
        (mask_ref, cot_ref, att_ref, up_down_ref, norm_ref, out_ref,
         gatt_ref, gweight_ref, gnorm_ref, total_s, act_ref, slope_ref, turn_s, whole_s) = refs
        feed_forward(
            att_ref, up_down_ref, norm_ref, out_ref, act_ref, slope_ref, turn_s, whole_s,
            chunk=chunk,
        )
    else:
        (up_ref, att_ref, act_ref, slope_ref, up_down_ref, norm_ref,
         gatt_ref, gweight_ref, gnorm_ref, total_s) = refs
    step, steps = pl.program_id(0), pl.num_programs(0)
    blks, _, both = up_down_ref.shape
    width = both // 2
    chunk = min(chunk, width)

    @pl.when(step == 0)
    def _():
        total_s[...] = jnp.zeros_like(total_s)
        gnorm_ref[...] = jnp.zeros_like(gnorm_ref)

    if first:
        for at in range(cot_ref.shape[1] // LANES):
            cols = lane(at)
            turn_s[...] = cot_ref[:, cols]

            def put(rows, values, cols=cols):
                whole_s[rows, cols] = values * mask_ref[rows, :]

            to_token_major(turn_s, put)
        upstream = whole_s[...]
    else:
        upstream = up_ref[...]
    unit, inv = normalize(att_ref[...])
    gain = norm_ref[2:3, :]
    normed = (unit * gain + norm_ref[3:4, :]).astype(BF16)
    down_in = upstream.astype(BF16)
    grad_mid = None
    for blk in range(blks):
        for at in range(0, width, chunk):
            cols = slice(blk * width + at, blk * width + at + chunk)
            ups = slice(at, at + chunk)
            downs = slice(width + at, width + at + chunk)
            grad_active = mm(down_in, up_down_ref[blk, :, downs])
            grad_hidden = (grad_active * slope_ref[:, cols].astype(F32)).astype(BF16)
            total_s[blk, :, ups] += mm_tn(normed, grad_hidden)
            total_s[blk, :, downs] += mm_tn(down_in, act_ref[:, cols])
            part = mm_nt(grad_hidden, up_down_ref[blk, :, ups])
            grad_mid = part if grad_mid is None else grad_mid + part
    gatt_ref[...] = upstream + norm_back(grad_mid, unit, inv, gain)
    gnorm_ref[0:1, :] += jnp.sum(grad_mid * unit, axis=0, keepdims=True)
    gnorm_ref[1:2, :] += jnp.sum(grad_mid, axis=0, keepdims=True)

    @pl.when(step == steps - 1)
    def _():
        gweight_ref[...] = total_s[...].astype(BF16)


def attend_back(
    gatt_ref, x_ref, conv_ref, packed_ref, rel_ref, mixed_ref, mask_ref,
    w_ref, norm_ref, cpe_in, crpe_in, gmid_ref, taps_ref,
    out_ref, gw_ref, small_ref, gnorm_ref, gcpe_ref, gcrpe_ref,
    w_s, x_cells, g_cells, v_cells, c_cells, cpe_ref, crpe_ref, q_s, k_s, v_s, f_s, dq_s, dk_s, dv_s, c_s, gp_s,
    *scratch,
):
    channels = x_ref.shape[1]
    tiles = channels // LANES
    head_dim = channels // HEADS
    half = channels // 2
    step, steps = pl.program_id(0), pl.num_programs(0)
    up_ref = scratch[0] if scratch else out_ref

    @pl.when(step == 0)
    def _():
        fill_taps(cpe_in, cpe_ref)
        fill_taps(crpe_in, crpe_ref)
        for ref in (w_s, gnorm_ref, gcpe_ref, gcrpe_ref):
            ref[...] = jnp.zeros_like(ref)

    att_in = gatt_ref[...].astype(BF16)
    att_t = att_in.T
    for side in range(2):
        cols = slice(side * half, (side + 1) * half)
        w_s[side, :, 3 * half :] += mm(att_t, mixed_ref[:, cols])
        grad_mixed = mm(att_in, w_ref[side, :, 3 * half :])
        for at in range(tiles // 2):
            f_s[side * (tiles // 2) + at] = grad_mixed[:, lane(at)]
        for third, keep in enumerate((q_s, k_s, v_s)):
            for at in range(tiles // 2):
                start = (3 * side + third) * half + at * LANES
                keep[side * (tiles // 2) + at] = packed_ref[:, start : start + LANES].astype(F32)
    block = head_mask(2 * LANES, head_dim)

    def one_image(image, carry):
        for quad in range(tiles // 2):
            keys = image_rows(k_s, quad, image).astype(BF16)
            values = image_rows(v_s, quad, image).astype(BF16)
            query = image_rows(q_s, quad, image).astype(BF16)
            grads = image_rows(f_s, quad, image).astype(BF16)
            context = (mm_tn(keys, values) * block).astype(BF16)
            grad_context = (mm_tn(query, grads) * block).astype(BF16)
            put_image_rows(dq_s, quad, image, mm_nt(grads, context))
            put_image_rows(dk_s, quad, image, mm_nt(values, grad_context))
            put_image_rows(dv_s, quad, image, mm(keys, grad_context))
        return carry

    lax.fori_loop(0, IMGS, one_image, 0, unroll=True)
    for pair in range(tiles // 2):
        mask = mask_ref[...]
        place = lambda at, third: slice(
            (3 * pair + third) * half + at * LANES, (3 * pair + third) * half + (at + 1) * LANES
        )
        for half_at in range(2):
            at = 2 * pair + half_at
            weights = k_s[at]
            share = weights * dk_s[at]
            total = jnp.sum(share.reshape(SLOT, IMGS, LANES), axis=0, keepdims=True)
            back = share.reshape(SLOT, IMGS, LANES) - weights.reshape(SLOT, IMGS, LANES) * total
            gp_s[:, place(half_at, 1)] = back.reshape(ROWS, LANES).astype(BF16)
            rel = rel_ref[:, lane(at)].astype(F32)
            gp_s[:, place(half_at, 0)] = (dq_s[at] + f_s[at] * rel).astype(BF16)
        reach = tile_radius(2 * pair + 1, head_dim)
        v_cells[...] = lane_pair(v_s[2 * pair] * mask, v_s[2 * pair + 1] * mask)
        c_cells[...] = lane_pair(
            *[f_s[at] * q_s[at] * mask for at in (2 * pair, 2 * pair + 1)]
        )
        for row_at in range(SIDE):
            rows = grid_rows(row_at)
            out = split_pair(conv_row(c_cells, crpe_ref, pair, row_at, reach, 7, True))
            for half_at, value in enumerate(out):
                dv_s[2 * pair + half_at, rows, :] += value * mask_ref[rows, :]
        conv_kernel_grad(c_cells, v_cells, gcrpe_ref, pair, reach, 7)
        for half_at in range(2):
            gp_s[:, place(half_at, 2)] = dv_s[2 * pair + half_at].astype(BF16)
    unit, inv = normalize(conv_ref[...])
    gain = norm_ref[0:1, :]
    normed_t = (unit * gain + norm_ref[1:2, :]).astype(BF16).T
    grad_rows = None
    for side in range(2):
        part_in = gp_s[:, side * 3 * half : (side + 1) * 3 * half]
        w_s[side, :, : 3 * half] += mm(normed_t, part_in)
        part = mm_nt(part_in, w_ref[side, :, : 3 * half])
        grad_rows = part if grad_rows is None else grad_rows + part
    gnorm_ref[0:1, :] += jnp.sum(grad_rows * unit, axis=0, keepdims=True)
    gnorm_ref[1:2, :] += jnp.sum(grad_rows, axis=0, keepdims=True)
    up_ref[...] = gatt_ref[...] + norm_back(grad_rows, unit, inv, gain)
    for pair in range(tiles // 2):
        both = (lane(2 * pair), lane(2 * pair + 1))
        mask = mask_ref[...]
        x_cells[...] = lane_pair(*[x_ref[:, cols] * mask for cols in both])
        g_cells[...] = lane_pair(*[up_ref[:, cols] * mask for cols in both])
        for row_at in range(SIDE):
            rows = grid_rows(row_at)
            out = split_pair(conv_row(g_cells, cpe_ref, pair, row_at, 1, 3, True))
            for cols, value in zip(both, out):
                up_ref[rows, cols] += value * mask_ref[rows, :]
        conv_kernel_grad(g_cells, x_cells, gcpe_ref, pair, 1, 3)
    for at in range(tiles if scratch else 0):
        cols = lane(at)
        c_s[...] = up_ref[:, cols]

        def put(rows, values, cols=cols):
            out_ref[rows, cols] = values

        to_image_major(c_s, put)

    @pl.when(step == steps - 1)
    def _():
        gw_ref[...] = w_s[...].astype(BF16)
        rows = [gnorm_ref[...], gmid_ref[...], jnp.sum(gcpe_ref[...], axis=1)]
        rows.append(jnp.sum(gcrpe_ref[...], axis=1) * taps_ref[...])
        count = sum(part.shape[0] for part in rows)
        rows.append(jnp.zeros((LANES - count, channels), F32))
        small_ref[...] = jnp.concatenate(rows, axis=0).T.astype(BF16)


def dot3(a, b, dims):
    a_hi, b_hi = a.astype(BF16), b.astype(BF16)
    a_lo = (a - a_hi.astype(F32)).astype(BF16)
    b_lo = (b - b_hi.astype(F32)).astype(BF16)
    one = lambda u, v: lax.dot_general(u, v, (dims, ((), ())), preferred_element_type=F32)
    return one(a_hi, b_hi) + (one(a_hi, b_lo) + one(a_lo, b_hi))


def schulz_turns(blocks):
    first, second, third = SCHULZ_COEFFS
    current = []
    for value in blocks:
        level = jnp.sum(jnp.sum(value * value, axis=0, keepdims=True), axis=1, keepdims=True)
        current.append(value / (jnp.sqrt(level) + 1e-07))
    for _ in range(5):
        grams = [dot3(value, value, ((0,), (0,))) for value in current]
        polys = [second * gram + third * dot3(gram, gram, ((1,), (0,))) for gram in grams]
        current = [
            first * value + dot3(value, poly, ((1,), (0,))) for value, poly in zip(current, polys)
        ]
    return current


def schulz(fresh_ref, out_ref, width):
    parts = (slice(0, width), slice(width, 2 * width))
    for cols, value in zip(parts, schulz_turns([fresh_ref[0, :, c].astype(F32) for c in parts])):
        out_ref[0, :, cols] = value.astype(BF16)


def finish_kernel(
    big_ref, little_ref, big_out, little_out, small_ref,
    big_got, little_got, big_turned, little_turned, big_back, little_back, sems,
):
    count, rows, width = big_ref.shape
    me, blk = lax.axis_index("tok"), lax.axis_index("blk")
    targets = [None] + [lax.rem(me + d, count) for d in range(1, count)]
    sources = [None] + [lax.rem(me + count - d, count) for d in range(1, count)]
    greet([(targets[d], blk) for d in range(1, count)])
    copies = []

    def send(src, dst, kind):
        for d in range(1, count):
            copy = pltpu.make_async_remote_copy(
                src_ref=src.at[targets[d]], dst_ref=dst.at[me],
                send_sem=sems.at[2 * kind, d], recv_sem=sems.at[2 * kind + 1, d],
                device_id=(targets[d], blk), device_id_type=pl.DeviceIdType.MESH,
            )
            copy.start()
            copies.append(copy)
        dst[me] = src[me]

    def arrive(dst, kind):
        for d in range(1, count):
            here = dst.at[sources[d]]
            pltpu.make_async_remote_copy(
                src_ref=here, dst_ref=here,
                send_sem=sems.at[2 * kind, d], recv_sem=sems.at[2 * kind + 1, d],
                device_id=(targets[d], blk), device_id_type=pl.DeviceIdType.MESH,
            ).wait_recv()

    def turn(got, turned):
        fresh = got[:, :, :width].reshape(count * rows, width)
        value = schulz_turns([fresh.astype(F32)])[0]
        turned[...] = value.astype(BF16).reshape(count, rows, width)

    send(big_ref, big_got, 0)
    send(little_ref, little_got, 1)
    arrive(big_got, 0)
    turn(big_got, big_turned)
    send(big_turned, big_back, 2)
    arrive(little_got, 1)
    turn(little_got, little_turned)
    send(little_turned, little_back, 3)
    small_ref[...] = little_got[:, :, width:].reshape(count * rows, little_got.shape[2] - width)
    arrive(big_back, 2)
    big_out[...] = big_back[...]
    arrive(little_back, 3)
    little_out[...] = little_back[...]
    for copy in copies:
        copy.wait_send()


def finish(big, little, collective_id):
    count, rows, width = big.shape
    vmem = pl.BlockSpec(memory_space=pltpu.VMEM)
    block = pltpu.VMEM(big.shape, BF16)
    small = (count * rows, little.shape[2] - width)
    return pl.pallas_call(
        finish_kernel,
        in_specs=[vmem, vmem],
        out_specs=[vmem, vmem, vmem],
        out_shape=[jax.ShapeDtypeStruct(shape, BF16) for shape in (big.shape, big.shape, small)],
        scratch_shapes=[
            block, pltpu.VMEM(little.shape, BF16), block, block, block, block,
            pltpu.SemaphoreType.DMA((8, count)),
        ],
        compiler_params=params_for(collective_id=collective_id, has_side_effects=True),
        cost_estimate=cost(25),
        name="finish",
    )(big, little)


def pack_kernel(qkv_ref, proj_ref, up_ref, down_ref, *outs):
    heads = qkv_ref.shape[2] // (3 * HEAD_DIM)
    for layer, out in enumerate(outs):
        wide = up_ref.shape[2]
        out[:, :wide] = up_ref[layer].astype(BF16)
        out[:, wide : 2 * wide] = down_ref[layer].astype(BF16)
        qkv = qkv_ref[layer]
        parts = [
            qkv[:, (3 * head + third) * HEAD_DIM : (3 * head + third + 1) * HEAD_DIM]
            for third in range(3)
            for head in range(heads)
        ]
        start = 2 * wide + qkv.shape[1]
        out[:, 2 * wide : start] = jnp.concatenate(parts, axis=1).astype(BF16)
        out[:, start:] = proj_ref[layer].astype(BF16)


def pack(mats):
    layers, rows = mats[0].shape[:2]
    cols = sum(mat.shape[2] for mat in mats)
    return pl.pallas_call(
        pack_kernel,
        out_shape=[jax.ShapeDtypeStruct((rows, cols), BF16)] * layers,
        compiler_params=params_for(),
        name="pack",
    )(*mats)


def prepare_kernel(total_ref, early_ref, *refs):
    moments, fresh_refs, (big_ref, little_ref) = refs[:4], refs[4:8], refs[8:]
    qkv_m, proj_m, up_m, down_m = moments
    layers, rows, wide = up_m.shape
    span = qkv_m.shape[2]
    heads = span // (3 * HEAD_DIM)
    half = heads * HEAD_DIM
    width = big_ref.shape[2]
    groups = wide // width
    cut = 4 * half + LANES
    little_ref[...] = jnp.zeros_like(little_ref)
    small = []
    for layer in range(layers):
        at = cut if layer == 0 else 0
        sums = total_ref[:, at : at + cut]
        feed = total_ref[:, 2 * cut :] if layer == 0 else early_ref[...].astype(F32)
        small.append(sums[:, 4 * half : 4 * half + SMALL_ROWS])
        parts = [
            sums[:, third * half + head * HEAD_DIM : third * half + (head + 1) * HEAD_DIM]
            for head in range(heads)
            for third in range(3)
        ]
        qkv = 0.5 * qkv_m[layer] + jnp.concatenate(parts, axis=1)
        fresh_refs[0][layer] = qkv
        proj = 0.5 * proj_m[layer] + sums[:, 3 * half : 4 * half]
        fresh_refs[1][layer] = proj
        up = 0.5 * up_m[layer] + feed[:, :wide]
        fresh_refs[2][layer] = up
        down = 0.5 * down_m[layer] + feed[:, wide:]
        fresh_refs[3][layer] = down
        unit = layer * 2 * groups
        for group in range(groups):
            cols = slice(group * width, (group + 1) * width)
            big_ref[unit + group] = up[:, cols].astype(BF16)
            big_ref[unit + groups + group] = down[:, cols].astype(BF16)
        unit = layer * 2 * heads
        for head in range(heads):
            block = qkv[:, 3 * head * HEAD_DIM : 3 * (head + 1) * HEAD_DIM]
            little_ref[unit + head, :, : 3 * HEAD_DIM] = block.astype(BF16)
            block = proj[:, head * HEAD_DIM : (head + 1) * HEAD_DIM]
            little_ref[unit + heads + head, :, :HEAD_DIM] = block.astype(BF16)
    small.append(jnp.zeros((rows, LANES - layers * SMALL_ROWS), F32))
    small = jnp.concatenate(small, axis=1).astype(BF16)
    for unit in range(little_ref.shape[0]):
        little_ref[unit, :, width:] = small


def prepare(total, early, moments, units, width):
    rows = moments[2].shape[1]
    shapes = [jax.ShapeDtypeStruct(moment.shape, F32) for moment in moments]
    shapes.append(jax.ShapeDtypeStruct((units, rows, width), BF16))
    shapes.append(jax.ShapeDtypeStruct((units, rows, width + LANES), BF16))
    return pl.pallas_call(
        prepare_kernel,
        out_shape=shapes,
        compiler_params=params_for(),
        name="prepare",
    )(total, early, *moments)


def small_step(param, moment, grad, rate, level):
    fresh = 0.5 * moment + grad
    return fresh, param - rate * fresh / (jnp.sqrt(level(fresh * fresh)) + 1e-06)


def update_kernel(big_ref, little_ref, small_ref, *refs, scales):
    mats, params, moments = refs[:4], refs[4:7], refs[7:10]
    outs = refs[10:]
    layers, rows, wide = mats[2].shape
    width = big_ref.shape[2]
    groups = wide // width
    heads = mats[0].shape[2] // (3 * HEAD_DIM)
    small = small_ref[...].astype(F32).T
    for layer in range(layers):
        unit = layer * 2 * heads
        join = lambda blocks: jnp.concatenate([block.astype(F32) for block in blocks], axis=1)
        qkv = join([little_ref[unit + head, :, : 3 * HEAD_DIM] for head in range(heads)])
        proj = join([little_ref[unit + heads + head, :, :HEAD_DIM] for head in range(heads)])
        unit = layer * 2 * groups
        up = join([big_ref[unit + group] for group in range(groups)])
        down = join([big_ref[unit + groups + group] for group in range(groups)])
        for kind, turned in enumerate((qkv, proj, up, down)):
            new = mats[kind][layer] - scales[kind] * turned
            outs[2 * kind][layer] = new
            outs[2 * kind + 1][layer] = new.astype(BF16)
        grads = small[layer * SMALL_ROWS : (layer + 1) * SMALL_ROWS]
        row_mean = lambda square: jnp.mean(square, axis=1, keepdims=True)
        all_mean = lambda square: jnp.mean(row_mean(square), axis=0, keepdims=True)

        def head_mean(square):
            column = jnp.mean(square, axis=0, keepdims=True)
            spans = [
                jnp.broadcast_to(
                    row_mean(column[:, head * HEAD_DIM : (head + 1) * HEAD_DIM]), (1, HEAD_DIM)
                )
                for head in range(HEADS)
            ]
            return jnp.concatenate(spans, axis=1)

        start = 0
        for kind, level in enumerate((row_mean, all_mean, head_mean)):
            place = (layer,) if kind == 0 else (slice(None), layer)
            count = params[kind].shape[1 if kind == 0 else 0]
            fresh, new = small_step(
                params[kind][place], moments[kind][place], grads[start : start + count],
                SMALL_RATES[kind], level,
            )
            outs[8 + 2 * kind][place] = fresh
            outs[9 + 2 * kind][place] = new
            start += count


def update(big, little, small, mats, params, moments, scales):
    shapes = []
    for mat in mats:
        shapes += [jax.ShapeDtypeStruct(mat.shape, F32), jax.ShapeDtypeStruct(mat.shape, BF16)]
    for param in params:
        shapes += [jax.ShapeDtypeStruct(param.shape, F32)] * 2
    return pl.pallas_call(
        functools.partial(update_kernel, scales=scales),
        out_shape=shapes,
        compiler_params=params_for(),
        name="update",
    )(big, little, small, *mats, *params, *moments)


def params_for(**more):
    return pltpu.CompilerParams(vmem_limit_bytes=VMEM_BYTES, **more)


def block_of(cols):
    return pl.BlockSpec((ROWS, cols), lambda g: (g, 0))


def whole(array):
    shape = array.shape
    return pl.BlockSpec(shape, lambda g: (0,) * len(shape), pipeline_mode=pl.Buffered(1))


def some_columns(weights):
    array, width, at = weights
    shape = array.shape[:2] + (width,)
    return pl.BlockSpec(shape, lambda g: (0, 0, at), pipeline_mode=pl.Buffered(1))


def whole_out(shape):
    return pl.BlockSpec(shape, lambda g: (0,) * len(shape))


def tap_tables(channels):
    return [pltpu.VMEM((channels // (2 * LANES), taps, 2 * IMGS, LANES), BF16) for taps in (9, 49)]


def cost(us):
    return pl.CostEstimate(flops=int(us * 1e9), bytes_accessed=int(us * 1e5), transcendentals=0)


def run_attend_forward(x, mask, weights, norm, cpe, crpe, first):
    count, channels = x.shape
    tiles = channels // LANES
    flat = pltpu.VMEM((tiles, ROWS, LANES), F32)
    cells = pltpu.VMEM((SIDE, SIDE, 2 * IMGS, LANES), BF16)
    out = lambda cols, kind: jax.ShapeDtypeStruct((count, cols), kind)
    outs = [out(channels, F32), out(3 * channels, BF16)] + [out(channels, BF16)] * 2
    outs = [out(channels, F32)] * first + outs + [out(channels, F32)]
    return pl.pallas_call(
        functools.partial(attend_forward, first=first),
        grid=(count // ROWS,),
        in_specs=[block_of(channels), block_of(LANES)]
        + [some_columns(weights)]
        + [whole(a) for a in (norm, cpe, crpe)],
        out_specs=[block_of(array.shape[1]) for array in outs],
        out_shape=outs,
        scratch_shapes=[
            cells, cells, *tap_tables(channels), flat, flat, flat, flat,
            pltpu.VMEM((2, ROWS, LANES), F32),
        ],
        compiler_params=params_for(),
        cost_estimate=cost(50),
        name="attend_forward",
    )(x, mask, weights[0], norm, cpe, crpe)


def run_feed_forward(att, up_down, norm, chunk=512):
    count, channels = att.shape
    hidden = up_down[0].shape[0] * up_down[1] // 2
    return pl.pallas_call(
        functools.partial(feed_forward, chunk=chunk),
        grid=(count // ROWS,),
        in_specs=[block_of(channels), some_columns(up_down), whole(norm)],
        out_specs=[block_of(channels), block_of(hidden), block_of(hidden)],
        out_shape=[
            jax.ShapeDtypeStruct((count, channels), F32),
            jax.ShapeDtypeStruct((count, hidden), BF16),
            jax.ShapeDtypeStruct((count, hidden), BF16),
        ],
        compiler_params=params_for(),
        cost_estimate=cost(24),
        name="feed_forward",
    )(att, up_down[0], norm)


def run_feed_back(inputs, up_down, norm, first, chunk=512):
    count, channels = inputs[1].shape
    hidden = up_down[0].shape[0] * up_down[1] // 2
    shape = up_down[0].shape[:2] + (up_down[1],)
    more = [
        pltpu.VMEM((ROWS, hidden), BF16), pltpu.VMEM((ROWS, hidden), BF16),
        pltpu.VMEM((ROWS, LANES), F32), pltpu.VMEM((ROWS, channels), F32),
    ]
    return pl.pallas_call(
        functools.partial(feed_back, first=first, chunk=chunk),
        grid=(count // ROWS,),
        in_specs=[block_of(array.shape[1]) for array in inputs]
        + [some_columns(up_down), whole(norm)],
        out_specs=[block_of(channels)] * first
        + [block_of(channels), whole_out(shape), whole_out((2, channels))],
        out_shape=[jax.ShapeDtypeStruct((count, channels), BF16)] * first
        + [
            jax.ShapeDtypeStruct((count, channels), F32),
            jax.ShapeDtypeStruct(shape, BF16),
            jax.ShapeDtypeStruct((2, channels), F32),
        ],
        scratch_shapes=[pltpu.VMEM(shape, F32)] + more * first,
        compiler_params=params_for(),
        cost_estimate=cost(50 if first else 37),
        name="feed_back",
    )(*inputs, up_down[0], norm)


def run_attend_back(
    gatt, x, conv, packed, rel, mixed, mask, weights, norm, cpe, crpe, gmid, taps, last
):
    count, channels = x.shape
    tiles = channels // LANES
    flat = pltpu.VMEM((tiles, ROWS, LANES), F32)
    cells = pltpu.VMEM((SIDE, SIDE, 2 * IMGS, LANES), BF16)
    small = [(2, channels), (9, IMGS, channels), (49, IMGS, channels)]
    shape = weights[0].shape[:2] + (weights[1],)
    return pl.pallas_call(
        attend_back,
        grid=(count // ROWS,),
        in_specs=[block_of(channels)] * 3
        + [block_of(3 * channels), block_of(channels), block_of(channels), block_of(LANES)]
        + [some_columns(weights)]
        + [whole(a) for a in (norm, cpe, crpe, gmid, taps)],
        out_specs=[block_of(channels), whole_out(shape), whole_out((channels, LANES))],
        out_shape=[
            jax.ShapeDtypeStruct((count, channels), F32),
            jax.ShapeDtypeStruct(shape, BF16),
            jax.ShapeDtypeStruct((channels, LANES), BF16),
        ],
        scratch_shapes=[pltpu.VMEM(each, F32) for each in small]
        + [
            pltpu.VMEM(shape, F32),
            cells, cells, cells, cells, *tap_tables(channels),
            flat, flat, flat, flat, flat, flat, flat,
            pltpu.VMEM((ROWS, LANES), F32),
            pltpu.VMEM((ROWS, 3 * channels), BF16),
        ]
        + [pltpu.VMEM((ROWS, channels), F32)] * last,
        compiler_params=params_for(),
        cost_estimate=cost(65),
        name="attend_back",
    )(gatt, x, conv, packed, rel, mixed, mask, weights[0], norm, cpe, crpe, gmid, taps)


def where_am_i():
    tok, blk = lax.axis_index("tok"), lax.axis_index("blk")
    core, x, z = lax.rem(tok, 2), lax.rem(tok // 2, 2), tok // 4
    return blk, z, x, core


def device_at(y, z, x, core):
    return (z * 4 + x * 2 + core, y)


def neighbours(y, z, x, core):
    fx, fy = 1 - core, core
    flip = lambda value, by: value + by - 2 * value * by
    first = (flip(y, fy), flip(x, fx))
    second = (flip(y, fx), flip(x, fy))
    cross = (1 - y, 1 - x)
    return first, second, cross


def greet(targets):
    barrier = pltpu.get_barrier_semaphore()
    for target in targets:
        pl.semaphore_signal(barrier, inc=1, device_id=target, device_id_type=pl.DeviceIdType.MESH)
    pl.semaphore_wait(barrier, len(targets))


def spread_kernel(shard_ref, out_ref, send_sem, recv_sem, own_sem):
    y, z, x, core = where_am_i()
    first, second, cross = neighbours(y, z, x, core)
    line = [lax.rem(z + d, 4) for d in range(4)]
    back = [lax.rem(z + 4 - d, 4) for d in range(4)]
    to_first = device_at(first[0], z, first[1], core)
    to_second = device_at(second[0], z, second[1], core)
    to_core = device_at(y, z, x, 1 - core)
    greet([to_first, to_second, to_core] + [device_at(y, line[d], x, core) for d in (1, 2, 3)])
    slot = lambda at, layer, side: at[0] * 16 + layer * 4 + at[1] * 2 + side
    own = pltpu.make_async_copy(shard_ref, out_ref.at[slot((y, x), z, core)], own_sem)
    own.start()
    copies = []

    def send(src, at, layer, side, target, number):
        copy = pltpu.make_async_remote_copy(
            src_ref=src, dst_ref=out_ref.at[slot(at, layer, side)],
            send_sem=send_sem.at[number], recv_sem=recv_sem.at[number],
            device_id=target, device_id_type=pl.DeviceIdType.MESH,
        )
        copy.start()
        copies.append(copy)

    def arrive(at, layer, side, number):
        here = out_ref.at[slot(at, layer, side)]
        pltpu.make_async_remote_copy(
            src_ref=here, dst_ref=here, send_sem=send_sem.at[number], recv_sem=recv_sem.at[number],
            device_id=to_core, device_id_type=pl.DeviceIdType.MESH,
        ).wait_recv()

    me = (y, x)
    for d in (1, 2, 3):
        send(shard_ref, me, z, core, device_at(y, line[d], x, core), d - 1)
    for d in range(4):
        layer = back[d]
        if d:
            arrive(me, layer, core, d - 1)
        src = out_ref.at[slot(me, layer, core)] if d else shard_ref
        send(src, me, layer, core, to_first, 3 + d)
        send(src, me, layer, core, to_second, 7 + d)
        send(src, me, layer, core, to_core, 15 + d)
    for d in range(4):
        arrive(first, back[d], core, 3 + d)
        src = out_ref.at[slot(first, back[d], core)]
        send(src, first, back[d], core, to_second, 11 + d)
        send(src, first, back[d], core, to_core, 19 + d)
    for d in range(4):
        arrive(second, back[d], core, 7 + d)
        send(out_ref.at[slot(second, back[d], core)], second, back[d], core, to_core, 23 + d)
    for d in range(4):
        arrive(cross, back[d], core, 11 + d)
        send(out_ref.at[slot(cross, back[d], core)], cross, back[d], core, to_core, 27 + d)
    for d in range(4):
        arrive(me, back[d], 1 - core, 15 + d)
        arrive(second, back[d], 1 - core, 19 + d)
        arrive(first, back[d], 1 - core, 23 + d)
        arrive(cross, back[d], 1 - core, 27 + d)
    own.wait()
    for copy in copies:
        copy.wait_send()


def spread(shard, collective_id):
    return pl.pallas_call(
        spread_kernel,
        in_specs=[pl.BlockSpec(memory_space=pl.ANY)],
        out_specs=pl.BlockSpec(memory_space=pl.ANY),
        out_shape=jax.ShapeDtypeStruct((32,) + shard.shape, shard.dtype),
        scratch_shapes=[
            pltpu.SemaphoreType.DMA((31,)), pltpu.SemaphoreType.DMA((31,)), pltpu.SemaphoreType.DMA,
        ],
        compiler_params=pltpu.CompilerParams(
            collective_id=collective_id, has_side_effects=True, vmem_limit_bytes=VMEM_BYTES
        ),
        name="spread",
    )(shard)


def collect_kernel(*refs, widths):
    parts = len(widths)
    grads, out_ref = refs[:parts], refs[parts]
    own_s, chip_s, second_s, first_s, line_s, send_sem, recv_sem, load_sem = refs[parts + 1 :]
    y, z, x, core = where_am_i()
    first, second, cross = neighbours(y, z, x, core)
    line = [lax.rem(z + d, 4) for d in range(4)]
    back = [lax.rem(z + 4 - d, 4) for d in range(4)]
    to_first = device_at(first[0], z, first[1], core)
    to_second = device_at(second[0], z, second[1], core)
    to_core = device_at(y, z, x, 1 - core)
    greet([to_first, to_second, to_core] + [device_at(y, line[d], x, core) for d in (1, 2, 3)])
    mine = lambda at, layer, side: own_s.at[at[0] * 8 + layer * 2 + at[1], side]
    loads = []
    for turn, side in enumerate((1 - core, core)):
        start = 0
        for number, (grad, width) in enumerate(zip(grads, widths)):
            copy = pltpu.make_async_copy(
                grad.at[:, side], own_s.at[: grad.shape[0], side, :, start : start + width],
                load_sem.at[turn, number, 0],
            )
            copy.start()
            loads.append((turn, copy))
            if grad.shape[0] == 8:
                copy = pltpu.make_async_copy(
                    grad.at[:, side], own_s.at[8:, side, :, start : start + width],
                    load_sem.at[turn, number, 1],
                )
                copy.start()
                loads.append((turn, copy))
            start += width
    for turn, copy in loads:
        if turn == 0:
            copy.wait()
    copies = []

    def send(src, dst, target, number):
        copy = pltpu.make_async_remote_copy(
            src_ref=src, dst_ref=dst, send_sem=send_sem.at[number], recv_sem=recv_sem.at[number],
            device_id=target, device_id_type=pl.DeviceIdType.MESH,
        )
        copy.start()
        copies.append(copy)

    def arrive(ref, number):
        pltpu.make_async_remote_copy(
            src_ref=ref, dst_ref=ref, send_sem=send_sem.at[number], recv_sem=recv_sem.at[number],
            device_id=to_core, device_id_type=pl.DeviceIdType.MESH,
        ).wait_recv()

    def add(ref, *others):
        total = ref[...].astype(F32)
        for other in others:
            total = total + other[...].astype(F32)
        ref[...] = total.astype(BF16)

    me = (y, x)
    places = (cross, first, second, me)
    theirs = (0, 2, 1, 3)
    turns = (2, 1, 3, 0)
    for d in turns:
        for kind in (0, 2, 1, 3):
            number = theirs[kind] * 4 + d
            send(mine(places[kind], line[d], 1 - core), chip_s.at[number], to_core, number)

    for turn, copy in loads:
        if turn == 1:
            copy.wait()

    def fold(kind, d):
        here = chip_s.at[kind * 4 + d]
        arrive(here, kind * 4 + d)
        own = mine(places[kind], line[d], core)
        if kind in (0, 2):
            there = 0 if kind == 0 else 4
            add(here, own)
            send(here, second_s.at[there + d], to_second, 16 + there + d)
        elif kind == 1:
            arrive(second_s.at[d], 16 + d)
            add(here, own, second_s.at[d])
            send(here, first_s.at[d], to_first, 24 + d)
        else:
            arrive(second_s.at[4 + d], 20 + d)
            arrive(first_s.at[d], 24 + d)
            if d:
                add(here, own, second_s.at[4 + d], first_s.at[d])
                send(here, line_s.at[d - 1], device_at(y, line[d], x, core), 27 + d)

    stages = [(0, 2), (1,), (3,)]
    for turn in range(len(turns) + 2):
        for stage, kinds in enumerate(stages):
            if 0 <= turn - stage < len(turns):
                for kind in kinds:
                    fold(kind, turns[turn - stage])
    for d in (1, 2, 3):
        arrive(line_s.at[d - 1], 27 + d)
    total = chip_s[12].astype(F32) + mine(me, z, core)[...].astype(F32)
    for ref in (second_s.at[4], first_s.at[0], line_s.at[0], line_s.at[1], line_s.at[2]):
        total = total + ref[...].astype(F32)
    out_ref[...] = total
    for copy in copies:
        copy.wait_send()


def collect(grads, collective_id):
    rows = grads[0].shape[2]
    widths = tuple(grad.shape[3] for grad in grads)
    block = lambda count: pltpu.VMEM((count, rows, sum(widths)), BF16)
    return pl.pallas_call(
        functools.partial(collect_kernel, widths=widths),
        in_specs=[pl.BlockSpec(memory_space=pl.ANY)] * len(grads),
        out_specs=pl.BlockSpec(memory_space=pltpu.VMEM),
        out_shape=jax.ShapeDtypeStruct((rows, sum(widths)), F32),
        scratch_shapes=[
            pltpu.VMEM((16, 2, rows, sum(widths)), BF16), block(16), block(8), block(4), block(3),
            pltpu.SemaphoreType.DMA((31,)), pltpu.SemaphoreType.DMA((31,)),
            pltpu.SemaphoreType.DMA((2, len(widths), 2)),
        ],
        compiler_params=pltpu.CompilerParams(
            collective_id=collective_id, has_side_effects=True, vmem_limit_bytes=VMEM_BYTES
        ),
        name="collect",
    )(*grads)


def run_schulz(fresh, width):
    units, height, _ = fresh.shape
    spec = pl.BlockSpec((1, height, 2 * width), lambda g: (g, 0, 0))
    return pl.pallas_call(
        lambda *refs: schulz(*refs, width=width),
        grid=(units,),
        in_specs=[spec],
        out_specs=spec,
        out_shape=jax.ShapeDtypeStruct((units, height, 2 * width), BF16),
        compiler_params=params_for(),
        name="schulz",
    )(fresh)


def token_major(rows):
    count, channels = rows.shape
    split = rows.reshape(count // ROWS, IMGS, SLOT, channels)
    return split.transpose(0, 2, 1, 3).reshape(count, channels)


def image_major(rows):
    count, channels = rows.shape
    split = rows.reshape(count // ROWS, SLOT, IMGS, channels)
    return split.transpose(0, 2, 1, 3).reshape(count, channels)


def key_masks(grid_class):
    extent = 5 + 2 * grid_class
    across = (jnp.arange(SIDE, dtype=jnp.int32)[None, :] < extent[:, None]).astype(F32)
    cells = (across[:, :, None] * across[:, None, :]).reshape(-1, SIDE * SIDE)
    return jnp.concatenate([jnp.ones((cells.shape[0], 1), F32), cells], axis=1)


def split_heads(shard, heads_own, head_dim):
    lead = shard.shape[:-1]
    parts = shard.reshape(lead + (heads_own, 3, head_dim))
    return jnp.swapaxes(parts, -3, -2).reshape(lead + (3 * heads_own * head_dim,))


def join_heads(shard, heads_own, head_dim):
    lead = shard.shape[:-1]
    parts = shard.reshape(lead + (3, heads_own, head_dim))
    return jnp.swapaxes(parts, -3, -2).reshape(lead + (3 * heads_own * head_dim,))


def block_scale(height, breadth):
    return math.sqrt(max(1.0, height / breadth))


def normalized_step(param_vals, moment, grads_in, rate, axes):
    fresh = 0.5 * moment + grads_in
    level = jnp.sqrt(jnp.mean(fresh * fresh, axis=axes, keepdims=True))
    return (fresh, param_vals - rate * fresh / (level + 1e-06))


def on_device(
    tokens, cotangent, grid_class,
    qkv_weight, proj_weight, up_weight, down_weight, norm_params, cpe_weight, crpe_weight,
    qkv_moment, proj_moment, up_moment, down_moment, norm_moment, cpe_moment, crpe_moment,
):
    own_count, channels = tokens.shape
    blk_count = lax.axis_size("blk")
    tok_count = lax.axis_size("tok")
    blk_at = lax.axis_index("blk")
    layers = qkv_weight.shape[0]
    images_own = grid_class.shape[0] // blk_count
    head_dim = channels // HEADS
    heads_own = HEADS // blk_count
    groups_own = GROUPS // blk_count
    group_width = up_weight.shape[2] // groups_own
    own_rows = qkv_weight.shape[1]
    both = ("blk", "tok")

    attn_cols, feed_cols = 4 * heads_own * head_dim, 2 * up_weight.shape[2]
    near = (tok_count, blk_count, layers) == (16, 2, 2)
    turn = lambda array: jnp.swapaxes(array, 1, 2)
    flip = lambda array: jnp.swapaxes(array, 0, 1)
    mats = (qkv_weight, turn(proj_weight), up_weight, turn(down_weight))
    moments = (qkv_moment, turn(proj_moment), up_moment, turn(down_moment))
    if near:
        shard = pack(mats)
    else:
        shard = jnp.concatenate(
            [
                up_weight,
                jnp.swapaxes(down_weight, 1, 2),
                split_heads(qkv_weight, heads_own, head_dim),
                jnp.swapaxes(proj_weight, 1, 2),
            ],
            axis=2,
        ).astype(BF16)

    def gather(piece, kernel):
        if kernel:
            return spread(piece, 1).reshape(blk_count, channels, piece.shape[1])
        full = lax.all_gather(piece, both, axis=0, tiled=True)
        return full.reshape(blk_count, channels, piece.shape[1])

    def halves(full):
        full = full.reshape(blk_count, channels, 4, heads_own * head_dim).transpose(1, 2, 0, 3)
        full = full.reshape(channels, 4, 2, channels // 2).transpose(2, 0, 1, 3)
        return full.reshape(2, channels, 2 * channels)

    def shares(grads):
        if blk_count == 2:
            return grads
        full = grads.reshape(2, channels, 4, channels // 2).transpose(1, 2, 0, 3)
        full = full.reshape(channels, 4, blk_count, heads_own * head_dim).transpose(2, 0, 1, 3)
        return full.reshape(blk_count, channels, attn_cols)

    attn_all, feed_all = [], []
    for layer in range(layers):
        piece = shard[layer]
        if layer and near:
            piece, full = lax.optimization_barrier((piece, full))
            attn_all[0], feed_all[0] = (full, attn_cols, 2), (full, feed_cols, 0)
        full = gather(piece, near and layer == 0)
        if blk_count == 2:
            attn_all.append((full, attn_cols, 2))
            feed_all.append((full, feed_cols, 0))
        else:
            attn_all.append((halves(full[:, :, feed_cols:]), 2 * channels, 0))
            feed_all.append((full[:, :, :feed_cols], feed_cols, 0))

    own_class = lax.dynamic_slice_in_dim(grid_class, blk_at * images_own, images_own)
    keys = key_masks(own_class)
    mask = jnp.broadcast_to(token_major(keys.reshape(own_count, 1)), (own_count, LANES))
    taps = jnp.repeat(tap_mask(jnp.arange(HEADS, dtype=jnp.int32)), head_dim, axis=1)

    stream = tokens
    saved = []
    for layer in range(layers):
        cpe, crpe = cpe_weight[layer], crpe_weight[layer] * taps
        outs = run_attend_forward(
            stream, mask, attn_all[layer], norm_params[layer], cpe, crpe, layer == 0
        )
        if layer:
            outs = [stream] + list(outs)
        active = slope = None
        if layer < layers - 1:
            stream, active, slope = run_feed_forward(outs[-1], feed_all[layer], norm_params[layer])
        saved.append(tuple(outs) + (active, slope, cpe, crpe))

    upstream = cotangent
    attn_sums, feed_sums = [None] * layers, [None] * layers
    small_rows = SMALL_ROWS
    for layer in reversed(range(layers)):
        x, conv, packed, rel, mixed, att, active, slope, cpe, crpe = saved[layer]
        last = layer == layers - 1
        inputs = [mask, upstream, att] if last else [upstream, att, active, slope]
        outs = run_feed_back(inputs, feed_all[layer], norm_params[layer], last)
        if last:
            block_out = outs[0]
        gatt, gfeed, gmid = outs[-3:]
        upstream, gattn, small = run_attend_back(
            gatt, x, conv, packed, rel, mixed, mask, attn_all[layer],
            norm_params[layer], cpe, crpe, gmid, taps, layer == 0,
        )
        if near and layer == layers - 1:
            early = lax.psum_scatter(
                gfeed.reshape(blk_count * channels, gfeed.shape[2]), both,
                scatter_dimension=0, tiled=True,
            )
        gattn = shares(gattn)
        if near:
            split = lambda g: g.reshape(-1, 2, own_rows, g.shape[-1])
            pieces = [split(g) for g in (gattn, small, gfeed)]
            waiting = pieces[:2] if layer else waiting + pieces
        else:
            small = jnp.broadcast_to(small, (blk_count, channels, LANES))
            scatter = lambda g: lax.psum_scatter(
                g.reshape(blk_count * channels, g.shape[2]), both, scatter_dimension=0, tiled=True
            ).astype(F32)
            feed_sums[layer] = scatter(gfeed)
            attn_sums[layer] = scatter(jnp.concatenate([gattn, small], axis=2))
    tokens_grad = upstream

    scales = (
        block_scale(channels, 3 * head_dim),
        block_scale(head_dim, channels),
        block_scale(channels, group_width),
        block_scale(group_width, channels),
    )
    if near:
        early, waiting = lax.optimization_barrier((early, waiting))
        total = collect(waiting, 2)
        ready = prepare(total, early, moments, tok_count, group_width)
        big, little, small_all = finish(ready[4], ready[5], 3)
        done = update(
            big, little, small_all, mats,
            (norm_params, flip(cpe_weight), flip(crpe_weight)),
            (norm_moment, flip(cpe_moment), flip(crpe_moment)),
            tuple(rate * scale for rate, scale in zip(MUON_RATES, scales)),
        )
        results = []
        for kind in range(4):
            three = (ready[kind], done[2 * kind], done[2 * kind + 1])
            results += [turn(array) if kind % 2 else array for array in three]
        return (block_out, tokens_grad, *results, *done[8:10], *map(flip, done[10:]))
    attn_sum = jnp.stack(attn_sums)
    feed_sum = jnp.stack(feed_sums)
    small_sum = attn_sum[:, :, -LANES:][:, :, :small_rows]
    attn_sum = attn_sum[:, :, :-LANES]
    attn_moment = jnp.concatenate(
        [split_heads(qkv_moment, heads_own, head_dim), jnp.swapaxes(proj_moment, 1, 2)], axis=2
    )
    feed_moment = jnp.concatenate([up_moment, jnp.swapaxes(down_moment, 1, 2)], axis=2)
    attn_fresh = 0.5 * attn_moment + attn_sum
    feed_fresh = 0.5 * feed_moment + feed_sum

    units = layers * 2 * groups_own
    per_dev = -(-units // tok_count)
    big = feed_fresh.reshape(layers, own_rows, 2 * groups_own, group_width)
    big = big.transpose(0, 2, 1, 3).reshape(units, own_rows, group_width)
    heads = attn_fresh.reshape(layers, own_rows, 4, heads_own, head_dim).transpose(0, 3, 1, 2, 4)
    heads_qkv = heads[:, :, :, :3].reshape(layers, heads_own, own_rows, 3 * head_dim)
    heads_proj = heads[:, :, :, 3]
    widen = lambda v: jnp.pad(v, ((0, 0), (0, 0), (0, 0), (0, group_width - v.shape[3])))
    little = jnp.concatenate([widen(heads_qkv), widen(heads_proj)], axis=1)
    little = little.reshape(units, own_rows, group_width)
    def owners(blocks):
        blocks = jnp.pad(blocks.astype(BF16), ((0, per_dev * tok_count - units), (0, 0), (0, 0)))
        return blocks.reshape(tok_count, per_dev, own_rows, group_width)

    big, little = owners(big), owners(little)
    small_own = jnp.swapaxes(small_sum, 0, 1).reshape(own_rows, layers * small_rows)
    small_own = jnp.pad(small_own, ((0, 0), (0, LANES - layers * small_rows))).astype(BF16)
    small_own = jnp.broadcast_to(small_own, (tok_count, per_dev, own_rows, LANES))
    little = jnp.concatenate([little, small_own], axis=3)
    got = lax.all_to_all(jnp.concatenate([big, little], axis=3), "tok", 0, 0, tiled=True)
    got = got.transpose(1, 0, 2, 3).reshape(per_dev, channels, 2 * group_width + LANES)
    small_all = got[0, :, 2 * group_width :]
    ortho = run_schulz(got, group_width)
    ortho = ortho.reshape(per_dev, tok_count, own_rows, 2 * group_width)
    ortho = lax.all_to_all(ortho.transpose(1, 0, 2, 3), "tok", 0, 0, tiled=True)
    ortho = ortho.reshape(per_dev * tok_count, own_rows, 2 * group_width)[:units]
    big, little = ortho[:, :, :group_width], ortho[:, :, group_width:]
    small_all = small_all.astype(F32).T[: layers * small_rows]
    small_all = small_all.reshape(layers, small_rows, channels)
    big = big.astype(F32).reshape(layers, 2, groups_own, own_rows, group_width)
    big = big.transpose(1, 0, 3, 2, 4).reshape(2, layers, own_rows, groups_own * group_width)
    little = little.astype(F32).reshape(layers, 2, heads_own, own_rows, group_width)
    little_qkv = little[:, 0, :, :, : 3 * head_dim].transpose(0, 2, 1, 3)
    little_qkv = little_qkv.reshape(layers, own_rows, heads_own * 3 * head_dim)
    little_proj = little[:, 1, :, :, :head_dim].transpose(0, 1, 3, 2)
    little_proj = little_proj.reshape(layers, heads_own * head_dim, own_rows)

    qkv_fresh = join_heads(attn_fresh[:, :, : qkv_weight.shape[2]], heads_own, head_dim)
    proj_fresh = jnp.swapaxes(attn_fresh[:, :, qkv_weight.shape[2] :], 1, 2)
    up_fresh = feed_fresh[:, :, : up_weight.shape[2]]
    down_fresh = jnp.swapaxes(feed_fresh[:, :, up_weight.shape[2] :], 1, 2)
    results = []
    for kind, (weight, fresh, turned) in enumerate(
        (
            (qkv_weight, qkv_fresh, little_qkv),
            (proj_weight, proj_fresh, little_proj),
            (up_weight, up_fresh, big[0]),
            (down_weight, down_fresh, jnp.swapaxes(big[1], 1, 2)),
        )
    ):
        new = weight - MUON_RATES[kind] * scales[kind] * turned
        results.extend([fresh, new, new.astype(BF16)])

    norm_fresh, norm_new = normalized_step(
        norm_params, norm_moment, small_all[:, :4], SMALL_RATES[0], (2,)
    )
    cpe_fresh, cpe_new = normalized_step(
        cpe_weight, cpe_moment, small_all[:, 4:13], SMALL_RATES[1], (1, 2)
    )
    head_shape = (layers, 49, HEADS, head_dim)
    crpe_fresh, crpe_new = normalized_step(
        crpe_weight.reshape(head_shape),
        crpe_moment.reshape(head_shape),
        small_all[:, 13:].reshape(head_shape),
        SMALL_RATES[2],
        (1, 3),
    )
    return (
        (block_out, tokens_grad)
        + tuple(results)
        + (norm_fresh, norm_new, cpe_fresh, cpe_new)
        + (crpe_fresh.reshape(crpe_weight.shape), crpe_new.reshape(crpe_weight.shape))
    )


def solution(mesh):
    rows = P(("tok", "blk"), None)
    down_cols = P(None, "tok", "blk")
    cross = P(None, "blk", "tok")
    mats = (down_cols, cross, down_cols, cross)
    in_specs = (rows, rows, P("tok")) + mats + (P(),) * 3 + mats + (P(),) * 3
    out_specs = (rows, rows) + tuple(spec for spec in mats for _ in range(3)) + (P(),) * 6
    return jax.shard_map(
        on_device, mesh=mesh, in_specs=in_specs, out_specs=out_specs, check_vma=False
    )
```

```python
import functools
import math

import jax
import jax.numpy as jnp
from jax import lax
from jax.experimental import pallas as pl
from jax.experimental.pallas import tpu as pltpu
from jax.sharding import PartitionSpec as P

HEADS = 8
GROUPS = 8
SLOT = 82
SIDE = 9
LANES = 128
IMGS = 8
ROWS = SLOT * IMGS
SCHULZ_COEFFS = (3.4445, -4.775, 2.0315)
MUON_RATES = (0.8, 0.8, 0.8, 0.4)
SMALL_RATES = (0.3, 0.3, 0.15)
SMALL_ROWS = 4 + 9 + 49
HEAD_DIM = 64
VMEM_BYTES = 60 * 1024 * 1024
F32 = jnp.float32
BF16 = jnp.bfloat16


def mm(a, b):
    return jnp.dot(a, b, preferred_element_type=F32)


def mm_nt(a, b):
    return lax.dot_general(a, b, (((1,), (1,)), ((), ())), preferred_element_type=F32)


def mm_tn(a, b):
    return lax.dot_general(a, b, (((0,), (0,)), ((), ())), preferred_element_type=F32)


def tap_mask(head_ids):
    radius = jnp.where(head_ids < 2, 1, jnp.where(head_ids < 5, 2, 3))
    offsets = jnp.abs(jnp.arange(7, dtype=jnp.int32) - 3)
    within = (offsets[:, None] <= radius[None, :]).astype(F32)
    return (within[:, None, :] * within[None, :, :]).reshape(49, head_ids.shape[0])


def tile_radius(lane_at, head_dim):
    last = ((lane_at + 1) * LANES - 1) // head_dim
    return 1 if last < 2 else (2 if last < 5 else 3)


def normalize(values):
    center = values - jnp.mean(values, axis=-1, keepdims=True)
    spread = jnp.mean(center * center, axis=-1, keepdims=True)
    inv = lax.rsqrt(spread + 1e-06)
    return center * inv, inv


def norm_back(grad, unit, inv, gain):
    scaled = grad * gain
    first = jnp.mean(scaled, axis=-1, keepdims=True)
    second = jnp.mean(scaled * unit, axis=-1, keepdims=True)
    return inv * (scaled - first - unit * second)


def lane(at):
    return slice(at * LANES, (at + 1) * LANES)


def grid_rows(row_at):
    return slice((1 + SIDE * row_at) * IMGS, (1 + SIDE * (row_at + 1)) * IMGS)


def lane_pair(low, high):
    cells = lambda tile: tile[IMGS:].reshape(SIDE, SIDE, IMGS, LANES)
    return jnp.concatenate([cells(low), cells(high)], axis=2).astype(BF16)


def split_pair(line):
    line = line.astype(F32)
    turn = lambda part: part.reshape(SIDE * IMGS, LANES)
    return turn(line[:, :IMGS]), turn(line[:, IMGS:])


def conv_row(cells_ref, kernel_ref, pair, row_at, reach, width, flip):
    mid = width // 2
    total = [None] * SIDE
    for down in range(-reach, reach + 1):
        if not 0 <= row_at + down < SIDE:
            continue
        line = cells_ref[row_at + down]
        acc = [None] * SIDE
        for along in range(-reach, reach + 1):
            tap = (mid - down, mid - along) if flip else (mid + down, mid + along)
            weight = kernel_ref[pair, tap[0] * width + tap[1]]
            for col in range(SIDE):
                if 0 <= col + along < SIDE:
                    term = line[col + along] * weight
                    acc[col] = term if acc[col] is None else acc[col] + term
        total = [new if old is None else old + new for old, new in zip(total, acc)]
    return jnp.stack(total, axis=0)


def conv_kernel_grad(grad_ref, cells_ref, total_ref, pair, reach, width):
    mid = width // 2
    for down in range(-reach, reach + 1):
        rows = [at for at in range(SIDE) if 0 <= at + down < SIDE]
        whole_sum = [None] * (2 * reach + 1)
        for start in range(0, len(rows), 3):
            acc = [None] * (2 * reach + 1)
            for row_at in rows[start : start + 3]:
                grad_line = grad_ref[row_at]
                line = cells_ref[row_at + down]
                for along in range(-reach, reach + 1):
                    for col in range(SIDE):
                        if 0 <= col + along < SIDE:
                            term = grad_line[col] * line[col + along]
                            at = along + reach
                            acc[at] = term if acc[at] is None else acc[at] + term
            acc = [value.astype(F32) for value in acc]
            whole_sum = [new if old is None else old + new for old, new in zip(whole_sum, acc)]
        for along in range(-reach, reach + 1):
            tap = (mid + down) * width + mid + along
            value = whole_sum[along + reach]
            total_ref[tap, :, lane(2 * pair)] += value[:IMGS]
            total_ref[tap, :, lane(2 * pair + 1)] += value[IMGS:]


def fill_taps(kernel_ref, table_ref):
    for pair in range(table_ref.shape[0]):
        for tap in range(table_ref.shape[1]):
            sides = [kernel_ref[tap : tap + 1, lane(2 * pair + side)] for side in range(2)]
            sides = [jnp.broadcast_to(side, (IMGS, LANES)) for side in sides]
            table_ref[pair, tap] = jnp.concatenate(sides, axis=0).astype(BF16)


def key_softmax(key_tile, mask_tile):
    keys = key_tile.reshape(SLOT, IMGS, LANES)
    live = mask_tile.reshape(SLOT, IMGS, LANES)
    top = jnp.max(jnp.where(live > 0, keys, -1e30), axis=0, keepdims=True)
    raw = jnp.exp(jnp.where(live > 0, keys - top, -60.0)) * live
    return (raw / jnp.sum(raw, axis=0, keepdims=True)).reshape(ROWS, LANES)


def head_mask(size, head_dim):
    down = lax.broadcasted_iota(jnp.int32, (size, size), 0) // head_dim
    along = lax.broadcasted_iota(jnp.int32, (size, size), 1) // head_dim
    return jnp.where(down == along, F32(head_dim ** -0.5), F32(0.0))


def image_rows(ref, quad, image):
    rows = pl.ds(image, SLOT, stride=IMGS)
    return jnp.concatenate([ref[2 * quad, rows, :], ref[2 * quad + 1, rows, :]], axis=1)


def put_image_rows(ref, quad, image, values):
    rows = pl.ds(image, SLOT, stride=IMGS)
    ref[2 * quad, rows, :] = values[:, :LANES]
    ref[2 * quad + 1, rows, :] = values[:, LANES:]


def to_token_major(src_ref, put):
    for token in range(SLOT):
        put(slice(token * IMGS, (token + 1) * IMGS), src_ref[pl.ds(token, IMGS, stride=SLOT), :])


def to_image_major(src_ref, put):
    for image in range(IMGS):
        put(slice(image * SLOT, (image + 1) * SLOT), src_ref[pl.ds(image, SLOT, stride=IMGS), :])


def attend_forward(*refs, first):
    if first:
        tokens_ref, refs = refs[0], refs[1:]
        (mask_ref, w_ref, norm_ref, cpe_in, crpe_in, x_ref, unit_ref, inv_ref, packed_ref,
         rel_ref, mixed_ref, att_ref, x_cells, v_cells, cpe_ref, crpe_ref, conv_ref,
         q_s, k_s, v_s, f_s, c_s) = refs
    else:
        (x_ref, mask_ref, w_ref, norm_ref, cpe_in, crpe_in, unit_ref, inv_ref, packed_ref,
         rel_ref, mixed_ref, att_ref, x_cells, v_cells, cpe_ref, crpe_ref, conv_ref,
         q_s, k_s, v_s, f_s, c_s) = refs
    channels = x_ref.shape[1]
    tiles = channels // LANES
    head_dim = channels // HEADS
    half = channels // 2

    @pl.when(pl.program_id(0) == 0)
    def _():
        fill_taps(cpe_in, cpe_ref)
        fill_taps(crpe_in, crpe_ref)

    if first:
        for at in range(tiles):
            cols = lane(at)
            f_s[at] = tokens_ref[:, cols].astype(F32)

            def put(rows, values, cols=cols):
                x_ref[rows, cols] = values

            to_token_major(f_s.at[at], put)
    for pair in range(tiles // 2):
        both = (lane(2 * pair), lane(2 * pair + 1))
        mask = mask_ref[...]
        x_cells[...] = lane_pair(*[x_ref[:, cols] * mask for cols in both])
        for cols in both:
            conv_ref[:IMGS, cols] = x_ref[:IMGS, cols]
        for row_at in range(SIDE):
            rows = grid_rows(row_at)
            out = split_pair(conv_row(x_cells, cpe_ref, pair, row_at, 1, 3, False))
            for cols, value in zip(both, out):
                conv_ref[rows, cols] = x_ref[rows, cols] + value * mask_ref[rows, :]
    unit, inv = normalize(conv_ref[...])
    unit_ref[...] = unit.astype(BF16)
    inv_ref[...] = inv
    normed = (unit * norm_ref[0:1, :] + norm_ref[1:2, :]).astype(BF16)
    for side in range(2):
        for third, keep in enumerate((q_s, k_s, v_s)):
            cols = slice(third * half, (third + 1) * half)
            part = mm(normed, w_ref[side, :, cols]).astype(BF16)
            if third != 1:
                start = (3 * side + third) * half
                packed_ref[:, start : start + half] = part
            part = part.astype(F32)
            for at in range(tiles // 2):
                keep[side * (tiles // 2) + at] = part[:, lane(at)]
    for at in range(tiles):
        weights = key_softmax(k_s[at], mask_ref[...])
        k_s[at] = weights
        start = (3 * (at // 2) + 1) * half + (at % 2) * LANES
        packed_ref[:, start : start + LANES] = weights.astype(BF16)
    block = head_mask(2 * LANES, head_dim)

    def one_image(image, carry):
        for quad in range(tiles // 2):
            keys = image_rows(k_s, quad, image).astype(BF16)
            values = image_rows(v_s, quad, image).astype(BF16)
            query = image_rows(q_s, quad, image).astype(BF16)
            context = (mm_tn(keys, values) * block).astype(BF16)
            put_image_rows(f_s, quad, image, mm(query, context))
        return carry

    lax.fori_loop(0, IMGS, one_image, 0, unroll=True)
    c_s[:, :IMGS, :] = jnp.zeros((2, IMGS, LANES), F32)
    for pair in range(tiles // 2):
        mask = mask_ref[...]
        v_cells[...] = lane_pair(v_s[2 * pair] * mask, v_s[2 * pair + 1] * mask)
        reach = tile_radius(2 * pair + 1, head_dim)
        for row_at in range(SIDE):
            rows = grid_rows(row_at)
            out = split_pair(conv_row(v_cells, crpe_ref, pair, row_at, reach, 7, False))
            for half_at, value in enumerate(out):
                c_s[half_at, rows, :] = value * mask_ref[rows, :]
        for half_at in range(2):
            at = 2 * pair + half_at
            rel = c_s[half_at]
            rel_ref[:, lane(at)] = rel.astype(BF16)
            mixed_ref[:, lane(at)] = (f_s[at] + q_s[at] * rel).astype(BF16)
    out = conv_ref[...]
    for side in range(2):
        cols = slice(side * half, (side + 1) * half)
        out = out + mm_nt(mixed_ref[:, cols], w_ref[side, :, 3 * half :])
    att_ref[...] = out


def gelu_parts(hidden):
    number = lambda value: jnp.asarray(value, BF16)
    values = hidden.astype(BF16)
    t = pl.reciprocal(
        number(1.0) + number(0.3275911 * 0.7071067811865476) * jnp.abs(values), approx=True
    )
    bell = jnp.exp2(number(-0.5 * 1.4426950408889634) * (values * values))
    poly = number(0.5 * 1.061405429)
    for coef in (-1.453152027, 1.421413741, -0.284496736, 0.254829592):
        poly = poly * t + number(0.5 * coef)
    tail = poly * t * bell
    phi = jnp.where(values >= 0, number(1.0) - tail, tail)
    return values * phi, phi + (values * number(0.3989422804014327)) * bell


def feed_forward(
    att_ref, up_down_ref, norm_ref, out_ref, act_ref, slope_ref, unit_ref, inv_ref, *scratch, chunk
):
    blks, _, both = up_down_ref.shape
    width = both // 2
    chunk = min(chunk, width)
    att = att_ref[...]
    unit, inv = normalize(att)
    unit_ref[...] = unit.astype(BF16)
    inv_ref[...] = inv
    normed = (unit * norm_ref[2:3, :] + norm_ref[3:4, :]).astype(BF16)
    total = att
    for blk in range(blks):
        for at in range(0, width, chunk):
            hidden = mm(normed, up_down_ref[blk, :, at : at + chunk])
            active, slope = gelu_parts(hidden)
            cols = slice(blk * width + at, blk * width + at + chunk)
            act_ref[:, cols] = active
            slope_ref[:, cols] = slope
            total = total + mm_nt(active, up_down_ref[blk, :, width + at : width + at + chunk])
    if not scratch:
        out_ref[...] = total
        return
    turn_s, whole_s = scratch
    for at in range(att.shape[1] // LANES):
        cols = lane(at)
        turn_s[...] = total[:, cols]

        def put(rows, values, cols=cols):
            whole_s[rows, cols] = values

        to_image_major(turn_s, put)
    out_ref[...] = whole_s[...].astype(BF16)


def feed_back(*refs, first, chunk):
    if first:
        (mask_ref, cot_ref, att_ref, up_down_ref, norm_ref, out_ref,
         gatt_ref, gweight_ref, gnorm_ref, total_s, act_ref, slope_ref, unit_ref, inv_ref,
         turn_s, whole_s) = refs
        feed_forward(
            att_ref, up_down_ref, norm_ref, out_ref, act_ref, slope_ref, unit_ref, inv_ref,
            turn_s, whole_s, chunk=chunk,
        )
    else:
        (up_ref, unit_ref, inv_ref, act_ref, slope_ref, up_down_ref, norm_ref,
         gatt_ref, gweight_ref, gnorm_ref, total_s) = refs
    step, steps = pl.program_id(0), pl.num_programs(0)
    blks, _, both = up_down_ref.shape
    width = both // 2
    chunk = min(chunk, width)

    @pl.when(step == 0)
    def _():
        total_s[...] = jnp.zeros_like(total_s)
        gnorm_ref[...] = jnp.zeros_like(gnorm_ref)

    if first:
        for at in range(cot_ref.shape[1] // LANES):
            cols = lane(at)
            turn_s[...] = cot_ref[:, cols]

            def put(rows, values, cols=cols):
                whole_s[rows, cols] = values * mask_ref[rows, :]

            to_token_major(turn_s, put)
        upstream = whole_s[...]
    else:
        upstream = up_ref[...]
    unit, inv = unit_ref[...].astype(F32), inv_ref[...]
    gain = norm_ref[2:3, :]
    normed = (unit * gain + norm_ref[3:4, :]).astype(BF16)
    down_in = upstream.astype(BF16)
    grad_mid = None
    for blk in range(blks):
        for at in range(0, width, chunk):
            cols = slice(blk * width + at, blk * width + at + chunk)
            ups = slice(at, at + chunk)
            downs = slice(width + at, width + at + chunk)
            grad_active = mm(down_in, up_down_ref[blk, :, downs])
            grad_hidden = (grad_active * slope_ref[:, cols].astype(F32)).astype(BF16)
            total_s[blk, :, ups] += mm_tn(normed, grad_hidden)
            total_s[blk, :, downs] += mm_tn(down_in, act_ref[:, cols])
            part = mm_nt(grad_hidden, up_down_ref[blk, :, ups])
            grad_mid = part if grad_mid is None else grad_mid + part
    gatt_ref[...] = upstream + norm_back(grad_mid, unit, inv, gain)
    gnorm_ref[0:1, :] += jnp.sum(grad_mid * unit, axis=0, keepdims=True)
    gnorm_ref[1:2, :] += jnp.sum(grad_mid, axis=0, keepdims=True)

    @pl.when(step == steps - 1)
    def _():
        gweight_ref[...] = total_s[...].astype(BF16)


def attend_back(
    gatt_ref, x_ref, unit_ref, inv_ref, packed_ref, rel_ref, mixed_ref, mask_ref,
    w_ref, norm_ref, cpe_in, crpe_in, gmid_ref, taps_ref,
    out_ref, gw_ref, small_ref, gnorm_ref, gcpe_ref, gcrpe_ref,
    w_s, x_cells, g_cells, v_cells, c_cells, cpe_ref, crpe_ref, q_s, k_s, v_s, f_s, dq_s, dk_s, dv_s, c_s, gp_s,
    *scratch,
):
    channels = x_ref.shape[1]
    tiles = channels // LANES
    head_dim = channels // HEADS
    half = channels // 2
    step, steps = pl.program_id(0), pl.num_programs(0)
    up_ref = scratch[0] if scratch else out_ref

    @pl.when(step == 0)
    def _():
        fill_taps(cpe_in, cpe_ref)
        fill_taps(crpe_in, crpe_ref)
        for ref in (w_s, gnorm_ref, gcpe_ref, gcrpe_ref):
            ref[...] = jnp.zeros_like(ref)

    att_in = gatt_ref[...].astype(BF16)
    att_t = att_in.T
    for side in range(2):
        cols = slice(side * half, (side + 1) * half)
        w_s[side, :, 3 * half :] += mm(att_t, mixed_ref[:, cols])
        grad_mixed = mm(att_in, w_ref[side, :, 3 * half :])
        for at in range(tiles // 2):
            f_s[side * (tiles // 2) + at] = grad_mixed[:, lane(at)]
        for third, keep in enumerate((q_s, k_s, v_s)):
            for at in range(tiles // 2):
                start = (3 * side + third) * half + at * LANES
                keep[side * (tiles // 2) + at] = packed_ref[:, start : start + LANES].astype(F32)
    block = head_mask(2 * LANES, head_dim)

    def one_image(image, carry):
        for quad in range(tiles // 2):
            keys = image_rows(k_s, quad, image).astype(BF16)
            values = image_rows(v_s, quad, image).astype(BF16)
            query = image_rows(q_s, quad, image).astype(BF16)
            grads = image_rows(f_s, quad, image).astype(BF16)
            context = (mm_tn(keys, values) * block).astype(BF16)
            grad_context = (mm_tn(query, grads) * block).astype(BF16)
            put_image_rows(dq_s, quad, image, mm_nt(grads, context))
            put_image_rows(dk_s, quad, image, mm_nt(values, grad_context))
            put_image_rows(dv_s, quad, image, mm(keys, grad_context))
        return carry

    lax.fori_loop(0, IMGS, one_image, 0, unroll=True)
    for pair in range(tiles // 2):
        mask = mask_ref[...]
        place = lambda at, third: slice(
            (3 * pair + third) * half + at * LANES, (3 * pair + third) * half + (at + 1) * LANES
        )
        for half_at in range(2):
            at = 2 * pair + half_at
            weights = k_s[at]
            share = weights * dk_s[at]
            total = jnp.sum(share.reshape(SLOT, IMGS, LANES), axis=0, keepdims=True)
            back = share.reshape(SLOT, IMGS, LANES) - weights.reshape(SLOT, IMGS, LANES) * total
            gp_s[:, place(half_at, 1)] = back.reshape(ROWS, LANES).astype(BF16)
            rel = rel_ref[:, lane(at)].astype(F32)
            gp_s[:, place(half_at, 0)] = (dq_s[at] + f_s[at] * rel).astype(BF16)
        reach = tile_radius(2 * pair + 1, head_dim)
        v_cells[...] = lane_pair(v_s[2 * pair] * mask, v_s[2 * pair + 1] * mask)
        c_cells[...] = lane_pair(
            *[f_s[at] * q_s[at] * mask for at in (2 * pair, 2 * pair + 1)]
        )
        for row_at in range(SIDE):
            rows = grid_rows(row_at)
            out = split_pair(conv_row(c_cells, crpe_ref, pair, row_at, reach, 7, True))
            for half_at, value in enumerate(out):
                dv_s[2 * pair + half_at, rows, :] += value * mask_ref[rows, :]
        conv_kernel_grad(c_cells, v_cells, gcrpe_ref, pair, reach, 7)
        for half_at in range(2):
            gp_s[:, place(half_at, 2)] = dv_s[2 * pair + half_at].astype(BF16)
    unit, inv = unit_ref[...].astype(F32), inv_ref[...]
    gain = norm_ref[0:1, :]
    normed_t = (unit * gain + norm_ref[1:2, :]).astype(BF16).T
    grad_rows = None
    for side in range(2):
        part_in = gp_s[:, side * 3 * half : (side + 1) * 3 * half]
        w_s[side, :, : 3 * half] += mm(normed_t, part_in)
        part = mm_nt(part_in, w_ref[side, :, : 3 * half])
        grad_rows = part if grad_rows is None else grad_rows + part
    gnorm_ref[0:1, :] += jnp.sum(grad_rows * unit, axis=0, keepdims=True)
    gnorm_ref[1:2, :] += jnp.sum(grad_rows, axis=0, keepdims=True)
    up_ref[...] = gatt_ref[...] + norm_back(grad_rows, unit, inv, gain)
    for pair in range(tiles // 2):
        both = (lane(2 * pair), lane(2 * pair + 1))
        mask = mask_ref[...]
        x_cells[...] = lane_pair(*[x_ref[:, cols] * mask for cols in both])
        g_cells[...] = lane_pair(*[up_ref[:, cols] * mask for cols in both])
        for row_at in range(SIDE):
            rows = grid_rows(row_at)
            out = split_pair(conv_row(g_cells, cpe_ref, pair, row_at, 1, 3, True))
            for cols, value in zip(both, out):
                up_ref[rows, cols] += value * mask_ref[rows, :]
        conv_kernel_grad(g_cells, x_cells, gcpe_ref, pair, 1, 3)
    for at in range(tiles if scratch else 0):
        cols = lane(at)
        c_s[...] = up_ref[:, cols]

        def put(rows, values, cols=cols):
            out_ref[rows, cols] = values

        to_image_major(c_s, put)

    @pl.when(step == steps - 1)
    def _():
        gw_ref[...] = w_s[...].astype(BF16)
        rows = [gnorm_ref[...], gmid_ref[...], jnp.sum(gcpe_ref[...], axis=1)]
        rows.append(jnp.sum(gcrpe_ref[...], axis=1) * taps_ref[...])
        count = sum(part.shape[0] for part in rows)
        rows.append(jnp.zeros((LANES - count, channels), F32))
        small_ref[...] = jnp.concatenate(rows, axis=0).T.astype(BF16)


def dot3(a, b, dims):
    a_hi, b_hi = a.astype(BF16), b.astype(BF16)
    a_lo = (a - a_hi.astype(F32)).astype(BF16)
    b_lo = (b - b_hi.astype(F32)).astype(BF16)
    one = lambda u, v: lax.dot_general(u, v, (dims, ((), ())), preferred_element_type=F32)
    return one(a_hi, b_hi) + (one(a_hi, b_lo) + one(a_lo, b_hi))


def schulz_turns(blocks):
    first, second, third = SCHULZ_COEFFS
    current = []
    for value in blocks:
        level = jnp.sum(jnp.sum(value * value, axis=0, keepdims=True), axis=1, keepdims=True)
        current.append(value / (jnp.sqrt(level) + 1e-07))
    for _ in range(5):
        grams = [dot3(value, value, ((0,), (0,))) for value in current]
        polys = [second * gram + third * dot3(gram, gram, ((1,), (0,))) for gram in grams]
        current = [
            first * value + dot3(value, poly, ((1,), (0,))) for value, poly in zip(current, polys)
        ]
    return current


def schulz(fresh_ref, out_ref, width):
    parts = (slice(0, width), slice(width, 2 * width))
    for cols, value in zip(parts, schulz_turns([fresh_ref[0, :, c].astype(F32) for c in parts])):
        out_ref[0, :, cols] = value.astype(BF16)


def finish_kernel(
    big_ref, little_ref, big_out, little_out, small_ref,
    big_got, little_got, big_turned, little_turned, big_back, little_back, sems,
):
    count, rows, width = big_ref.shape
    me, blk = lax.axis_index("tok"), lax.axis_index("blk")
    targets = [None] + [lax.rem(me + d, count) for d in range(1, count)]
    sources = [None] + [lax.rem(me + count - d, count) for d in range(1, count)]
    greet([(targets[d], blk) for d in range(1, count)])
    copies = []

    def send(src, dst, kind):
        for d in range(1, count):
            copy = pltpu.make_async_remote_copy(
                src_ref=src.at[targets[d]], dst_ref=dst.at[me],
                send_sem=sems.at[2 * kind, d], recv_sem=sems.at[2 * kind + 1, d],
                device_id=(targets[d], blk), device_id_type=pl.DeviceIdType.MESH,
            )
            copy.start()
            copies.append(copy)
        dst[me] = src[me]

    def arrive(dst, kind):
        for d in range(1, count):
            here = dst.at[sources[d]]
            pltpu.make_async_remote_copy(
                src_ref=here, dst_ref=here,
                send_sem=sems.at[2 * kind, d], recv_sem=sems.at[2 * kind + 1, d],
                device_id=(targets[d], blk), device_id_type=pl.DeviceIdType.MESH,
            ).wait_recv()

    def turn(got, turned):
        fresh = got[:, :, :width].reshape(count * rows, width)
        value = schulz_turns([fresh.astype(F32)])[0]
        turned[...] = value.astype(BF16).reshape(count, rows, width)

    send(big_ref, big_got, 0)
    send(little_ref, little_got, 1)
    arrive(big_got, 0)
    turn(big_got, big_turned)
    send(big_turned, big_back, 2)
    arrive(little_got, 1)
    turn(little_got, little_turned)
    send(little_turned, little_back, 3)
    small_ref[...] = little_got[:, :, width:].reshape(count * rows, little_got.shape[2] - width)
    arrive(big_back, 2)
    big_out[...] = big_back[...]
    arrive(little_back, 3)
    little_out[...] = little_back[...]
    for copy in copies:
        copy.wait_send()


def finish(big, little, collective_id):
    count, rows, width = big.shape
    vmem = pl.BlockSpec(memory_space=pltpu.VMEM)
    block = pltpu.VMEM(big.shape, BF16)
    small = (count * rows, little.shape[2] - width)
    return pl.pallas_call(
        finish_kernel,
        in_specs=[vmem, vmem],
        out_specs=[vmem, vmem, vmem],
        out_shape=[jax.ShapeDtypeStruct(shape, BF16) for shape in (big.shape, big.shape, small)],
        scratch_shapes=[
            block, pltpu.VMEM(little.shape, BF16), block, block, block, block,
            pltpu.SemaphoreType.DMA((8, count)),
        ],
        compiler_params=params_for(collective_id=collective_id, has_side_effects=True),
        cost_estimate=cost(25),
        name="finish",
    )(big, little)


def pack_kernel(qkv_ref, proj_ref, up_ref, down_ref, *outs):
    heads = qkv_ref.shape[2] // (3 * HEAD_DIM)
    for layer, out in enumerate(outs):
        wide = up_ref.shape[2]
        out[:, :wide] = up_ref[layer].astype(BF16)
        out[:, wide : 2 * wide] = down_ref[layer].astype(BF16)
        qkv = qkv_ref[layer]
        parts = [
            qkv[:, (3 * head + third) * HEAD_DIM : (3 * head + third + 1) * HEAD_DIM]
            for third in range(3)
            for head in range(heads)
        ]
        start = 2 * wide + qkv.shape[1]
        out[:, 2 * wide : start] = jnp.concatenate(parts, axis=1).astype(BF16)
        out[:, start:] = proj_ref[layer].astype(BF16)


def pack(mats):
    layers, rows = mats[0].shape[:2]
    cols = sum(mat.shape[2] for mat in mats)
    return pl.pallas_call(
        pack_kernel,
        out_shape=[jax.ShapeDtypeStruct((rows, cols), BF16)] * layers,
        compiler_params=params_for(),
        name="pack",
    )(*mats)


def prepare_kernel(total_ref, early_ref, *refs):
    moments, fresh_refs, (big_ref, little_ref) = refs[:4], refs[4:8], refs[8:]
    qkv_m, proj_m, up_m, down_m = moments
    layers, rows, wide = up_m.shape
    span = qkv_m.shape[2]
    heads = span // (3 * HEAD_DIM)
    half = heads * HEAD_DIM
    width = big_ref.shape[2]
    groups = wide // width
    cut = 4 * half + LANES
    little_ref[...] = jnp.zeros_like(little_ref)
    small = []
    for layer in range(layers):
        at = cut if layer == 0 else 0
        sums = total_ref[:, at : at + cut]
        feed = total_ref[:, 2 * cut :] if layer == 0 else early_ref[...].astype(F32)
        small.append(sums[:, 4 * half : 4 * half + SMALL_ROWS])
        parts = [
            sums[:, third * half + head * HEAD_DIM : third * half + (head + 1) * HEAD_DIM]
            for head in range(heads)
            for third in range(3)
        ]
        qkv = 0.5 * qkv_m[layer] + jnp.concatenate(parts, axis=1)
        fresh_refs[0][layer] = qkv
        proj = 0.5 * proj_m[layer] + sums[:, 3 * half : 4 * half]
        fresh_refs[1][layer] = proj
        up = 0.5 * up_m[layer] + feed[:, :wide]
        fresh_refs[2][layer] = up
        down = 0.5 * down_m[layer] + feed[:, wide:]
        fresh_refs[3][layer] = down
        unit = layer * 2 * groups
        for group in range(groups):
            cols = slice(group * width, (group + 1) * width)
            big_ref[unit + group] = up[:, cols].astype(BF16)
            big_ref[unit + groups + group] = down[:, cols].astype(BF16)
        unit = layer * 2 * heads
        for head in range(heads):
            block = qkv[:, 3 * head * HEAD_DIM : 3 * (head + 1) * HEAD_DIM]
            little_ref[unit + head, :, : 3 * HEAD_DIM] = block.astype(BF16)
            block = proj[:, head * HEAD_DIM : (head + 1) * HEAD_DIM]
            little_ref[unit + heads + head, :, :HEAD_DIM] = block.astype(BF16)
    small.append(jnp.zeros((rows, LANES - layers * SMALL_ROWS), F32))
    small = jnp.concatenate(small, axis=1).astype(BF16)
    for unit in range(little_ref.shape[0]):
        little_ref[unit, :, width:] = small


def prepare(total, early, moments, units, width):
    rows = moments[2].shape[1]
    shapes = [jax.ShapeDtypeStruct(moment.shape, F32) for moment in moments]
    shapes.append(jax.ShapeDtypeStruct((units, rows, width), BF16))
    shapes.append(jax.ShapeDtypeStruct((units, rows, width + LANES), BF16))
    return pl.pallas_call(
        prepare_kernel,
        out_shape=shapes,
        compiler_params=params_for(),
        name="prepare",
    )(total, early, *moments)


def small_step(param, moment, grad, rate, level):
    fresh = 0.5 * moment + grad
    return fresh, param - rate * fresh / (jnp.sqrt(level(fresh * fresh)) + 1e-06)


def update_kernel(big_ref, little_ref, small_ref, *refs, scales):
    mats, params, moments = refs[:4], refs[4:7], refs[7:10]
    outs = refs[10:]
    layers, rows, wide = mats[2].shape
    width = big_ref.shape[2]
    groups = wide // width
    heads = mats[0].shape[2] // (3 * HEAD_DIM)
    small = small_ref[...].astype(F32).T
    for layer in range(layers):
        unit = layer * 2 * heads
        join = lambda blocks: jnp.concatenate([block.astype(F32) for block in blocks], axis=1)
        qkv = join([little_ref[unit + head, :, : 3 * HEAD_DIM] for head in range(heads)])
        proj = join([little_ref[unit + heads + head, :, :HEAD_DIM] for head in range(heads)])
        unit = layer * 2 * groups
        up = join([big_ref[unit + group] for group in range(groups)])
        down = join([big_ref[unit + groups + group] for group in range(groups)])
        for kind, turned in enumerate((qkv, proj, up, down)):
            new = mats[kind][layer] - scales[kind] * turned
            outs[2 * kind][layer] = new
            outs[2 * kind + 1][layer] = new.astype(BF16)
        grads = small[layer * SMALL_ROWS : (layer + 1) * SMALL_ROWS]
        row_mean = lambda square: jnp.mean(square, axis=1, keepdims=True)
        all_mean = lambda square: jnp.mean(row_mean(square), axis=0, keepdims=True)

        def head_mean(square):
            column = jnp.mean(square, axis=0, keepdims=True)
            spans = [
                jnp.broadcast_to(
                    row_mean(column[:, head * HEAD_DIM : (head + 1) * HEAD_DIM]), (1, HEAD_DIM)
                )
                for head in range(HEADS)
            ]
            return jnp.concatenate(spans, axis=1)

        start = 0
        for kind, level in enumerate((row_mean, all_mean, head_mean)):
            place = (layer,) if kind == 0 else (slice(None), layer)
            count = params[kind].shape[1 if kind == 0 else 0]
            fresh, new = small_step(
                params[kind][place], moments[kind][place], grads[start : start + count],
                SMALL_RATES[kind], level,
            )
            outs[8 + 2 * kind][place] = fresh
            outs[9 + 2 * kind][place] = new
            start += count


def update(big, little, small, mats, params, moments, scales):
    shapes = []
    for mat in mats:
        shapes += [jax.ShapeDtypeStruct(mat.shape, F32), jax.ShapeDtypeStruct(mat.shape, BF16)]
    for param in params:
        shapes += [jax.ShapeDtypeStruct(param.shape, F32)] * 2
    return pl.pallas_call(
        functools.partial(update_kernel, scales=scales),
        out_shape=shapes,
        compiler_params=params_for(),
        name="update",
    )(big, little, small, *mats, *params, *moments)


def params_for(**more):
    return pltpu.CompilerParams(vmem_limit_bytes=VMEM_BYTES, **more)


def block_of(cols):
    return pl.BlockSpec((ROWS, cols), lambda g: (g, 0))


def whole(array):
    shape = array.shape
    return pl.BlockSpec(shape, lambda g: (0,) * len(shape), pipeline_mode=pl.Buffered(1))


def some_columns(weights):
    array, width, at = weights
    shape = array.shape[:2] + (width,)
    return pl.BlockSpec(shape, lambda g: (0, 0, at), pipeline_mode=pl.Buffered(1))


def whole_out(shape):
    return pl.BlockSpec(shape, lambda g: (0,) * len(shape))


def tap_tables(channels):
    return [pltpu.VMEM((channels // (2 * LANES), taps, 2 * IMGS, LANES), BF16) for taps in (9, 49)]


def cost(us):
    return pl.CostEstimate(flops=int(us * 1e9), bytes_accessed=int(us * 1e5), transcendentals=0)


def run_attend_forward(x, mask, weights, norm, cpe, crpe, first):
    count, channels = x.shape
    tiles = channels // LANES
    flat = pltpu.VMEM((tiles, ROWS, LANES), F32)
    cells = pltpu.VMEM((SIDE, SIDE, 2 * IMGS, LANES), BF16)
    out = lambda cols, kind: jax.ShapeDtypeStruct((count, cols), kind)
    outs = [out(channels, BF16), out(1, F32), out(3 * channels, BF16)]
    outs += [out(channels, BF16)] * 2
    outs = [out(channels, F32)] * first + outs + [out(channels, F32)]
    return pl.pallas_call(
        functools.partial(attend_forward, first=first),
        grid=(count // ROWS,),
        in_specs=[block_of(channels), block_of(LANES)]
        + [some_columns(weights)]
        + [whole(a) for a in (norm, cpe, crpe)],
        out_specs=[block_of(array.shape[1]) for array in outs],
        out_shape=outs,
        scratch_shapes=[
            cells, cells, *tap_tables(channels), pltpu.VMEM((ROWS, channels), F32),
            flat, flat, flat, flat,
            pltpu.VMEM((2, ROWS, LANES), F32),
        ],
        compiler_params=params_for(),
        cost_estimate=cost(50),
        name="attend_forward",
    )(x, mask, weights[0], norm, cpe, crpe)


def run_feed_forward(att, up_down, norm, chunk=512):
    count, channels = att.shape
    hidden = up_down[0].shape[0] * up_down[1] // 2
    return pl.pallas_call(
        functools.partial(feed_forward, chunk=chunk),
        grid=(count // ROWS,),
        in_specs=[block_of(channels), some_columns(up_down), whole(norm)],
        out_specs=[block_of(channels), block_of(hidden), block_of(hidden)]
        + [block_of(channels), block_of(1)],
        out_shape=[
            jax.ShapeDtypeStruct((count, channels), F32),
            jax.ShapeDtypeStruct((count, hidden), BF16),
            jax.ShapeDtypeStruct((count, hidden), BF16),
            jax.ShapeDtypeStruct((count, channels), BF16),
            jax.ShapeDtypeStruct((count, 1), F32),
        ],
        compiler_params=params_for(),
        cost_estimate=cost(24),
        name="feed_forward",
    )(att, up_down[0], norm)


def run_feed_back(inputs, up_down, norm, first, chunk=512):
    count, channels = inputs[2 if first else 0].shape
    hidden = up_down[0].shape[0] * up_down[1] // 2
    shape = up_down[0].shape[:2] + (up_down[1],)
    more = [
        pltpu.VMEM((ROWS, hidden), BF16), pltpu.VMEM((ROWS, hidden), BF16),
        pltpu.VMEM((ROWS, channels), BF16), pltpu.VMEM((ROWS, 1), F32),
        pltpu.VMEM((ROWS, LANES), F32), pltpu.VMEM((ROWS, channels), F32),
    ]
    return pl.pallas_call(
        functools.partial(feed_back, first=first, chunk=chunk),
        grid=(count // ROWS,),
        in_specs=[block_of(array.shape[1]) for array in inputs]
        + [some_columns(up_down), whole(norm)],
        out_specs=[block_of(channels)] * first
        + [block_of(channels), whole_out(shape), whole_out((2, channels))],
        out_shape=[jax.ShapeDtypeStruct((count, channels), BF16)] * first
        + [
            jax.ShapeDtypeStruct((count, channels), F32),
            jax.ShapeDtypeStruct(shape, BF16),
            jax.ShapeDtypeStruct((2, channels), F32),
        ],
        scratch_shapes=[pltpu.VMEM(shape, F32)] + more * first,
        compiler_params=params_for(),
        cost_estimate=cost(50 if first else 37),
        name="feed_back",
    )(*inputs, up_down[0], norm)


def run_attend_back(
    gatt, x, unit, inv, packed, rel, mixed, mask, weights, norm, cpe, crpe, gmid, taps, last
):
    count, channels = x.shape
    tiles = channels // LANES
    flat = pltpu.VMEM((tiles, ROWS, LANES), F32)
    cells = pltpu.VMEM((SIDE, SIDE, 2 * IMGS, LANES), BF16)
    small = [(2, channels), (9, IMGS, channels), (49, IMGS, channels)]
    shape = weights[0].shape[:2] + (weights[1],)
    return pl.pallas_call(
        attend_back,
        grid=(count // ROWS,),
        in_specs=[block_of(channels)] * 3
        + [block_of(1), block_of(3 * channels), block_of(channels), block_of(channels)]
        + [block_of(LANES)]
        + [some_columns(weights)]
        + [whole(a) for a in (norm, cpe, crpe, gmid, taps)],
        out_specs=[block_of(channels), whole_out(shape), whole_out((channels, LANES))],
        out_shape=[
            jax.ShapeDtypeStruct((count, channels), F32),
            jax.ShapeDtypeStruct(shape, BF16),
            jax.ShapeDtypeStruct((channels, LANES), BF16),
        ],
        scratch_shapes=[pltpu.VMEM(each, F32) for each in small]
        + [
            pltpu.VMEM(shape, F32),
            cells, cells, cells, cells, *tap_tables(channels),
            flat, flat, flat, flat, flat, flat, flat,
            pltpu.VMEM((ROWS, LANES), F32),
            pltpu.VMEM((ROWS, 3 * channels), BF16),
        ]
        + [pltpu.VMEM((ROWS, channels), F32)] * last,
        compiler_params=params_for(),
        cost_estimate=cost(65),
        name="attend_back",
    )(gatt, x, unit, inv, packed, rel, mixed, mask, weights[0], norm, cpe, crpe, gmid, taps)


def where_am_i():
    tok, blk = lax.axis_index("tok"), lax.axis_index("blk")
    core, x, z = lax.rem(tok, 2), lax.rem(tok // 2, 2), tok // 4
    return blk, z, x, core


def device_at(y, z, x, core):
    return (z * 4 + x * 2 + core, y)


def neighbours(y, z, x, core):
    fx, fy = 1 - core, core
    flip = lambda value, by: value + by - 2 * value * by
    first = (flip(y, fy), flip(x, fx))
    second = (flip(y, fx), flip(x, fy))
    cross = (1 - y, 1 - x)
    return first, second, cross


def greet(targets):
    barrier = pltpu.get_barrier_semaphore()
    for target in targets:
        pl.semaphore_signal(barrier, inc=1, device_id=target, device_id_type=pl.DeviceIdType.MESH)
    pl.semaphore_wait(barrier, len(targets))


def spread_kernel(shard_ref, out_ref, send_sem, recv_sem, own_sem):
    y, z, x, core = where_am_i()
    first, second, cross = neighbours(y, z, x, core)
    line = [lax.rem(z + d, 4) for d in range(4)]
    back = [lax.rem(z + 4 - d, 4) for d in range(4)]
    to_first = device_at(first[0], z, first[1], core)
    to_second = device_at(second[0], z, second[1], core)
    to_core = device_at(y, z, x, 1 - core)
    greet([to_first, to_second, to_core] + [device_at(y, line[d], x, core) for d in (1, 2, 3)])
    slot = lambda at, layer, side: at[0] * 16 + layer * 4 + at[1] * 2 + side
    own = pltpu.make_async_copy(shard_ref, out_ref.at[slot((y, x), z, core)], own_sem)
    own.start()
    copies = []

    def send(src, at, layer, side, target, number):
        copy = pltpu.make_async_remote_copy(
            src_ref=src, dst_ref=out_ref.at[slot(at, layer, side)],
            send_sem=send_sem.at[number], recv_sem=recv_sem.at[number],
            device_id=target, device_id_type=pl.DeviceIdType.MESH,
        )
        copy.start()
        copies.append(copy)

    def arrive(at, layer, side, number):
        here = out_ref.at[slot(at, layer, side)]
        pltpu.make_async_remote_copy(
            src_ref=here, dst_ref=here, send_sem=send_sem.at[number], recv_sem=recv_sem.at[number],
            device_id=to_core, device_id_type=pl.DeviceIdType.MESH,
        ).wait_recv()

    me = (y, x)
    for d in (1, 2, 3):
        send(shard_ref, me, z, core, device_at(y, line[d], x, core), d - 1)
    for d in range(4):
        layer = back[d]
        if d:
            arrive(me, layer, core, d - 1)
        src = out_ref.at[slot(me, layer, core)] if d else shard_ref
        send(src, me, layer, core, to_first, 3 + d)
        send(src, me, layer, core, to_second, 7 + d)
        send(src, me, layer, core, to_core, 15 + d)
    for d in range(4):
        arrive(first, back[d], core, 3 + d)
        src = out_ref.at[slot(first, back[d], core)]
        send(src, first, back[d], core, to_second, 11 + d)
        send(src, first, back[d], core, to_core, 19 + d)
    for d in range(4):
        arrive(second, back[d], core, 7 + d)
        send(out_ref.at[slot(second, back[d], core)], second, back[d], core, to_core, 23 + d)
    for d in range(4):
        arrive(cross, back[d], core, 11 + d)
        send(out_ref.at[slot(cross, back[d], core)], cross, back[d], core, to_core, 27 + d)
    for d in range(4):
        arrive(me, back[d], 1 - core, 15 + d)
        arrive(second, back[d], 1 - core, 19 + d)
        arrive(first, back[d], 1 - core, 23 + d)
        arrive(cross, back[d], 1 - core, 27 + d)
    own.wait()
    for copy in copies:
        copy.wait_send()


def spread(shard, collective_id):
    return pl.pallas_call(
        spread_kernel,
        in_specs=[pl.BlockSpec(memory_space=pl.ANY)],
        out_specs=pl.BlockSpec(memory_space=pl.ANY),
        out_shape=jax.ShapeDtypeStruct((32,) + shard.shape, shard.dtype),
        scratch_shapes=[
            pltpu.SemaphoreType.DMA((31,)), pltpu.SemaphoreType.DMA((31,)), pltpu.SemaphoreType.DMA,
        ],
        compiler_params=pltpu.CompilerParams(
            collective_id=collective_id, has_side_effects=True, vmem_limit_bytes=VMEM_BYTES
        ),
        name="spread",
    )(shard)


def collect_kernel(*refs, widths):
    parts = len(widths)
    grads, out_ref = refs[:parts], refs[parts]
    own_s, chip_s, second_s, first_s, line_s, send_sem, recv_sem, load_sem = refs[parts + 1 :]
    y, z, x, core = where_am_i()
    first, second, cross = neighbours(y, z, x, core)
    line = [lax.rem(z + d, 4) for d in range(4)]
    back = [lax.rem(z + 4 - d, 4) for d in range(4)]
    to_first = device_at(first[0], z, first[1], core)
    to_second = device_at(second[0], z, second[1], core)
    to_core = device_at(y, z, x, 1 - core)
    greet([to_first, to_second, to_core] + [device_at(y, line[d], x, core) for d in (1, 2, 3)])
    mine = lambda at, layer, side: own_s.at[at[0] * 8 + layer * 2 + at[1], side]
    loads = []
    for turn, side in enumerate((1 - core, core)):
        start = 0
        for number, (grad, width) in enumerate(zip(grads, widths)):
            copy = pltpu.make_async_copy(
                grad.at[:, side], own_s.at[: grad.shape[0], side, :, start : start + width],
                load_sem.at[turn, number, 0],
            )
            copy.start()
            loads.append((turn, copy))
            if grad.shape[0] == 8:
                copy = pltpu.make_async_copy(
                    grad.at[:, side], own_s.at[8:, side, :, start : start + width],
                    load_sem.at[turn, number, 1],
                )
                copy.start()
                loads.append((turn, copy))
            start += width
    for turn, copy in loads:
        if turn == 0:
            copy.wait()
    copies = []

    def send(src, dst, target, number):
        copy = pltpu.make_async_remote_copy(
            src_ref=src, dst_ref=dst, send_sem=send_sem.at[number], recv_sem=recv_sem.at[number],
            device_id=target, device_id_type=pl.DeviceIdType.MESH,
        )
        copy.start()
        copies.append(copy)

    def arrive(ref, number):
        pltpu.make_async_remote_copy(
            src_ref=ref, dst_ref=ref, send_sem=send_sem.at[number], recv_sem=recv_sem.at[number],
            device_id=to_core, device_id_type=pl.DeviceIdType.MESH,
        ).wait_recv()

    def add(ref, *others):
        total = ref[...].astype(F32)
        for other in others:
            total = total + other[...].astype(F32)
        ref[...] = total.astype(BF16)

    me = (y, x)
    places = (cross, first, second, me)
    theirs = (0, 2, 1, 3)
    turns = (2, 1, 3, 0)
    for d in turns:
        for kind in (0, 2, 1, 3):
            number = theirs[kind] * 4 + d
            send(mine(places[kind], line[d], 1 - core), chip_s.at[number], to_core, number)

    for turn, copy in loads:
        if turn == 1:
            copy.wait()

    def fold(kind, d):
        here = chip_s.at[kind * 4 + d]
        arrive(here, kind * 4 + d)
        own = mine(places[kind], line[d], core)
        if kind in (0, 2):
            there = 0 if kind == 0 else 4
            add(here, own)
            send(here, second_s.at[there + d], to_second, 16 + there + d)
        elif kind == 1:
            arrive(second_s.at[d], 16 + d)
            add(here, own, second_s.at[d])
            send(here, first_s.at[d], to_first, 24 + d)
        else:
            arrive(second_s.at[4 + d], 20 + d)
            arrive(first_s.at[d], 24 + d)
            if d:
                add(here, own, second_s.at[4 + d], first_s.at[d])
                send(here, line_s.at[d - 1], device_at(y, line[d], x, core), 27 + d)

    stages = [(0, 2), (1,), (3,)]
    for turn in range(len(turns) + 2):
        for stage, kinds in enumerate(stages):
            if 0 <= turn - stage < len(turns):
                for kind in kinds:
                    fold(kind, turns[turn - stage])
    for d in (1, 2, 3):
        arrive(line_s.at[d - 1], 27 + d)
    total = chip_s[12].astype(F32) + mine(me, z, core)[...].astype(F32)
    for ref in (second_s.at[4], first_s.at[0], line_s.at[0], line_s.at[1], line_s.at[2]):
        total = total + ref[...].astype(F32)
    out_ref[...] = total
    for copy in copies:
        copy.wait_send()


def collect(grads, collective_id):
    rows = grads[0].shape[2]
    widths = tuple(grad.shape[3] for grad in grads)
    block = lambda count: pltpu.VMEM((count, rows, sum(widths)), BF16)
    return pl.pallas_call(
        functools.partial(collect_kernel, widths=widths),
        in_specs=[pl.BlockSpec(memory_space=pl.ANY)] * len(grads),
        out_specs=pl.BlockSpec(memory_space=pltpu.VMEM),
        out_shape=jax.ShapeDtypeStruct((rows, sum(widths)), F32),
        scratch_shapes=[
            pltpu.VMEM((16, 2, rows, sum(widths)), BF16), block(16), block(8), block(4), block(3),
            pltpu.SemaphoreType.DMA((31,)), pltpu.SemaphoreType.DMA((31,)),
            pltpu.SemaphoreType.DMA((2, len(widths), 2)),
        ],
        compiler_params=pltpu.CompilerParams(
            collective_id=collective_id, has_side_effects=True, vmem_limit_bytes=VMEM_BYTES
        ),
        name="collect",
    )(*grads)


def run_schulz(fresh, width):
    units, height, _ = fresh.shape
    spec = pl.BlockSpec((1, height, 2 * width), lambda g: (g, 0, 0))
    return pl.pallas_call(
        lambda *refs: schulz(*refs, width=width),
        grid=(units,),
        in_specs=[spec],
        out_specs=spec,
        out_shape=jax.ShapeDtypeStruct((units, height, 2 * width), BF16),
        compiler_params=params_for(),
        name="schulz",
    )(fresh)


def token_major(rows):
    count, channels = rows.shape
    split = rows.reshape(count // ROWS, IMGS, SLOT, channels)
    return split.transpose(0, 2, 1, 3).reshape(count, channels)


def image_major(rows):
    count, channels = rows.shape
    split = rows.reshape(count // ROWS, SLOT, IMGS, channels)
    return split.transpose(0, 2, 1, 3).reshape(count, channels)


def key_masks(grid_class):
    extent = 5 + 2 * grid_class
    across = (jnp.arange(SIDE, dtype=jnp.int32)[None, :] < extent[:, None]).astype(F32)
    cells = (across[:, :, None] * across[:, None, :]).reshape(-1, SIDE * SIDE)
    return jnp.concatenate([jnp.ones((cells.shape[0], 1), F32), cells], axis=1)


def split_heads(shard, heads_own, head_dim):
    lead = shard.shape[:-1]
    parts = shard.reshape(lead + (heads_own, 3, head_dim))
    return jnp.swapaxes(parts, -3, -2).reshape(lead + (3 * heads_own * head_dim,))


def join_heads(shard, heads_own, head_dim):
    lead = shard.shape[:-1]
    parts = shard.reshape(lead + (3, heads_own, head_dim))
    return jnp.swapaxes(parts, -3, -2).reshape(lead + (3 * heads_own * head_dim,))


def block_scale(height, breadth):
    return math.sqrt(max(1.0, height / breadth))


def normalized_step(param_vals, moment, grads_in, rate, axes):
    fresh = 0.5 * moment + grads_in
    level = jnp.sqrt(jnp.mean(fresh * fresh, axis=axes, keepdims=True))
    return (fresh, param_vals - rate * fresh / (level + 1e-06))


def on_device(
    tokens, cotangent, grid_class,
    qkv_weight, proj_weight, up_weight, down_weight, norm_params, cpe_weight, crpe_weight,
    qkv_moment, proj_moment, up_moment, down_moment, norm_moment, cpe_moment, crpe_moment,
):
    own_count, channels = tokens.shape
    blk_count = lax.axis_size("blk")
    tok_count = lax.axis_size("tok")
    blk_at = lax.axis_index("blk")
    layers = qkv_weight.shape[0]
    images_own = grid_class.shape[0] // blk_count
    head_dim = channels // HEADS
    heads_own = HEADS // blk_count
    groups_own = GROUPS // blk_count
    group_width = up_weight.shape[2] // groups_own
    own_rows = qkv_weight.shape[1]
    both = ("blk", "tok")

    attn_cols, feed_cols = 4 * heads_own * head_dim, 2 * up_weight.shape[2]
    near = (tok_count, blk_count, layers) == (16, 2, 2)
    turn = lambda array: jnp.swapaxes(array, 1, 2)
    flip = lambda array: jnp.swapaxes(array, 0, 1)
    mats = (qkv_weight, turn(proj_weight), up_weight, turn(down_weight))
    moments = (qkv_moment, turn(proj_moment), up_moment, turn(down_moment))
    if near:
        shard = pack(mats)
    else:
        shard = jnp.concatenate(
            [
                up_weight,
                jnp.swapaxes(down_weight, 1, 2),
                split_heads(qkv_weight, heads_own, head_dim),
                jnp.swapaxes(proj_weight, 1, 2),
            ],
            axis=2,
        ).astype(BF16)

    def gather(piece, kernel):
        if kernel:
            return spread(piece, 1).reshape(blk_count, channels, piece.shape[1])
        full = lax.all_gather(piece, both, axis=0, tiled=True)
        return full.reshape(blk_count, channels, piece.shape[1])

    def halves(full):
        full = full.reshape(blk_count, channels, 4, heads_own * head_dim).transpose(1, 2, 0, 3)
        full = full.reshape(channels, 4, 2, channels // 2).transpose(2, 0, 1, 3)
        return full.reshape(2, channels, 2 * channels)

    def shares(grads):
        if blk_count == 2:
            return grads
        full = grads.reshape(2, channels, 4, channels // 2).transpose(1, 2, 0, 3)
        full = full.reshape(channels, 4, blk_count, heads_own * head_dim).transpose(2, 0, 1, 3)
        return full.reshape(blk_count, channels, attn_cols)

    attn_all, feed_all = [], []
    for layer in range(layers):
        piece = shard[layer]
        if layer and near:
            piece, full = lax.optimization_barrier((piece, full))
            attn_all[0], feed_all[0] = (full, attn_cols, 2), (full, feed_cols, 0)
        full = gather(piece, near and layer == 0)
        if blk_count == 2:
            attn_all.append((full, attn_cols, 2))
            feed_all.append((full, feed_cols, 0))
        else:
            attn_all.append((halves(full[:, :, feed_cols:]), 2 * channels, 0))
            feed_all.append((full[:, :, :feed_cols], feed_cols, 0))

    own_class = lax.dynamic_slice_in_dim(grid_class, blk_at * images_own, images_own)
    keys = key_masks(own_class)
    mask = jnp.broadcast_to(token_major(keys.reshape(own_count, 1)), (own_count, LANES))
    taps = jnp.repeat(tap_mask(jnp.arange(HEADS, dtype=jnp.int32)), head_dim, axis=1)

    stream = tokens
    saved = []
    for layer in range(layers):
        cpe, crpe = cpe_weight[layer], crpe_weight[layer] * taps
        outs = run_attend_forward(
            stream, mask, attn_all[layer], norm_params[layer], cpe, crpe, layer == 0
        )
        if layer:
            outs = [stream] + list(outs)
        middle = None
        if layer < layers - 1:
            stream, *middle = run_feed_forward(outs[-1], feed_all[layer], norm_params[layer])
        saved.append(tuple(outs) + (middle, cpe, crpe))

    upstream = cotangent
    attn_sums, feed_sums = [None] * layers, [None] * layers
    small_rows = SMALL_ROWS
    for layer in reversed(range(layers)):
        x, unit, inv, packed, rel, mixed, att, middle, cpe, crpe = saved[layer]
        last = layer == layers - 1
        if last:
            inputs = [mask, upstream, att]
        else:
            inputs = [upstream, middle[2], middle[3], middle[0], middle[1]]
        outs = run_feed_back(inputs, feed_all[layer], norm_params[layer], last)
        if last:
            block_out = outs[0]
        gatt, gfeed, gmid = outs[-3:]
        upstream, gattn, small = run_attend_back(
            gatt, x, unit, inv, packed, rel, mixed, mask, attn_all[layer],
            norm_params[layer], cpe, crpe, gmid, taps, layer == 0,
        )
        if near and layer == layers - 1:
            early = lax.psum_scatter(
                gfeed.reshape(blk_count * channels, gfeed.shape[2]), both,
                scatter_dimension=0, tiled=True,
            )
        gattn = shares(gattn)
        if near:
            split = lambda g: g.reshape(-1, 2, own_rows, g.shape[-1])
            pieces = [split(g) for g in (gattn, small, gfeed)]
            waiting = pieces[:2] if layer else waiting + pieces
        else:
            small = jnp.broadcast_to(small, (blk_count, channels, LANES))
            scatter = lambda g: lax.psum_scatter(
                g.reshape(blk_count * channels, g.shape[2]), both, scatter_dimension=0, tiled=True
            ).astype(F32)
            feed_sums[layer] = scatter(gfeed)
            attn_sums[layer] = scatter(jnp.concatenate([gattn, small], axis=2))
    tokens_grad = upstream

    scales = (
        block_scale(channels, 3 * head_dim),
        block_scale(head_dim, channels),
        block_scale(channels, group_width),
        block_scale(group_width, channels),
    )
    if near:
        early, waiting = lax.optimization_barrier((early, waiting))
        total = collect(waiting, 2)
        ready = prepare(total, early, moments, tok_count, group_width)
        big, little, small_all = finish(ready[4], ready[5], 3)
        done = update(
            big, little, small_all, mats,
            (norm_params, flip(cpe_weight), flip(crpe_weight)),
            (norm_moment, flip(cpe_moment), flip(crpe_moment)),
            tuple(rate * scale for rate, scale in zip(MUON_RATES, scales)),
        )
        results = []
        for kind in range(4):
            three = (ready[kind], done[2 * kind], done[2 * kind + 1])
            results += [turn(array) if kind % 2 else array for array in three]
        return (block_out, tokens_grad, *results, *done[8:10], *map(flip, done[10:]))
    attn_sum = jnp.stack(attn_sums)
    feed_sum = jnp.stack(feed_sums)
    small_sum = attn_sum[:, :, -LANES:][:, :, :small_rows]
    attn_sum = attn_sum[:, :, :-LANES]
    attn_moment = jnp.concatenate(
        [split_heads(qkv_moment, heads_own, head_dim), jnp.swapaxes(proj_moment, 1, 2)], axis=2
    )
    feed_moment = jnp.concatenate([up_moment, jnp.swapaxes(down_moment, 1, 2)], axis=2)
    attn_fresh = 0.5 * attn_moment + attn_sum
    feed_fresh = 0.5 * feed_moment + feed_sum

    units = layers * 2 * groups_own
    per_dev = -(-units // tok_count)
    big = feed_fresh.reshape(layers, own_rows, 2 * groups_own, group_width)
    big = big.transpose(0, 2, 1, 3).reshape(units, own_rows, group_width)
    heads = attn_fresh.reshape(layers, own_rows, 4, heads_own, head_dim).transpose(0, 3, 1, 2, 4)
    heads_qkv = heads[:, :, :, :3].reshape(layers, heads_own, own_rows, 3 * head_dim)
    heads_proj = heads[:, :, :, 3]
    widen = lambda v: jnp.pad(v, ((0, 0), (0, 0), (0, 0), (0, group_width - v.shape[3])))
    little = jnp.concatenate([widen(heads_qkv), widen(heads_proj)], axis=1)
    little = little.reshape(units, own_rows, group_width)
    def owners(blocks):
        blocks = jnp.pad(blocks.astype(BF16), ((0, per_dev * tok_count - units), (0, 0), (0, 0)))
        return blocks.reshape(tok_count, per_dev, own_rows, group_width)

    big, little = owners(big), owners(little)
    small_own = jnp.swapaxes(small_sum, 0, 1).reshape(own_rows, layers * small_rows)
    small_own = jnp.pad(small_own, ((0, 0), (0, LANES - layers * small_rows))).astype(BF16)
    small_own = jnp.broadcast_to(small_own, (tok_count, per_dev, own_rows, LANES))
    little = jnp.concatenate([little, small_own], axis=3)
    got = lax.all_to_all(jnp.concatenate([big, little], axis=3), "tok", 0, 0, tiled=True)
    got = got.transpose(1, 0, 2, 3).reshape(per_dev, channels, 2 * group_width + LANES)
    small_all = got[0, :, 2 * group_width :]
    ortho = run_schulz(got, group_width)
    ortho = ortho.reshape(per_dev, tok_count, own_rows, 2 * group_width)
    ortho = lax.all_to_all(ortho.transpose(1, 0, 2, 3), "tok", 0, 0, tiled=True)
    ortho = ortho.reshape(per_dev * tok_count, own_rows, 2 * group_width)[:units]
    big, little = ortho[:, :, :group_width], ortho[:, :, group_width:]
    small_all = small_all.astype(F32).T[: layers * small_rows]
    small_all = small_all.reshape(layers, small_rows, channels)
    big = big.astype(F32).reshape(layers, 2, groups_own, own_rows, group_width)
    big = big.transpose(1, 0, 3, 2, 4).reshape(2, layers, own_rows, groups_own * group_width)
    little = little.astype(F32).reshape(layers, 2, heads_own, own_rows, group_width)
    little_qkv = little[:, 0, :, :, : 3 * head_dim].transpose(0, 2, 1, 3)
    little_qkv = little_qkv.reshape(layers, own_rows, heads_own * 3 * head_dim)
    little_proj = little[:, 1, :, :, :head_dim].transpose(0, 1, 3, 2)
    little_proj = little_proj.reshape(layers, heads_own * head_dim, own_rows)

    qkv_fresh = join_heads(attn_fresh[:, :, : qkv_weight.shape[2]], heads_own, head_dim)
    proj_fresh = jnp.swapaxes(attn_fresh[:, :, qkv_weight.shape[2] :], 1, 2)
    up_fresh = feed_fresh[:, :, : up_weight.shape[2]]
    down_fresh = jnp.swapaxes(feed_fresh[:, :, up_weight.shape[2] :], 1, 2)
    results = []
    for kind, (weight, fresh, turned) in enumerate(
        (
            (qkv_weight, qkv_fresh, little_qkv),
            (proj_weight, proj_fresh, little_proj),
            (up_weight, up_fresh, big[0]),
            (down_weight, down_fresh, jnp.swapaxes(big[1], 1, 2)),
        )
    ):
        new = weight - MUON_RATES[kind] * scales[kind] * turned
        results.extend([fresh, new, new.astype(BF16)])

    norm_fresh, norm_new = normalized_step(
        norm_params, norm_moment, small_all[:, :4], SMALL_RATES[0], (2,)
    )
    cpe_fresh, cpe_new = normalized_step(
        cpe_weight, cpe_moment, small_all[:, 4:13], SMALL_RATES[1], (1, 2)
    )
    head_shape = (layers, 49, HEADS, head_dim)
    crpe_fresh, crpe_new = normalized_step(
        crpe_weight.reshape(head_shape),
        crpe_moment.reshape(head_shape),
        small_all[:, 13:].reshape(head_shape),
        SMALL_RATES[2],
        (1, 3),
    )
    return (
        (block_out, tokens_grad)
        + tuple(results)
        + (norm_fresh, norm_new, cpe_fresh, cpe_new)
        + (crpe_fresh.reshape(crpe_weight.shape), crpe_new.reshape(crpe_weight.shape))
    )


def solution(mesh):
    rows = P(("tok", "blk"), None)
    down_cols = P(None, "tok", "blk")
    cross = P(None, "blk", "tok")
    mats = (down_cols, cross, down_cols, cross)
    in_specs = (rows, rows, P("tok")) + mats + (P(),) * 3 + mats + (P(),) * 3
    out_specs = (rows, rows) + tuple(spec for spec in mats for _ in range(3)) + (P(),) * 6
    return jax.shard_map(
        on_device, mesh=mesh, in_specs=in_specs, out_specs=out_specs, check_vma=False
    )
```

```python
import functools
import math

import jax
import jax.numpy as jnp
from jax import lax
from jax.experimental import pallas as pl
from jax.experimental.pallas import tpu as pltpu
from jax.sharding import PartitionSpec as P

HEADS = 8
GROUPS = 8
SLOT = 82
SIDE = 9
LANES = 128
IMGS = 8
ROWS = SLOT * IMGS
SCHULZ_COEFFS = (3.4445, -4.775, 2.0315)
MUON_RATES = (0.8, 0.8, 0.8, 0.4)
SMALL_RATES = (0.3, 0.3, 0.15)
SMALL_ROWS = 4 + 9 + 49
HEAD_DIM = 64
VMEM_BYTES = 60 * 1024 * 1024
F32 = jnp.float32
BF16 = jnp.bfloat16


def mm(a, b):
    return jnp.dot(a, b, preferred_element_type=F32)


def mm_nt(a, b):
    return lax.dot_general(a, b, (((1,), (1,)), ((), ())), preferred_element_type=F32)


def mm_tn(a, b):
    return lax.dot_general(a, b, (((0,), (0,)), ((), ())), preferred_element_type=F32)


def tap_mask(head_ids):
    radius = jnp.where(head_ids < 2, 1, jnp.where(head_ids < 5, 2, 3))
    offsets = jnp.abs(jnp.arange(7, dtype=jnp.int32) - 3)
    within = (offsets[:, None] <= radius[None, :]).astype(F32)
    return (within[:, None, :] * within[None, :, :]).reshape(49, head_ids.shape[0])


def tile_radius(lane_at, head_dim):
    last = ((lane_at + 1) * LANES - 1) // head_dim
    return 1 if last < 2 else (2 if last < 5 else 3)


def normalize(values):
    center = values - jnp.mean(values, axis=-1, keepdims=True)
    spread = jnp.mean(center * center, axis=-1, keepdims=True)
    inv = lax.rsqrt(spread + 1e-06)
    return center * inv, inv


def norm_back(grad, unit, inv, gain):
    scaled = grad * gain
    first = jnp.mean(scaled, axis=-1, keepdims=True)
    second = jnp.mean(scaled * unit, axis=-1, keepdims=True)
    return inv * (scaled - first - unit * second)


def lane(at):
    return slice(at * LANES, (at + 1) * LANES)


def grid_rows(row_at):
    return slice((1 + SIDE * row_at) * IMGS, (1 + SIDE * (row_at + 1)) * IMGS)


def lane_pair(low, high):
    cells = lambda tile: tile[IMGS:].reshape(SIDE, SIDE, IMGS, LANES)
    return jnp.concatenate([cells(low), cells(high)], axis=2).astype(BF16)


def split_pair(line):
    line = line.astype(F32)
    turn = lambda part: part.reshape(SIDE * IMGS, LANES)
    return turn(line[:, :IMGS]), turn(line[:, IMGS:])


def conv_row(cells_ref, kernel_ref, pair, row_at, reach, width, flip):
    mid = width // 2
    total = [None] * SIDE
    for down in range(-reach, reach + 1):
        if not 0 <= row_at + down < SIDE:
            continue
        line = cells_ref[row_at + down]
        acc = [None] * SIDE
        for along in range(-reach, reach + 1):
            tap = (mid - down, mid - along) if flip else (mid + down, mid + along)
            weight = kernel_ref[pair, tap[0] * width + tap[1]]
            for col in range(SIDE):
                if 0 <= col + along < SIDE:
                    term = line[col + along] * weight
                    acc[col] = term if acc[col] is None else acc[col] + term
        total = [new if old is None else old + new for old, new in zip(total, acc)]
    return jnp.stack(total, axis=0)


def conv_kernel_grad(grad_ref, cells_ref, total_ref, pair, reach, width):
    mid = width // 2
    for down in range(-reach, reach + 1):
        rows = [at for at in range(SIDE) if 0 <= at + down < SIDE]
        whole_sum = [None] * (2 * reach + 1)
        for start in range(0, len(rows), 3):
            acc = [None] * (2 * reach + 1)
            for row_at in rows[start : start + 3]:
                grad_line = grad_ref[row_at]
                line = cells_ref[row_at + down]
                for along in range(-reach, reach + 1):
                    for col in range(SIDE):
                        if 0 <= col + along < SIDE:
                            term = grad_line[col] * line[col + along]
                            at = along + reach
                            acc[at] = term if acc[at] is None else acc[at] + term
            acc = [value.astype(F32) for value in acc]
            whole_sum = [new if old is None else old + new for old, new in zip(whole_sum, acc)]
        for along in range(-reach, reach + 1):
            tap = (mid + down) * width + mid + along
            value = whole_sum[along + reach]
            total_ref[tap, :, lane(2 * pair)] += value[:IMGS]
            total_ref[tap, :, lane(2 * pair + 1)] += value[IMGS:]


def fill_taps(kernel_ref, table_ref):
    for pair in range(table_ref.shape[0]):
        for tap in range(table_ref.shape[1]):
            sides = [kernel_ref[tap : tap + 1, lane(2 * pair + side)] for side in range(2)]
            sides = [jnp.broadcast_to(side, (IMGS, LANES)) for side in sides]
            table_ref[pair, tap] = jnp.concatenate(sides, axis=0).astype(BF16)


def key_softmax(key_tile, mask_tile):
    keys = key_tile.reshape(SLOT, IMGS, LANES)
    live = mask_tile.reshape(SLOT, IMGS, LANES)
    top = jnp.max(jnp.where(live > 0, keys, -1e30), axis=0, keepdims=True)
    raw = jnp.exp(jnp.where(live > 0, keys - top, -60.0)) * live
    return (raw / jnp.sum(raw, axis=0, keepdims=True)).reshape(ROWS, LANES)


def head_mask(size, head_dim):
    down = lax.broadcasted_iota(jnp.int32, (size, size), 0) // head_dim
    along = lax.broadcasted_iota(jnp.int32, (size, size), 1) // head_dim
    return jnp.where(down == along, F32(head_dim ** -0.5), F32(0.0))


def image_rows(ref, quad, image):
    rows = pl.ds(image, SLOT, stride=IMGS)
    return jnp.concatenate([ref[2 * quad, rows, :], ref[2 * quad + 1, rows, :]], axis=1)


def put_image_rows(ref, quad, image, values):
    rows = pl.ds(image, SLOT, stride=IMGS)
    ref[2 * quad, rows, :] = values[:, :LANES]
    ref[2 * quad + 1, rows, :] = values[:, LANES:]


def to_token_major(src_ref, put):
    for token in range(SLOT):
        put(slice(token * IMGS, (token + 1) * IMGS), src_ref[pl.ds(token, IMGS, stride=SLOT), :])


def to_image_major(src_ref, put):
    for image in range(IMGS):
        put(slice(image * SLOT, (image + 1) * SLOT), src_ref[pl.ds(image, SLOT, stride=IMGS), :])


def attend_forward(*refs, first):
    if first:
        tokens_ref, refs = refs[0], refs[1:]
        (mask_ref, w_ref, norm_ref, cpe_in, crpe_in, x_ref, unit_ref, inv_ref, packed_ref,
         rel_ref, mixed_ref, att_ref, x_cells, v_cells, cpe_ref, crpe_ref, conv_ref,
         q_s, k_s, v_s, f_s, c_s) = refs
    else:
        (x_ref, mask_ref, w_ref, norm_ref, cpe_in, crpe_in, unit_ref, inv_ref, packed_ref,
         rel_ref, mixed_ref, att_ref, x_cells, v_cells, cpe_ref, crpe_ref, conv_ref,
         q_s, k_s, v_s, f_s, c_s) = refs
    channels = x_ref.shape[1]
    tiles = channels // LANES
    head_dim = channels // HEADS
    half = channels // 2

    @pl.when(pl.program_id(0) == 0)
    def _():
        fill_taps(cpe_in, cpe_ref)
        fill_taps(crpe_in, crpe_ref)

    if first:
        for at in range(tiles):
            cols = lane(at)
            f_s[at] = tokens_ref[:, cols].astype(F32)

            def put(rows, values, cols=cols):
                x_ref[rows, cols] = values

            to_token_major(f_s.at[at], put)
    for pair in range(tiles // 2):
        both = (lane(2 * pair), lane(2 * pair + 1))
        mask = mask_ref[...]
        x_cells[...] = lane_pair(*[x_ref[:, cols] * mask for cols in both])
        for cols in both:
            conv_ref[:IMGS, cols] = x_ref[:IMGS, cols]
        for row_at in range(SIDE):
            rows = grid_rows(row_at)
            out = split_pair(conv_row(x_cells, cpe_ref, pair, row_at, 1, 3, False))
            for cols, value in zip(both, out):
                conv_ref[rows, cols] = x_ref[rows, cols] + value * mask_ref[rows, :]
    unit, inv = normalize(conv_ref[...])
    unit_ref[...] = unit.astype(BF16)
    inv_ref[...] = inv
    normed = (unit * norm_ref[0:1, :] + norm_ref[1:2, :]).astype(BF16)
    for side in range(2):
        for third, keep in enumerate((q_s, k_s, v_s)):
            cols = slice(third * half, (third + 1) * half)
            part = mm(normed, w_ref[side, :, cols]).astype(BF16)
            if third != 1:
                start = (3 * side + third) * half
                packed_ref[:, start : start + half] = part
            part = part.astype(F32)
            for at in range(tiles // 2):
                keep[side * (tiles // 2) + at] = part[:, lane(at)]
    for at in range(tiles):
        weights = key_softmax(k_s[at], mask_ref[...])
        k_s[at] = weights
        start = (3 * (at // 2) + 1) * half + (at % 2) * LANES
        packed_ref[:, start : start + LANES] = weights.astype(BF16)
    block = head_mask(2 * LANES, head_dim)

    def one_image(image, carry):
        for quad in range(tiles // 2):
            keys = image_rows(k_s, quad, image).astype(BF16)
            values = image_rows(v_s, quad, image).astype(BF16)
            query = image_rows(q_s, quad, image).astype(BF16)
            context = (mm_tn(keys, values) * block).astype(BF16)
            put_image_rows(f_s, quad, image, mm(query, context))
        return carry

    lax.fori_loop(0, IMGS, one_image, 0, unroll=True)
    c_s[:, :IMGS, :] = jnp.zeros((2, IMGS, LANES), F32)
    for pair in range(tiles // 2):
        mask = mask_ref[...]
        v_cells[...] = lane_pair(v_s[2 * pair] * mask, v_s[2 * pair + 1] * mask)
        reach = tile_radius(2 * pair + 1, head_dim)
        for row_at in range(SIDE):
            rows = grid_rows(row_at)
            out = split_pair(conv_row(v_cells, crpe_ref, pair, row_at, reach, 7, False))
            for half_at, value in enumerate(out):
                c_s[half_at, rows, :] = value * mask_ref[rows, :]
        for half_at in range(2):
            at = 2 * pair + half_at
            rel = c_s[half_at]
            rel_ref[:, lane(at)] = rel.astype(BF16)
            mixed_ref[:, lane(at)] = (f_s[at] + q_s[at] * rel).astype(BF16)
    out = conv_ref[...]
    for side in range(2):
        cols = slice(side * half, (side + 1) * half)
        out = out + mm_nt(mixed_ref[:, cols], w_ref[side, :, 3 * half :])
    att_ref[...] = out


def gelu_parts(hidden):
    number = lambda value: jnp.asarray(value, BF16)
    values = hidden.astype(BF16)
    t = pl.reciprocal(
        number(1.0) + number(0.3275911 * 0.7071067811865476) * jnp.abs(values), approx=True
    )
    bell = jnp.exp2(number(-0.5 * 1.4426950408889634) * (values * values))
    poly = number(0.5 * 1.061405429)
    for coef in (-1.453152027, 1.421413741, -0.284496736, 0.254829592):
        poly = poly * t + number(0.5 * coef)
    tail = poly * t * bell
    phi = jnp.where(values >= 0, number(1.0) - tail, tail)
    return values * phi, phi + (values * number(0.3989422804014327)) * bell


def feed_forward(
    att_ref, up_down_ref, norm_ref, out_ref, act_ref, slope_ref, unit_ref, inv_ref, *scratch, chunk
):
    blks, _, both = up_down_ref.shape
    width = both // 2
    chunk = min(chunk, width)
    att = att_ref[...]
    unit, inv = normalize(att)
    unit_ref[...] = unit.astype(BF16)
    inv_ref[...] = inv
    normed = (unit * norm_ref[2:3, :] + norm_ref[3:4, :]).astype(BF16)
    total = att
    for blk in range(blks):
        for at in range(0, width, chunk):
            hidden = mm(normed, up_down_ref[blk, :, at : at + chunk])
            active, slope = gelu_parts(hidden)
            cols = slice(blk * width + at, blk * width + at + chunk)
            act_ref[:, cols] = active
            slope_ref[:, cols] = slope
            total = total + mm_nt(active, up_down_ref[blk, :, width + at : width + at + chunk])
    if not scratch:
        out_ref[...] = total
        return
    turn_s, whole_s = scratch
    for at in range(att.shape[1] // LANES):
        cols = lane(at)
        turn_s[0] = total[:, cols]

        def put(rows, values, cols=cols):
            whole_s[rows, cols] = values

        to_image_major(turn_s.at[0], put)
    out_ref[...] = whole_s[...].astype(BF16)


def feed_back(*refs, first, chunk):
    if first:
        (mask_ref, cot_ref, att_ref, up_down_ref, norm_ref, out_ref,
         gatt_ref, gweight_ref, gnorm_ref, total_s, act_ref, slope_ref, unit_ref, inv_ref,
         turn_s, whole_s) = refs
        feed_forward(
            att_ref, up_down_ref, norm_ref, out_ref, act_ref, slope_ref, unit_ref, inv_ref,
            turn_s, whole_s, chunk=chunk,
        )
    else:
        (up_ref, unit_ref, inv_ref, act_ref, slope_ref, up_down_ref, norm_ref,
         gatt_ref, gweight_ref, gnorm_ref, total_s) = refs
    step, steps = pl.program_id(0), pl.num_programs(0)
    blks, _, both = up_down_ref.shape
    width = both // 2
    chunk = min(chunk, width)

    @pl.when(step == 0)
    def _():
        total_s[...] = jnp.zeros_like(total_s)
        gnorm_ref[...] = jnp.zeros_like(gnorm_ref)

    if first:
        for at in range(cot_ref.shape[1] // LANES):
            cols = lane(at)
            turn_s[0] = cot_ref[:, cols]

            def put(rows, values, cols=cols):
                whole_s[rows, cols] = values * mask_ref[rows, :]

            to_token_major(turn_s.at[0], put)
        upstream = whole_s[...]
    else:
        upstream = up_ref[...]
    unit, inv = unit_ref[...].astype(F32), inv_ref[...]
    gain = norm_ref[2:3, :]
    normed = (unit * gain + norm_ref[3:4, :]).astype(BF16)
    down_in = upstream.astype(BF16)
    grad_mid = None
    for blk in range(blks):
        for at in range(0, width, chunk):
            cols = slice(blk * width + at, blk * width + at + chunk)
            ups = slice(at, at + chunk)
            downs = slice(width + at, width + at + chunk)
            grad_active = mm(down_in, up_down_ref[blk, :, downs])
            grad_hidden = (grad_active * slope_ref[:, cols].astype(F32)).astype(BF16)
            total_s[blk, :, ups] += mm_tn(normed, grad_hidden)
            total_s[blk, :, downs] += mm_tn(down_in, act_ref[:, cols])
            part = mm_nt(grad_hidden, up_down_ref[blk, :, ups])
            grad_mid = part if grad_mid is None else grad_mid + part
    gatt_ref[...] = upstream + norm_back(grad_mid, unit, inv, gain)
    gnorm_ref[0:1, :] += jnp.sum(grad_mid * unit, axis=0, keepdims=True)
    gnorm_ref[1:2, :] += jnp.sum(grad_mid, axis=0, keepdims=True)

    @pl.when(step == steps - 1)
    def _():
        gweight_ref[...] = total_s[...].astype(BF16)


def attend_back(
    gatt_ref, x_ref, unit_ref, inv_ref, packed_ref, rel_ref, mixed_ref, mask_ref,
    w_ref, norm_ref, cpe_in, crpe_in, gmid_ref, taps_ref,
    out_ref, gw_ref, small_ref, gnorm_ref, gcpe_ref, gcrpe_ref,
    w_s, x_cells, g_cells, v_cells, c_cells, cpe_ref, crpe_ref, q_s, k_s, v_s, f_s, dq_s, dk_s, dv_s, c_s, gp_s,
    *scratch,
):
    channels = x_ref.shape[1]
    tiles = channels // LANES
    head_dim = channels // HEADS
    half = channels // 2
    step, steps = pl.program_id(0), pl.num_programs(0)
    up_ref = scratch[0] if scratch else out_ref

    @pl.when(step == 0)
    def _():
        fill_taps(cpe_in, cpe_ref)
        fill_taps(crpe_in, crpe_ref)
        for ref in (w_s, gnorm_ref, gcpe_ref, gcrpe_ref):
            ref[...] = jnp.zeros_like(ref)

    att_in = gatt_ref[...].astype(BF16)
    att_t = att_in.T
    for side in range(2):
        cols = slice(side * half, (side + 1) * half)
        w_s[side, :, 3 * half :] += mm(att_t, mixed_ref[:, cols])
        grad_mixed = mm(att_in, w_ref[side, :, 3 * half :])
        for at in range(tiles // 2):
            f_s[side * (tiles // 2) + at] = grad_mixed[:, lane(at)]
        for third, keep in enumerate((q_s, k_s, v_s)):
            for at in range(tiles // 2):
                start = (3 * side + third) * half + at * LANES
                keep[side * (tiles // 2) + at] = packed_ref[:, start : start + LANES].astype(F32)
    block = head_mask(2 * LANES, head_dim)

    def one_image(image, carry):
        for quad in range(tiles // 2):
            keys = image_rows(k_s, quad, image).astype(BF16)
            values = image_rows(v_s, quad, image).astype(BF16)
            query = image_rows(q_s, quad, image).astype(BF16)
            grads = image_rows(f_s, quad, image).astype(BF16)
            context = (mm_tn(keys, values) * block).astype(BF16)
            grad_context = (mm_tn(query, grads) * block).astype(BF16)
            put_image_rows(dq_s, quad, image, mm_nt(grads, context))
            put_image_rows(dk_s, quad, image, mm_nt(values, grad_context))
            put_image_rows(dv_s, quad, image, mm(keys, grad_context))
        return carry

    lax.fori_loop(0, IMGS, one_image, 0, unroll=True)
    for pair in range(tiles // 2):
        mask = mask_ref[...]
        place = lambda at, third: slice(
            (3 * pair + third) * half + at * LANES, (3 * pair + third) * half + (at + 1) * LANES
        )
        for half_at in range(2):
            at = 2 * pair + half_at
            weights = k_s[at]
            share = weights * dk_s[at]
            total = jnp.sum(share.reshape(SLOT, IMGS, LANES), axis=0, keepdims=True)
            back = share.reshape(SLOT, IMGS, LANES) - weights.reshape(SLOT, IMGS, LANES) * total
            gp_s[:, place(half_at, 1)] = back.reshape(ROWS, LANES).astype(BF16)
            rel = rel_ref[:, lane(at)].astype(F32)
            gp_s[:, place(half_at, 0)] = (dq_s[at] + f_s[at] * rel).astype(BF16)
        reach = tile_radius(2 * pair + 1, head_dim)
        v_cells[...] = lane_pair(v_s[2 * pair] * mask, v_s[2 * pair + 1] * mask)
        c_cells[...] = lane_pair(
            *[f_s[at] * q_s[at] * mask for at in (2 * pair, 2 * pair + 1)]
        )
        for row_at in range(SIDE):
            rows = grid_rows(row_at)
            out = split_pair(conv_row(c_cells, crpe_ref, pair, row_at, reach, 7, True))
            for half_at, value in enumerate(out):
                dv_s[2 * pair + half_at, rows, :] += value * mask_ref[rows, :]
        conv_kernel_grad(c_cells, v_cells, gcrpe_ref, pair, reach, 7)
        for half_at in range(2):
            gp_s[:, place(half_at, 2)] = dv_s[2 * pair + half_at].astype(BF16)
    unit, inv = unit_ref[...].astype(F32), inv_ref[...]
    gain = norm_ref[0:1, :]
    normed_t = (unit * gain + norm_ref[1:2, :]).astype(BF16).T
    grad_rows = None
    for side in range(2):
        part_in = gp_s[:, side * 3 * half : (side + 1) * 3 * half]
        w_s[side, :, : 3 * half] += mm(normed_t, part_in)
        part = mm_nt(part_in, w_ref[side, :, : 3 * half])
        grad_rows = part if grad_rows is None else grad_rows + part
    gnorm_ref[0:1, :] += jnp.sum(grad_rows * unit, axis=0, keepdims=True)
    gnorm_ref[1:2, :] += jnp.sum(grad_rows, axis=0, keepdims=True)
    up_ref[...] = gatt_ref[...] + norm_back(grad_rows, unit, inv, gain)
    for pair in range(tiles // 2):
        both = (lane(2 * pair), lane(2 * pair + 1))
        mask = mask_ref[...]
        x_cells[...] = lane_pair(*[x_ref[:, cols] * mask for cols in both])
        g_cells[...] = lane_pair(*[up_ref[:, cols] * mask for cols in both])
        for row_at in range(SIDE):
            rows = grid_rows(row_at)
            out = split_pair(conv_row(g_cells, cpe_ref, pair, row_at, 1, 3, True))
            for cols, value in zip(both, out):
                up_ref[rows, cols] += value * mask_ref[rows, :]
        conv_kernel_grad(g_cells, x_cells, gcpe_ref, pair, 1, 3)
    for at in range(tiles if scratch else 0):
        cols = lane(at)
        c_s[0] = up_ref[:, cols]

        def put(rows, values, cols=cols):
            out_ref[rows, cols] = values

        to_image_major(c_s.at[0], put)

    @pl.when(step == steps - 1)
    def _():
        gw_ref[...] = w_s[...].astype(BF16)
        rows = [gnorm_ref[...], gmid_ref[...], jnp.sum(gcpe_ref[...], axis=1)]
        rows.append(jnp.sum(gcrpe_ref[...], axis=1) * taps_ref[...])
        count = sum(part.shape[0] for part in rows)
        rows.append(jnp.zeros((LANES - count, channels), F32))
        small_ref[...] = jnp.concatenate(rows, axis=0).T.astype(BF16)


def dot3(a, b, dims):
    a_hi, b_hi = a.astype(BF16), b.astype(BF16)
    a_lo = (a - a_hi.astype(F32)).astype(BF16)
    b_lo = (b - b_hi.astype(F32)).astype(BF16)
    one = lambda u, v: lax.dot_general(u, v, (dims, ((), ())), preferred_element_type=F32)
    return one(a_hi, b_hi) + (one(a_hi, b_lo) + one(a_lo, b_hi))


def schulz_turns(blocks):
    first, second, third = SCHULZ_COEFFS
    current = []
    for value in blocks:
        level = jnp.sum(jnp.sum(value * value, axis=0, keepdims=True), axis=1, keepdims=True)
        current.append(value / (jnp.sqrt(level) + 1e-07))
    for _ in range(5):
        grams = [dot3(value, value, ((0,), (0,))) for value in current]
        polys = [second * gram + third * dot3(gram, gram, ((1,), (0,))) for gram in grams]
        current = [
            first * value + dot3(value, poly, ((1,), (0,))) for value, poly in zip(current, polys)
        ]
    return current


def schulz(fresh_ref, out_ref, width):
    parts = (slice(0, width), slice(width, 2 * width))
    for cols, value in zip(parts, schulz_turns([fresh_ref[0, :, c].astype(F32) for c in parts])):
        out_ref[0, :, cols] = value.astype(BF16)


def finish_kernel(
    big_ref, little_ref, big_out, little_out, small_ref,
    big_got, little_got, big_turned, little_turned, big_back, little_back, sems,
):
    count, rows, width = big_ref.shape
    me, blk = lax.axis_index("tok"), lax.axis_index("blk")
    targets = [None] + [lax.rem(me + d, count) for d in range(1, count)]
    sources = [None] + [lax.rem(me + count - d, count) for d in range(1, count)]
    greet([(targets[d], blk) for d in range(1, count)])
    copies = []

    def send(src, dst, kind):
        for d in range(1, count):
            copy = pltpu.make_async_remote_copy(
                src_ref=src.at[targets[d]], dst_ref=dst.at[me],
                send_sem=sems.at[2 * kind, d], recv_sem=sems.at[2 * kind + 1, d],
                device_id=(targets[d], blk), device_id_type=pl.DeviceIdType.MESH,
            )
            copy.start()
            copies.append(copy)
        dst[me] = src[me]

    def arrive(dst, kind):
        for d in range(1, count):
            here = dst.at[sources[d]]
            pltpu.make_async_remote_copy(
                src_ref=here, dst_ref=here,
                send_sem=sems.at[2 * kind, d], recv_sem=sems.at[2 * kind + 1, d],
                device_id=(targets[d], blk), device_id_type=pl.DeviceIdType.MESH,
            ).wait_recv()

    def turn(got, turned):
        fresh = got[:, :, :width].reshape(count * rows, width)
        value = schulz_turns([fresh.astype(F32)])[0]
        turned[...] = value.astype(BF16).reshape(count, rows, width)

    send(big_ref, big_got, 0)
    send(little_ref, little_got, 1)
    arrive(big_got, 0)
    turn(big_got, big_turned)
    send(big_turned, big_back, 2)
    arrive(little_got, 1)
    turn(little_got, little_turned)
    send(little_turned, little_back, 3)
    small_ref[...] = little_got[:, :, width:].reshape(count * rows, little_got.shape[2] - width)
    arrive(big_back, 2)
    big_out[...] = big_back[...]
    arrive(little_back, 3)
    little_out[...] = little_back[...]
    for copy in copies:
        copy.wait_send()


def finish(big, little, collective_id):
    count, rows, width = big.shape
    vmem = pl.BlockSpec(memory_space=pltpu.VMEM)
    block = pltpu.VMEM(big.shape, BF16)
    small = (count * rows, little.shape[2] - width)
    return pl.pallas_call(
        finish_kernel,
        in_specs=[vmem, vmem],
        out_specs=[vmem, vmem, vmem],
        out_shape=[jax.ShapeDtypeStruct(shape, BF16) for shape in (big.shape, big.shape, small)],
        scratch_shapes=[
            block, pltpu.VMEM(little.shape, BF16), block, block, block, block,
            pltpu.SemaphoreType.DMA((8, count)),
        ],
        compiler_params=params_for(collective_id=collective_id, has_side_effects=True),
        cost_estimate=cost(25),
        name="finish",
    )(big, little)


def pack_kernel(qkv_ref, proj_ref, up_ref, down_ref, *outs):
    heads = qkv_ref.shape[2] // (3 * HEAD_DIM)
    for layer, out in enumerate(outs):
        wide = up_ref.shape[2]
        out[:, :wide] = up_ref[layer].astype(BF16)
        out[:, wide : 2 * wide] = down_ref[layer].astype(BF16)
        qkv = qkv_ref[layer]
        parts = [
            qkv[:, (3 * head + third) * HEAD_DIM : (3 * head + third + 1) * HEAD_DIM]
            for third in range(3)
            for head in range(heads)
        ]
        start = 2 * wide + qkv.shape[1]
        out[:, 2 * wide : start] = jnp.concatenate(parts, axis=1).astype(BF16)
        out[:, start:] = proj_ref[layer].astype(BF16)


def pack(mats):
    layers, rows = mats[0].shape[:2]
    cols = sum(mat.shape[2] for mat in mats)
    return pl.pallas_call(
        pack_kernel,
        out_shape=[jax.ShapeDtypeStruct((rows, cols), BF16)] * layers,
        compiler_params=params_for(),
        name="pack",
    )(*mats)


def prepare_kernel(total_ref, early_ref, *refs):
    moments, fresh_refs, (big_ref, little_ref) = refs[:4], refs[4:8], refs[8:]
    qkv_m, proj_m, up_m, down_m = moments
    layers, rows, wide = up_m.shape
    span = qkv_m.shape[2]
    heads = span // (3 * HEAD_DIM)
    half = heads * HEAD_DIM
    width = big_ref.shape[2]
    groups = wide // width
    cut = 4 * half + LANES
    little_ref[...] = jnp.zeros_like(little_ref)
    small = []
    for layer in range(layers):
        at = cut if layer == 0 else 0
        sums = total_ref[:, at : at + cut]
        feed = total_ref[:, 2 * cut :] if layer == 0 else early_ref[...].astype(F32)
        small.append(sums[:, 4 * half : 4 * half + SMALL_ROWS])
        parts = [
            sums[:, third * half + head * HEAD_DIM : third * half + (head + 1) * HEAD_DIM]
            for head in range(heads)
            for third in range(3)
        ]
        qkv = 0.5 * qkv_m[layer] + jnp.concatenate(parts, axis=1)
        fresh_refs[0][layer] = qkv
        proj = 0.5 * proj_m[layer] + sums[:, 3 * half : 4 * half]
        fresh_refs[1][layer] = proj
        up = 0.5 * up_m[layer] + feed[:, :wide]
        fresh_refs[2][layer] = up
        down = 0.5 * down_m[layer] + feed[:, wide:]
        fresh_refs[3][layer] = down
        unit = layer * 2 * groups
        for group in range(groups):
            cols = slice(group * width, (group + 1) * width)
            big_ref[unit + group] = up[:, cols].astype(BF16)
            big_ref[unit + groups + group] = down[:, cols].astype(BF16)
        unit = layer * 2 * heads
        for head in range(heads):
            block = qkv[:, 3 * head * HEAD_DIM : 3 * (head + 1) * HEAD_DIM]
            little_ref[unit + head, :, : 3 * HEAD_DIM] = block.astype(BF16)
            block = proj[:, head * HEAD_DIM : (head + 1) * HEAD_DIM]
            little_ref[unit + heads + head, :, :HEAD_DIM] = block.astype(BF16)
    small.append(jnp.zeros((rows, LANES - layers * SMALL_ROWS), F32))
    small = jnp.concatenate(small, axis=1).astype(BF16)
    for unit in range(little_ref.shape[0]):
        little_ref[unit, :, width:] = small


def prepare(total, early, moments, units, width):
    rows = moments[2].shape[1]
    shapes = [jax.ShapeDtypeStruct(moment.shape, F32) for moment in moments]
    shapes.append(jax.ShapeDtypeStruct((units, rows, width), BF16))
    shapes.append(jax.ShapeDtypeStruct((units, rows, width + LANES), BF16))
    return pl.pallas_call(
        prepare_kernel,
        out_shape=shapes,
        compiler_params=params_for(),
        name="prepare",
    )(total, early, *moments)


def small_step(param, moment, grad, rate, level):
    fresh = 0.5 * moment + grad
    return fresh, param - rate * fresh / (jnp.sqrt(level(fresh * fresh)) + 1e-06)


def update_kernel(big_ref, little_ref, small_ref, *refs, scales):
    mats, params, moments = refs[:4], refs[4:7], refs[7:10]
    outs = refs[10:]
    layers, rows, wide = mats[2].shape
    width = big_ref.shape[2]
    groups = wide // width
    heads = mats[0].shape[2] // (3 * HEAD_DIM)
    small = small_ref[...].astype(F32).T
    for layer in range(layers):
        unit = layer * 2 * heads
        join = lambda blocks: jnp.concatenate([block.astype(F32) for block in blocks], axis=1)
        qkv = join([little_ref[unit + head, :, : 3 * HEAD_DIM] for head in range(heads)])
        proj = join([little_ref[unit + heads + head, :, :HEAD_DIM] for head in range(heads)])
        unit = layer * 2 * groups
        up = join([big_ref[unit + group] for group in range(groups)])
        down = join([big_ref[unit + groups + group] for group in range(groups)])
        for kind, turned in enumerate((qkv, proj, up, down)):
            new = mats[kind][layer] - scales[kind] * turned
            outs[2 * kind][layer] = new
            outs[2 * kind + 1][layer] = new.astype(BF16)
        grads = small[layer * SMALL_ROWS : (layer + 1) * SMALL_ROWS]
        row_mean = lambda square: jnp.mean(square, axis=1, keepdims=True)
        all_mean = lambda square: jnp.mean(row_mean(square), axis=0, keepdims=True)

        def head_mean(square):
            column = jnp.mean(square, axis=0, keepdims=True)
            spans = [
                jnp.broadcast_to(
                    row_mean(column[:, head * HEAD_DIM : (head + 1) * HEAD_DIM]), (1, HEAD_DIM)
                )
                for head in range(HEADS)
            ]
            return jnp.concatenate(spans, axis=1)

        start = 0
        for kind, level in enumerate((row_mean, all_mean, head_mean)):
            place = (layer,) if kind == 0 else (slice(None), layer)
            count = params[kind].shape[1 if kind == 0 else 0]
            fresh, new = small_step(
                params[kind][place], moments[kind][place], grads[start : start + count],
                SMALL_RATES[kind], level,
            )
            outs[8 + 2 * kind][place] = fresh
            outs[9 + 2 * kind][place] = new
            start += count


def update(big, little, small, mats, params, moments, scales):
    shapes = []
    for mat in mats:
        shapes += [jax.ShapeDtypeStruct(mat.shape, F32), jax.ShapeDtypeStruct(mat.shape, BF16)]
    for param in params:
        shapes += [jax.ShapeDtypeStruct(param.shape, F32)] * 2
    return pl.pallas_call(
        functools.partial(update_kernel, scales=scales),
        out_shape=shapes,
        compiler_params=params_for(),
        name="update",
    )(big, little, small, *mats, *params, *moments)


def params_for(**more):
    return pltpu.CompilerParams(vmem_limit_bytes=VMEM_BYTES, **more)


def block_of(cols):
    return pl.BlockSpec((ROWS, cols), lambda g: (g, 0))


def whole(array):
    shape = array.shape
    return pl.BlockSpec(shape, lambda g: (0,) * len(shape), pipeline_mode=pl.Buffered(1))


def some_columns(weights):
    array, width, at = weights
    shape = array.shape[:2] + (width,)
    return pl.BlockSpec(shape, lambda g: (0, 0, at), pipeline_mode=pl.Buffered(1))


def whole_out(shape):
    return pl.BlockSpec(shape, lambda g: (0,) * len(shape))


def tap_tables(channels):
    return [pltpu.VMEM((channels // (2 * LANES), taps, 2 * IMGS, LANES), BF16) for taps in (9, 49)]


def cost(us):
    return pl.CostEstimate(flops=int(us * 1e9), bytes_accessed=int(us * 1e5), transcendentals=0)


def run_attend_forward(x, mask, weights, norm, cpe, crpe, first):
    count, channels = x.shape
    tiles = channels // LANES
    flat = pltpu.VMEM((tiles + 1, ROWS, LANES), F32)
    cells = pltpu.VMEM((SIDE, SIDE, 2 * IMGS, LANES), BF16)
    out = lambda cols, kind: jax.ShapeDtypeStruct((count, cols), kind)
    outs = [out(channels, BF16), out(1, F32), out(3 * channels, BF16)]
    outs += [out(channels, BF16)] * 2
    outs = [out(channels, F32)] * first + outs + [out(channels, F32)]
    return pl.pallas_call(
        functools.partial(attend_forward, first=first),
        grid=(count // ROWS,),
        in_specs=[block_of(channels), block_of(LANES)]
        + [some_columns(weights)]
        + [whole(a) for a in (norm, cpe, crpe)],
        out_specs=[block_of(array.shape[1]) for array in outs],
        out_shape=outs,
        scratch_shapes=[
            cells, cells, *tap_tables(channels), pltpu.VMEM((ROWS, channels), F32),
            flat, flat, flat, flat,
            pltpu.VMEM((2, ROWS, LANES), F32),
        ],
        compiler_params=params_for(),
        cost_estimate=cost(50),
        name="attend_forward",
    )(x, mask, weights[0], norm, cpe, crpe)


def run_feed_forward(att, up_down, norm, chunk=512):
    count, channels = att.shape
    hidden = up_down[0].shape[0] * up_down[1] // 2
    return pl.pallas_call(
        functools.partial(feed_forward, chunk=chunk),
        grid=(count // ROWS,),
        in_specs=[block_of(channels), some_columns(up_down), whole(norm)],
        out_specs=[block_of(channels), block_of(hidden), block_of(hidden)]
        + [block_of(channels), block_of(1)],
        out_shape=[
            jax.ShapeDtypeStruct((count, channels), F32),
            jax.ShapeDtypeStruct((count, hidden), BF16),
            jax.ShapeDtypeStruct((count, hidden), BF16),
            jax.ShapeDtypeStruct((count, channels), BF16),
            jax.ShapeDtypeStruct((count, 1), F32),
        ],
        compiler_params=params_for(),
        cost_estimate=cost(24),
        name="feed_forward",
    )(att, up_down[0], norm)


def run_feed_back(inputs, up_down, norm, first, chunk=512):
    count, channels = inputs[2 if first else 0].shape
    hidden = up_down[0].shape[0] * up_down[1] // 2
    shape = up_down[0].shape[:2] + (up_down[1],)
    more = [
        pltpu.VMEM((ROWS, hidden), BF16), pltpu.VMEM((ROWS, hidden), BF16),
        pltpu.VMEM((ROWS, channels), BF16), pltpu.VMEM((ROWS, 1), F32),
        pltpu.VMEM((2, ROWS, LANES), F32), pltpu.VMEM((ROWS, channels), F32),
    ]
    return pl.pallas_call(
        functools.partial(feed_back, first=first, chunk=chunk),
        grid=(count // ROWS,),
        in_specs=[block_of(array.shape[1]) for array in inputs]
        + [some_columns(up_down), whole(norm)],
        out_specs=[block_of(channels)] * first
        + [block_of(channels), whole_out(shape), whole_out((2, channels))],
        out_shape=[jax.ShapeDtypeStruct((count, channels), BF16)] * first
        + [
            jax.ShapeDtypeStruct((count, channels), F32),
            jax.ShapeDtypeStruct(shape, BF16),
            jax.ShapeDtypeStruct((2, channels), F32),
        ],
        scratch_shapes=[pltpu.VMEM(shape, F32)] + more * first,
        compiler_params=params_for(),
        cost_estimate=cost(50 if first else 37),
        name="feed_back",
    )(*inputs, up_down[0], norm)


def run_attend_back(
    gatt, x, unit, inv, packed, rel, mixed, mask, weights, norm, cpe, crpe, gmid, taps, last
):
    count, channels = x.shape
    tiles = channels // LANES
    flat = pltpu.VMEM((tiles + 1, ROWS, LANES), F32)
    cells = pltpu.VMEM((SIDE, SIDE, 2 * IMGS, LANES), BF16)
    small = [(2, channels), (9, IMGS, channels), (49, IMGS, channels)]
    shape = weights[0].shape[:2] + (weights[1],)
    return pl.pallas_call(
        attend_back,
        grid=(count // ROWS,),
        in_specs=[block_of(channels)] * 3
        + [block_of(1), block_of(3 * channels), block_of(channels), block_of(channels)]
        + [block_of(LANES)]
        + [some_columns(weights)]
        + [whole(a) for a in (norm, cpe, crpe, gmid, taps)],
        out_specs=[block_of(channels), whole_out(shape), whole_out((channels, LANES))],
        out_shape=[
            jax.ShapeDtypeStruct((count, channels), F32),
            jax.ShapeDtypeStruct(shape, BF16),
            jax.ShapeDtypeStruct((channels, LANES), BF16),
        ],
        scratch_shapes=[pltpu.VMEM(each, F32) for each in small]
        + [
            pltpu.VMEM(shape, F32),
            cells, cells, cells, cells, *tap_tables(channels),
            flat, flat, flat, flat, flat, flat, flat,
            pltpu.VMEM((2, ROWS, LANES), F32),
            pltpu.VMEM((ROWS, 3 * channels), BF16),
        ]
        + [pltpu.VMEM((ROWS, channels), F32)] * last,
        compiler_params=params_for(),
        cost_estimate=cost(65),
        name="attend_back",
    )(gatt, x, unit, inv, packed, rel, mixed, mask, weights[0], norm, cpe, crpe, gmid, taps)


def where_am_i():
    tok, blk = lax.axis_index("tok"), lax.axis_index("blk")
    core, x, z = lax.rem(tok, 2), lax.rem(tok // 2, 2), tok // 4
    return blk, z, x, core


def device_at(y, z, x, core):
    return (z * 4 + x * 2 + core, y)


def neighbours(y, z, x, core):
    fx, fy = 1 - core, core
    flip = lambda value, by: value + by - 2 * value * by
    first = (flip(y, fy), flip(x, fx))
    second = (flip(y, fx), flip(x, fy))
    cross = (1 - y, 1 - x)
    return first, second, cross


def greet(targets):
    barrier = pltpu.get_barrier_semaphore()
    for target in targets:
        pl.semaphore_signal(barrier, inc=1, device_id=target, device_id_type=pl.DeviceIdType.MESH)
    pl.semaphore_wait(barrier, len(targets))


def spread_kernel(shard_ref, out_ref, send_sem, recv_sem, own_sem):
    y, z, x, core = where_am_i()
    first, second, cross = neighbours(y, z, x, core)
    line = [lax.rem(z + d, 4) for d in range(4)]
    back = [lax.rem(z + 4 - d, 4) for d in range(4)]
    to_first = device_at(first[0], z, first[1], core)
    to_second = device_at(second[0], z, second[1], core)
    to_core = device_at(y, z, x, 1 - core)
    greet([to_first, to_second, to_core] + [device_at(y, line[d], x, core) for d in (1, 2, 3)])
    slot = lambda at, layer, side: at[0] * 16 + layer * 4 + at[1] * 2 + side
    own = pltpu.make_async_copy(shard_ref, out_ref.at[slot((y, x), z, core)], own_sem)
    own.start()
    copies = []

    def send(src, at, layer, side, target, number):
        copy = pltpu.make_async_remote_copy(
            src_ref=src, dst_ref=out_ref.at[slot(at, layer, side)],
            send_sem=send_sem.at[number], recv_sem=recv_sem.at[number],
            device_id=target, device_id_type=pl.DeviceIdType.MESH,
        )
        copy.start()
        copies.append(copy)

    def arrive(at, layer, side, number):
        here = out_ref.at[slot(at, layer, side)]
        pltpu.make_async_remote_copy(
            src_ref=here, dst_ref=here, send_sem=send_sem.at[number], recv_sem=recv_sem.at[number],
            device_id=to_core, device_id_type=pl.DeviceIdType.MESH,
        ).wait_recv()

    me = (y, x)
    for d in (1, 2, 3):
        send(shard_ref, me, z, core, device_at(y, line[d], x, core), d - 1)
    for d in range(4):
        layer = back[d]
        if d:
            arrive(me, layer, core, d - 1)
        src = out_ref.at[slot(me, layer, core)] if d else shard_ref
        send(src, me, layer, core, to_first, 3 + d)
        send(src, me, layer, core, to_second, 7 + d)
        send(src, me, layer, core, to_core, 15 + d)
    for d in range(4):
        arrive(first, back[d], core, 3 + d)
        src = out_ref.at[slot(first, back[d], core)]
        send(src, first, back[d], core, to_second, 11 + d)
        send(src, first, back[d], core, to_core, 19 + d)
    for d in range(4):
        arrive(second, back[d], core, 7 + d)
        send(out_ref.at[slot(second, back[d], core)], second, back[d], core, to_core, 23 + d)
    for d in range(4):
        arrive(cross, back[d], core, 11 + d)
        send(out_ref.at[slot(cross, back[d], core)], cross, back[d], core, to_core, 27 + d)
    for d in range(4):
        arrive(me, back[d], 1 - core, 15 + d)
        arrive(second, back[d], 1 - core, 19 + d)
        arrive(first, back[d], 1 - core, 23 + d)
        arrive(cross, back[d], 1 - core, 27 + d)
    own.wait()
    for copy in copies:
        copy.wait_send()


def spread(shard, collective_id):
    return pl.pallas_call(
        spread_kernel,
        in_specs=[pl.BlockSpec(memory_space=pl.ANY)],
        out_specs=pl.BlockSpec(memory_space=pl.ANY),
        out_shape=jax.ShapeDtypeStruct((32,) + shard.shape, shard.dtype),
        scratch_shapes=[
            pltpu.SemaphoreType.DMA((31,)), pltpu.SemaphoreType.DMA((31,)), pltpu.SemaphoreType.DMA,
        ],
        compiler_params=pltpu.CompilerParams(
            collective_id=collective_id, has_side_effects=True, vmem_limit_bytes=VMEM_BYTES
        ),
        name="spread",
    )(shard)


def collect_kernel(*refs, widths):
    parts = len(widths)
    grads, out_ref = refs[:parts], refs[parts]
    own_s, chip_s, second_s, first_s, line_s, send_sem, recv_sem, load_sem = refs[parts + 1 :]
    y, z, x, core = where_am_i()
    first, second, cross = neighbours(y, z, x, core)
    line = [lax.rem(z + d, 4) for d in range(4)]
    back = [lax.rem(z + 4 - d, 4) for d in range(4)]
    to_first = device_at(first[0], z, first[1], core)
    to_second = device_at(second[0], z, second[1], core)
    to_core = device_at(y, z, x, 1 - core)
    greet([to_first, to_second, to_core] + [device_at(y, line[d], x, core) for d in (1, 2, 3)])
    mine = lambda at, layer, side: own_s.at[at[0] * 8 + layer * 2 + at[1], side]
    loads = []
    for turn, side in enumerate((1 - core, core)):
        start = 0
        for number, (grad, width) in enumerate(zip(grads, widths)):
            copy = pltpu.make_async_copy(
                grad.at[:, side], own_s.at[: grad.shape[0], side, :, start : start + width],
                load_sem.at[turn, number, 0],
            )
            copy.start()
            loads.append((turn, copy))
            if grad.shape[0] == 8:
                copy = pltpu.make_async_copy(
                    grad.at[:, side], own_s.at[8:, side, :, start : start + width],
                    load_sem.at[turn, number, 1],
                )
                copy.start()
                loads.append((turn, copy))
            start += width
    for turn, copy in loads:
        if turn == 0:
            copy.wait()
    copies = []

    def send(src, dst, target, number):
        copy = pltpu.make_async_remote_copy(
            src_ref=src, dst_ref=dst, send_sem=send_sem.at[number], recv_sem=recv_sem.at[number],
            device_id=target, device_id_type=pl.DeviceIdType.MESH,
        )
        copy.start()
        copies.append(copy)

    def arrive(ref, number):
        pltpu.make_async_remote_copy(
            src_ref=ref, dst_ref=ref, send_sem=send_sem.at[number], recv_sem=recv_sem.at[number],
            device_id=to_core, device_id_type=pl.DeviceIdType.MESH,
        ).wait_recv()

    def add(ref, *others):
        total = ref[...].astype(F32)
        for other in others:
            total = total + other[...].astype(F32)
        ref[...] = total.astype(BF16)

    me = (y, x)
    places = (cross, first, second, me)
    theirs = (0, 2, 1, 3)
    turns = (2, 1, 3, 0)
    for d in turns:
        for kind in (0, 2, 1, 3):
            number = theirs[kind] * 4 + d
            send(mine(places[kind], line[d], 1 - core), chip_s.at[number], to_core, number)

    for turn, copy in loads:
        if turn == 1:
            copy.wait()

    def fold(kind, d):
        here = chip_s.at[kind * 4 + d]
        arrive(here, kind * 4 + d)
        own = mine(places[kind], line[d], core)
        if kind in (0, 2):
            there = 0 if kind == 0 else 4
            add(here, own)
            send(here, second_s.at[there + d], to_second, 16 + there + d)
        elif kind == 1:
            arrive(second_s.at[d], 16 + d)
            add(here, own, second_s.at[d])
            send(here, first_s.at[d], to_first, 24 + d)
        else:
            arrive(second_s.at[4 + d], 20 + d)
            arrive(first_s.at[d], 24 + d)
            if d:
                add(here, own, second_s.at[4 + d], first_s.at[d])
                send(here, line_s.at[d - 1], device_at(y, line[d], x, core), 27 + d)

    stages = [(0, 2), (1,), (3,)]
    for turn in range(len(turns) + 2):
        for stage, kinds in enumerate(stages):
            if 0 <= turn - stage < len(turns):
                for kind in kinds:
                    fold(kind, turns[turn - stage])
    for d in (1, 2, 3):
        arrive(line_s.at[d - 1], 27 + d)
    total = chip_s[12].astype(F32) + mine(me, z, core)[...].astype(F32)
    for ref in (second_s.at[4], first_s.at[0], line_s.at[0], line_s.at[1], line_s.at[2]):
        total = total + ref[...].astype(F32)
    out_ref[...] = total
    for copy in copies:
        copy.wait_send()


def collect(grads, collective_id):
    rows = grads[0].shape[2]
    widths = tuple(grad.shape[3] for grad in grads)
    block = lambda count: pltpu.VMEM((count, rows, sum(widths)), BF16)
    return pl.pallas_call(
        functools.partial(collect_kernel, widths=widths),
        in_specs=[pl.BlockSpec(memory_space=pl.ANY)] * len(grads),
        out_specs=pl.BlockSpec(memory_space=pltpu.VMEM),
        out_shape=jax.ShapeDtypeStruct((rows, sum(widths)), F32),
        scratch_shapes=[
            pltpu.VMEM((16, 2, rows, sum(widths)), BF16), block(16), block(8), block(4), block(3),
            pltpu.SemaphoreType.DMA((31,)), pltpu.SemaphoreType.DMA((31,)),
            pltpu.SemaphoreType.DMA((2, len(widths), 2)),
        ],
        compiler_params=pltpu.CompilerParams(
            collective_id=collective_id, has_side_effects=True, vmem_limit_bytes=VMEM_BYTES
        ),
        name="collect",
    )(*grads)


def run_schulz(fresh, width):
    units, height, _ = fresh.shape
    spec = pl.BlockSpec((1, height, 2 * width), lambda g: (g, 0, 0))
    return pl.pallas_call(
        lambda *refs: schulz(*refs, width=width),
        grid=(units,),
        in_specs=[spec],
        out_specs=spec,
        out_shape=jax.ShapeDtypeStruct((units, height, 2 * width), BF16),
        compiler_params=params_for(),
        name="schulz",
    )(fresh)


def token_major(rows):
    count, channels = rows.shape
    split = rows.reshape(count // ROWS, IMGS, SLOT, channels)
    return split.transpose(0, 2, 1, 3).reshape(count, channels)


def image_major(rows):
    count, channels = rows.shape
    split = rows.reshape(count // ROWS, SLOT, IMGS, channels)
    return split.transpose(0, 2, 1, 3).reshape(count, channels)


def key_masks(grid_class):
    extent = 5 + 2 * grid_class
    across = (jnp.arange(SIDE, dtype=jnp.int32)[None, :] < extent[:, None]).astype(F32)
    cells = (across[:, :, None] * across[:, None, :]).reshape(-1, SIDE * SIDE)
    return jnp.concatenate([jnp.ones((cells.shape[0], 1), F32), cells], axis=1)


def split_heads(shard, heads_own, head_dim):
    lead = shard.shape[:-1]
    parts = shard.reshape(lead + (heads_own, 3, head_dim))
    return jnp.swapaxes(parts, -3, -2).reshape(lead + (3 * heads_own * head_dim,))


def join_heads(shard, heads_own, head_dim):
    lead = shard.shape[:-1]
    parts = shard.reshape(lead + (3, heads_own, head_dim))
    return jnp.swapaxes(parts, -3, -2).reshape(lead + (3 * heads_own * head_dim,))


def block_scale(height, breadth):
    return math.sqrt(max(1.0, height / breadth))


def normalized_step(param_vals, moment, grads_in, rate, axes):
    fresh = 0.5 * moment + grads_in
    level = jnp.sqrt(jnp.mean(fresh * fresh, axis=axes, keepdims=True))
    return (fresh, param_vals - rate * fresh / (level + 1e-06))


def on_device(
    tokens, cotangent, grid_class,
    qkv_weight, proj_weight, up_weight, down_weight, norm_params, cpe_weight, crpe_weight,
    qkv_moment, proj_moment, up_moment, down_moment, norm_moment, cpe_moment, crpe_moment,
):
    own_count, channels = tokens.shape
    blk_count = lax.axis_size("blk")
    tok_count = lax.axis_size("tok")
    blk_at = lax.axis_index("blk")
    layers = qkv_weight.shape[0]
    images_own = grid_class.shape[0] // blk_count
    head_dim = channels // HEADS
    heads_own = HEADS // blk_count
    groups_own = GROUPS // blk_count
    group_width = up_weight.shape[2] // groups_own
    own_rows = qkv_weight.shape[1]
    both = ("blk", "tok")

    attn_cols, feed_cols = 4 * heads_own * head_dim, 2 * up_weight.shape[2]
    near = (tok_count, blk_count, layers) == (16, 2, 2)
    turn = lambda array: jnp.swapaxes(array, 1, 2)
    flip = lambda array: jnp.swapaxes(array, 0, 1)
    mats = (qkv_weight, turn(proj_weight), up_weight, turn(down_weight))
    moments = (qkv_moment, turn(proj_moment), up_moment, turn(down_moment))
    if near:
        shard = pack(mats)
    else:
        shard = jnp.concatenate(
            [
                up_weight,
                jnp.swapaxes(down_weight, 1, 2),
                split_heads(qkv_weight, heads_own, head_dim),
                jnp.swapaxes(proj_weight, 1, 2),
            ],
            axis=2,
        ).astype(BF16)

    def gather(piece, kernel):
        if kernel:
            return spread(piece, 1).reshape(blk_count, channels, piece.shape[1])
        full = lax.all_gather(piece, both, axis=0, tiled=True)
        return full.reshape(blk_count, channels, piece.shape[1])

    def halves(full):
        full = full.reshape(blk_count, channels, 4, heads_own * head_dim).transpose(1, 2, 0, 3)
        full = full.reshape(channels, 4, 2, channels // 2).transpose(2, 0, 1, 3)
        return full.reshape(2, channels, 2 * channels)

    def shares(grads):
        if blk_count == 2:
            return grads
        full = grads.reshape(2, channels, 4, channels // 2).transpose(1, 2, 0, 3)
        full = full.reshape(channels, 4, blk_count, heads_own * head_dim).transpose(2, 0, 1, 3)
        return full.reshape(blk_count, channels, attn_cols)

    attn_all, feed_all = [], []
    for layer in range(layers):
        piece = shard[layer]
        if layer and near:
            piece, full = lax.optimization_barrier((piece, full))
            attn_all[0], feed_all[0] = (full, attn_cols, 2), (full, feed_cols, 0)
        full = gather(piece, near and layer == 0)
        if blk_count == 2:
            attn_all.append((full, attn_cols, 2))
            feed_all.append((full, feed_cols, 0))
        else:
            attn_all.append((halves(full[:, :, feed_cols:]), 2 * channels, 0))
            feed_all.append((full[:, :, :feed_cols], feed_cols, 0))

    own_class = lax.dynamic_slice_in_dim(grid_class, blk_at * images_own, images_own)
    keys = key_masks(own_class)
    mask = jnp.broadcast_to(token_major(keys.reshape(own_count, 1)), (own_count, LANES))
    taps = jnp.repeat(tap_mask(jnp.arange(HEADS, dtype=jnp.int32)), head_dim, axis=1)

    stream = tokens
    saved = []
    for layer in range(layers):
        cpe, crpe = cpe_weight[layer], crpe_weight[layer] * taps
        outs = run_attend_forward(
            stream, mask, attn_all[layer], norm_params[layer], cpe, crpe, layer == 0
        )
        if layer:
            outs = [stream] + list(outs)
        middle = None
        if layer < layers - 1:
            stream, *middle = run_feed_forward(outs[-1], feed_all[layer], norm_params[layer])
        saved.append(tuple(outs) + (middle, cpe, crpe))

    upstream = cotangent
    attn_sums, feed_sums = [None] * layers, [None] * layers
    small_rows = SMALL_ROWS
    for layer in reversed(range(layers)):
        x, unit, inv, packed, rel, mixed, att, middle, cpe, crpe = saved[layer]
        last = layer == layers - 1
        if last:
            inputs = [mask, upstream, att]
        else:
            inputs = [upstream, middle[2], middle[3], middle[0], middle[1]]
        outs = run_feed_back(inputs, feed_all[layer], norm_params[layer], last)
        if last:
            block_out = outs[0]
        gatt, gfeed, gmid = outs[-3:]
        upstream, gattn, small = run_attend_back(
            gatt, x, unit, inv, packed, rel, mixed, mask, attn_all[layer],
            norm_params[layer], cpe, crpe, gmid, taps, layer == 0,
        )
        if near and layer == layers - 1:
            early = lax.psum_scatter(
                gfeed.reshape(blk_count * channels, gfeed.shape[2]), both,
                scatter_dimension=0, tiled=True,
            )
        gattn = shares(gattn)
        if near:
            split = lambda g: g.reshape(-1, 2, own_rows, g.shape[-1])
            pieces = [split(g) for g in (gattn, small, gfeed)]
            waiting = pieces[:2] if layer else waiting + pieces
        else:
            small = jnp.broadcast_to(small, (blk_count, channels, LANES))
            scatter = lambda g: lax.psum_scatter(
                g.reshape(blk_count * channels, g.shape[2]), both, scatter_dimension=0, tiled=True
            ).astype(F32)
            feed_sums[layer] = scatter(gfeed)
            attn_sums[layer] = scatter(jnp.concatenate([gattn, small], axis=2))
    tokens_grad = upstream

    scales = (
        block_scale(channels, 3 * head_dim),
        block_scale(head_dim, channels),
        block_scale(channels, group_width),
        block_scale(group_width, channels),
    )
    if near:
        early, waiting = lax.optimization_barrier((early, waiting))
        total = collect(waiting, 2)
        ready = prepare(total, early, moments, tok_count, group_width)
        big, little, small_all = finish(ready[4], ready[5], 3)
        done = update(
            big, little, small_all, mats,
            (norm_params, flip(cpe_weight), flip(crpe_weight)),
            (norm_moment, flip(cpe_moment), flip(crpe_moment)),
            tuple(rate * scale for rate, scale in zip(MUON_RATES, scales)),
        )
        results = []
        for kind in range(4):
            three = (ready[kind], done[2 * kind], done[2 * kind + 1])
            results += [turn(array) if kind % 2 else array for array in three]
        return (block_out, tokens_grad, *results, *done[8:10], *map(flip, done[10:]))
    attn_sum = jnp.stack(attn_sums)
    feed_sum = jnp.stack(feed_sums)
    small_sum = attn_sum[:, :, -LANES:][:, :, :small_rows]
    attn_sum = attn_sum[:, :, :-LANES]
    attn_moment = jnp.concatenate(
        [split_heads(qkv_moment, heads_own, head_dim), jnp.swapaxes(proj_moment, 1, 2)], axis=2
    )
    feed_moment = jnp.concatenate([up_moment, jnp.swapaxes(down_moment, 1, 2)], axis=2)
    attn_fresh = 0.5 * attn_moment + attn_sum
    feed_fresh = 0.5 * feed_moment + feed_sum

    units = layers * 2 * groups_own
    per_dev = -(-units // tok_count)
    big = feed_fresh.reshape(layers, own_rows, 2 * groups_own, group_width)
    big = big.transpose(0, 2, 1, 3).reshape(units, own_rows, group_width)
    heads = attn_fresh.reshape(layers, own_rows, 4, heads_own, head_dim).transpose(0, 3, 1, 2, 4)
    heads_qkv = heads[:, :, :, :3].reshape(layers, heads_own, own_rows, 3 * head_dim)
    heads_proj = heads[:, :, :, 3]
    widen = lambda v: jnp.pad(v, ((0, 0), (0, 0), (0, 0), (0, group_width - v.shape[3])))
    little = jnp.concatenate([widen(heads_qkv), widen(heads_proj)], axis=1)
    little = little.reshape(units, own_rows, group_width)
    def owners(blocks):
        blocks = jnp.pad(blocks.astype(BF16), ((0, per_dev * tok_count - units), (0, 0), (0, 0)))
        return blocks.reshape(tok_count, per_dev, own_rows, group_width)

    big, little = owners(big), owners(little)
    small_own = jnp.swapaxes(small_sum, 0, 1).reshape(own_rows, layers * small_rows)
    small_own = jnp.pad(small_own, ((0, 0), (0, LANES - layers * small_rows))).astype(BF16)
    small_own = jnp.broadcast_to(small_own, (tok_count, per_dev, own_rows, LANES))
    little = jnp.concatenate([little, small_own], axis=3)
    got = lax.all_to_all(jnp.concatenate([big, little], axis=3), "tok", 0, 0, tiled=True)
    got = got.transpose(1, 0, 2, 3).reshape(per_dev, channels, 2 * group_width + LANES)
    small_all = got[0, :, 2 * group_width :]
    ortho = run_schulz(got, group_width)
    ortho = ortho.reshape(per_dev, tok_count, own_rows, 2 * group_width)
    ortho = lax.all_to_all(ortho.transpose(1, 0, 2, 3), "tok", 0, 0, tiled=True)
    ortho = ortho.reshape(per_dev * tok_count, own_rows, 2 * group_width)[:units]
    big, little = ortho[:, :, :group_width], ortho[:, :, group_width:]
    small_all = small_all.astype(F32).T[: layers * small_rows]
    small_all = small_all.reshape(layers, small_rows, channels)
    big = big.astype(F32).reshape(layers, 2, groups_own, own_rows, group_width)
    big = big.transpose(1, 0, 3, 2, 4).reshape(2, layers, own_rows, groups_own * group_width)
    little = little.astype(F32).reshape(layers, 2, heads_own, own_rows, group_width)
    little_qkv = little[:, 0, :, :, : 3 * head_dim].transpose(0, 2, 1, 3)
    little_qkv = little_qkv.reshape(layers, own_rows, heads_own * 3 * head_dim)
    little_proj = little[:, 1, :, :, :head_dim].transpose(0, 1, 3, 2)
    little_proj = little_proj.reshape(layers, heads_own * head_dim, own_rows)

    qkv_fresh = join_heads(attn_fresh[:, :, : qkv_weight.shape[2]], heads_own, head_dim)
    proj_fresh = jnp.swapaxes(attn_fresh[:, :, qkv_weight.shape[2] :], 1, 2)
    up_fresh = feed_fresh[:, :, : up_weight.shape[2]]
    down_fresh = jnp.swapaxes(feed_fresh[:, :, up_weight.shape[2] :], 1, 2)
    results = []
    for kind, (weight, fresh, turned) in enumerate(
        (
            (qkv_weight, qkv_fresh, little_qkv),
            (proj_weight, proj_fresh, little_proj),
            (up_weight, up_fresh, big[0]),
            (down_weight, down_fresh, jnp.swapaxes(big[1], 1, 2)),
        )
    ):
        new = weight - MUON_RATES[kind] * scales[kind] * turned
        results.extend([fresh, new, new.astype(BF16)])

    norm_fresh, norm_new = normalized_step(
        norm_params, norm_moment, small_all[:, :4], SMALL_RATES[0], (2,)
    )
    cpe_fresh, cpe_new = normalized_step(
        cpe_weight, cpe_moment, small_all[:, 4:13], SMALL_RATES[1], (1, 2)
    )
    head_shape = (layers, 49, HEADS, head_dim)
    crpe_fresh, crpe_new = normalized_step(
        crpe_weight.reshape(head_shape),
        crpe_moment.reshape(head_shape),
        small_all[:, 13:].reshape(head_shape),
        SMALL_RATES[2],
        (1, 3),
    )
    return (
        (block_out, tokens_grad)
        + tuple(results)
        + (norm_fresh, norm_new, cpe_fresh, cpe_new)
        + (crpe_fresh.reshape(crpe_weight.shape), crpe_new.reshape(crpe_weight.shape))
    )


def solution(mesh):
    rows = P(("tok", "blk"), None)
    down_cols = P(None, "tok", "blk")
    cross = P(None, "blk", "tok")
    mats = (down_cols, cross, down_cols, cross)
    in_specs = (rows, rows, P("tok")) + mats + (P(),) * 3 + mats + (P(),) * 3
    out_specs = (rows, rows) + tuple(spec for spec in mats for _ in range(3)) + (P(),) * 6
    return jax.shard_map(
        on_device, mesh=mesh, in_specs=in_specs, out_specs=out_specs, check_vma=False
    )
```
